32 devices in a mesh: slab: 8 (over z, y), grid: 4 (over x, core).
Axes of the slice: x: 2, y: 2, z: 4, core: 2. Of those that a mesh axis runs over, the one named last changes fastest.
Arguments:
- orbitals: bfloat16 [64, 110592], P(None, 'grid'), may hold values from -6 to 6
- targets: int32 [16], replicated, may hold values from 0 to 63
- points: int32 [32], P('slab'), may hold values from 0 to 110591, as said below
- fit: float32 [32, 4], P('slab'), may hold values from -2 to 4, as said below
Outputs:
- applied_exchange: float32 [16, 110592], P('slab', 'grid')
The draws below stay inside these ranges and needn't reach their ends.
Inputs may be any that keep to these rules, and one draw needn't show every extreme that they name: `points`: 32 distinct grid cells. `fit`: each block of 4 rows is a symmetric matrix.
All inputs are finite; a program needn't handle non-finite values.
Results may differ from the reference program's by a relative error of at most 0.004.
Values may be sent and summed in bfloat16 or wider, within the bound.
No kernel may reach another device: no remote copies, remote signals or barrier semaphores. Data moves between devices by JAX's collectives and lax.ppermute only.
A program may use at most 64 MiB of HBM per device.

```python
import math
import jax
import jax.numpy as jnp
from jax import lax

NG = 48
NOCC = 64
CELLS = 110592
MU_GRP = 4
NMU = 32
K = 16
N_SLAB = 8


def draw_points(key, part):
    key_inner, key_order = jax.random.split(key)
    interior = jax.random.permutation(key_inner, CELLS - 2)[:NMU - 2].astype(jnp.int32) + 1
    corners = jnp.array([0, CELLS - 1], dtype=jnp.int32)
    joined = jnp.concatenate([corners, interior])
    return jax.random.permutation(key_order, joined).astype(jnp.int32)


def draw_fit(key, part):
    key_diag, key_off = jax.random.split(key)
    blocks = NMU // MU_GRP
    spread = (6.0 / MU_GRP) ** 0.5
    diagonal = jnp.exp(jax.random.uniform(key_diag, (blocks, MU_GRP), jnp.float32, 0.0, 1.0986))
    noise = jax.random.uniform(key_off, (blocks, MU_GRP, MU_GRP), jnp.float32, -spread, spread)
    symmetric = 0.5 * (noise + jnp.swapaxes(noise, 1, 2))
    identity = jnp.eye(MU_GRP, dtype=jnp.float32)
    matrix = symmetric * (1.0 - identity) + identity * diagonal[:, :, None]
    return matrix.reshape(NMU, MU_GRP).astype(jnp.float32)


def plant(values, rng, low, top_value):
    dims = values.shape
    place = [jax.random.randint(jax.random.fold_in(rng, axis), (), 0, dims[axis]) for axis in range(len(dims))]
    values = values.at[tuple(place)].set(low)
    longest = dims.index(max(dims))
    place[longest] = (place[longest] + 1) % dims[longest]
    return values.at[tuple(place)].set(top_value)


def block_levels(key, dims, pieces, least, largest):
    level = 1.0
    for axis_at, parts in pieces:
        draws = jax.random.uniform(jax.random.fold_in(jax.random.fold_in(key, 6), axis_at), (parts,), jnp.float32, least / len(pieces), largest / len(pieces))
        level = level * jnp.repeat(jnp.exp(draws), dims[axis_at] // parts).reshape((-1,) + (1,) * (len(dims) - 1 - axis_at))
    return level


def bell_draw(own_key, shape, scale, most, shards=(), kind=jnp.bfloat16):
    drawn = scale * jax.random.normal(own_key, shape, jnp.float32)
    if shards:
        drawn = drawn * block_levels(own_key, shape, shards, -0.22, 0.18)
    return jnp.clip(drawn, -most, most).astype(kind)


def setup_inputs(seed: int = 0) -> dict:
    arg_keys = jax.random.split(jax.random.key(seed), 5)
    orbitals = bell_draw(arg_keys[0], (NOCC, CELLS), 1.0, 6.0, ((1, 4),))
    targets = plant(jax.random.randint(arg_keys[1], (K,), 0, NOCC), jax.random.fold_in(arg_keys[1], 1), 0, NOCC - 1).astype(jnp.int32)
    points = draw_points(jax.random.fold_in(arg_keys[4], 71), 0)
    fit = draw_fit(jax.random.fold_in(arg_keys[4], 71), 0)
    return dict(orbitals=orbitals, targets=targets, points=points, fit=fit)


screening = 4.0

def kernel_table():
    full_index = jnp.arange(NG)
    wrapped = jnp.where(full_index > NG // 2, full_index - NG, full_index).astype(jnp.float32)
    half_index = jnp.arange(NG // 2 + 1).astype(jnp.float32)
    step_size = 2.0 * math.pi / NG
    full_sq = wrapped * step_size * (wrapped * step_size)
    half_sq = half_index * step_size * (half_index * step_size)
    summed = full_sq[:, None, None] + full_sq[None, :, None] + half_sq[None, None, :]
    return screening / (screening + summed)

def screened(fields):
    cubes = fields.reshape(fields.shape[0], NG, NG, NG)
    spectrum = jnp.fft.rfftn(cubes, axes=(1, 2, 3)) * kernel_table()
    solved = jnp.fft.irfftn(spectrum, s=(NG, NG, NG), axes=(1, 2, 3))
    return solved.reshape(fields.shape).astype(jnp.float32)

def reference(orbitals, targets, points, fit):
    occupied = orbitals.shape[0]
    target_count = targets.shape[0]
    chosen = jnp.take(orbitals, targets, axis=0)
    point_blocks = points.reshape(N_SLAB, MU_GRP)
    fit_blocks = fit.reshape(N_SLAB, MU_GRP, MU_GRP)

    def one_group(running, item):
        block_points, block_fit = item
        at_points = jnp.take(orbitals, block_points, axis=1)
        target_points = jnp.take(at_points, targets, axis=0)
        density = jnp.dot(at_points.T, orbitals, preferred_element_type=jnp.float32) * (1.0 / math.sqrt(occupied))
        target_density = jnp.dot(target_points.T, chosen, preferred_element_type=jnp.float32) * (1.0 / math.sqrt(target_count))
        pairs = density * target_density
        fitted = jnp.dot(block_fit.T, pairs, precision=lax.Precision.HIGHEST).astype(jnp.bfloat16)
        fitted = lax.optimization_barrier(fitted)
        potential = screened(fitted.astype(jnp.float32)).astype(jnp.bfloat16)
        potential = lax.optimization_barrier(potential)
        weighted = (potential.astype(jnp.float32) * density).astype(jnp.bfloat16)
        return (running + jnp.dot(target_points, weighted, preferred_element_type=jnp.float32), None)
    initial = jnp.zeros((target_count, CELLS), jnp.float32)
    summed, unused = lax.scan(one_group, initial, (point_blocks, fit_blocks))
    return summed * (-1.0 / math.sqrt(NMU))
```

```python
import math

import jax
import jax.numpy as jnp
import ml_dtypes
import numpy as np
from jax import lax
from jax.experimental import pallas as pl
from jax.experimental.pallas import tpu as pltpu
from jax.sharding import PartitionSpec as P

NG = 48


screening = 4.0
careful = lax.Precision.HIGH
lanes = 128
f32 = jnp.float32
bf16 = jnp.bfloat16
everyone = ("slab", "grid")
contract_last = (((1,), (1,)), ((), ()))


def dft_tables(length):
    positions = jnp.arange(length, dtype=jnp.int32)
    product = positions[:, None] * positions[None, :] % length
    angles = product.astype(jnp.float32) * (2.0 * math.pi / length)
    return (jnp.cos(angles), jnp.sin(angles))


def kernel_table():
    full_index = jnp.arange(NG, dtype=jnp.int32)
    wrapped = jnp.where(full_index > NG // 2, full_index - NG, full_index).astype(jnp.float32)
    half_index = jnp.arange(NG // 2 + 1, dtype=jnp.int32).astype(jnp.float32)
    step_size = 2.0 * math.pi / NG
    full_sq = wrapped * step_size * (wrapped * step_size)
    half_sq = half_index * step_size * (half_index * step_size)
    summed = full_sq[:, None, None] + full_sq[None, :, None] + half_sq[None, None, :]
    return screening / (screening + summed)


def apply_axis(values, matrix, pattern):
    return jnp.einsum(
        pattern, values, matrix, precision=careful, preferred_element_type=jnp.float32
    )


def split_apply(values, matrix, pattern):
    upper = matrix.astype(jnp.bfloat16)
    lower = (matrix - upper.astype(jnp.float32)).astype(jnp.bfloat16)
    first = jnp.einsum(pattern, values, upper, preferred_element_type=jnp.float32)
    return first + jnp.einsum(pattern, values, lower, preferred_element_type=jnp.float32)


def solve_one(vector_row):
    half_len = NG // 2 + 1
    cosine, sin_table = dft_tables(NG)
    cos_half = cosine[:, :half_len]
    sin_half = sin_table[:, :half_len]
    cube_vals = vector_row.reshape(NG, NG, NG)
    real_part = split_apply(cube_vals, cos_half, "xyz,zm->xym")
    imag_part = -split_apply(cube_vals, sin_half, "xyz,zm->xym")
    for pattern in ("xym,yb->xbm", "xym,xb->bym"):
        real_next = apply_axis(real_part, cosine, pattern) + apply_axis(
            imag_part, sin_table, pattern
        )
        imag_part = apply_axis(imag_part, cosine, pattern) - apply_axis(
            real_part, sin_table, pattern
        )
        real_part = real_next
    weights = kernel_table()
    real_part = real_part * weights
    imag_part = imag_part * weights
    for pattern in ("xym,xb->bym", "xym,yb->xbm"):
        real_next = apply_axis(real_part, cosine, pattern) - apply_axis(
            imag_part, sin_table, pattern
        )
        imag_part = apply_axis(real_part, sin_table, pattern) + apply_axis(
            imag_part, cosine, pattern
        )
        real_part = real_next
    frequency = jnp.arange(half_len, dtype=jnp.int32)
    fold_weight = jnp.where((frequency == 0) | (frequency == NG // 2), 1.0, 2.0).astype(jnp.float32)
    result = apply_axis(real_part * fold_weight, cos_half, "xym,zm->xyz") - apply_axis(
        imag_part * fold_weight, sin_half, "xym,zm->xyz"
    )
    return (result * (1.0 / (NG * NG * NG))).reshape(-1).astype(jnp.bfloat16)


def plain_body(orbitals, targets, points, fit):
    occupied, shard_len = orbitals.shape
    target_count = targets.shape[0]
    group_size = points.shape[0]
    slab_count = lax.axis_size("slab")
    offsets = points - lax.axis_index("grid") * shard_len
    cell_ids = lax.broadcasted_iota(jnp.int32, (group_size, shard_len), 1)
    one_hot = (cell_ids == offsets[:, None]).astype(jnp.bfloat16)
    point_terms = lax.dot_general(
        orbitals, one_hot, (((1,), (1,)), ((), ())), preferred_element_type=jnp.float32
    )
    at_points = lax.psum(point_terms, "grid").astype(jnp.bfloat16)
    chosen = jnp.take(orbitals, targets, axis=0)
    target_points = jnp.take(at_points, targets, axis=0)
    contract_first = (((0,), (0,)), ((), ()))
    density = lax.dot_general(
        at_points, orbitals, contract_first, preferred_element_type=jnp.float32
    ) * (1.0 / math.sqrt(occupied))
    target_density = lax.dot_general(
        target_points, chosen, contract_first, preferred_element_type=jnp.float32
    ) * (1.0 / math.sqrt(target_count))
    pairs = density * target_density
    fitted = lax.dot_general(
        fit,
        pairs,
        contract_first,
        precision=lax.Precision.HIGHEST,
        preferred_element_type=jnp.float32,
    ).astype(jnp.bfloat16)
    vectors = lax.all_to_all(fitted, "grid", split_axis=0, concat_axis=1, tiled=True)
    potential = lax.map(solve_one, vectors)
    returned = lax.all_to_all(potential, "grid", split_axis=1, concat_axis=0, tiled=True)
    weighted = (returned.astype(jnp.float32) * density).astype(jnp.bfloat16)
    prefactor = -1.0 / math.sqrt(group_size * slab_count)
    regrouped = lax.all_to_all(weighted, "slab", split_axis=1, concat_axis=0, tiled=True)
    all_targets = lax.all_gather(target_points, "slab", axis=1, tiled=True)
    block_out = jnp.dot(all_targets, regrouped, preferred_element_type=jnp.float32)
    summed = lax.all_to_all(block_out, "slab", split_axis=0, concat_axis=1, tiled=True)
    return summed * prefactor


def hartley(length):
    product = np.outer(np.arange(length), np.arange(length)) % length
    angles = product * (2.0 * math.pi / length)
    return (np.cos(angles) + np.sin(angles)) / math.sqrt(length)


def split_table(table):
    upper = table.astype(ml_dtypes.bfloat16)
    lower = (table - upper.astype(np.float64)).astype(ml_dtypes.bfloat16)
    return upper, lower


def split_value(value):
    upper = value.astype(bf16)
    return upper, (value - upper.astype(jnp.float32)).astype(bf16)


class Plan:
    def __init__(self, edge):
        self.edge = edge
        self.half = edge // 2
        self.slot = lanes // 2
        self.inner = lanes // math.gcd(edge, lanes)
        self.outer = edge // self.inner
        self.block = self.inner * edge
        self.block_rows = self.block // lanes
        self.plane_rows = edge * edge // lanes
        self.rows = edge * self.plane_rows
        matrix = hartley(edge)
        pairs = self.inner // 2
        wide = np.zeros((2, self.inner, edge, self.inner, 2, self.slot))
        for h in range(2):
            for y in range(self.inner):
                wide[h, y, :, y, h, :edge] = matrix
        wide = wide.reshape(2, self.block, self.inner * lanes)
        self.forward = []
        for j in range(pairs):
            low = 2 * j * edge // lanes * lanes
            high = -(-(2 * j + 2) * edge // lanes) * lanes
            part = wide[:, low:high, 2 * j * lanes:(2 * j + 2) * lanes].reshape(2 * (high - low), 2 * lanes)
            self.forward.append((low, high, part))
        back = np.transpose(wide, (2, 0, 1))
        self.backward = []
        for c in range(self.block_rows):
            low = c * lanes // edge * lanes
            high = -(-(c + 1) * lanes // edge) * lanes
            part = back[low:high, :, c * lanes:(c + 1) * lanes].reshape(high - low, 2 * lanes)
            self.backward.append((low, high, part))
        step = 2.0 * math.pi / edge
        index = np.arange(edge)
        square = (np.where(index > edge // 2, index - edge, index) * step) ** 2
        weights = screening / (screening + square[:, None, None] + square[None, :, None] + square[None, None, :])
        weights = weights.reshape(2, self.half, edge, edge)
        table = np.zeros((self.half, edge, 2, self.slot))
        table[..., :edge] = np.transpose(weights, (1, 2, 0, 3))
        self.weights = table.reshape(self.half, edge, lanes).astype(np.float32)
        self.left = np.concatenate([*split_table(matrix), split_table(matrix)[0]], axis=1)

    def tables(self):
        fh, fl = split_table(np.concatenate([p for _, _, p in self.forward]))
        bh, bl = split_table(np.concatenate([p for _, _, p in self.backward]))
        return [self.left, fh, fl, bh, bl, self.weights]


def three(value):
    upper, lower = split_value(value)
    return jnp.concatenate([upper, upper, lower], axis=0)


def dot(a, b):
    return jnp.dot(a, b, preferred_element_type=jnp.float32)


def solve(plan, cube, left, fh, fl, bh, bl, weights, mid):
    edge, half, inner, outer = plan.edge, plan.half, plan.inner, plan.outer
    left_all = left[...]
    values = jnp.concatenate(
        [cube[pl.ds(c, edge, stride=plan.plane_rows), :].astype(bf16) for c in range(plan.plane_rows)], axis=1)
    spectrum = dot(left_all[:, :2 * edge], jnp.concatenate([values, values], axis=0))
    folded = jnp.concatenate([
        jnp.concatenate([spectrum[:half, b * plan.block:(b + 1) * plan.block],
                         spectrum[half:, b * plan.block:(b + 1) * plan.block]], axis=1)
        for b in range(outer)], axis=0)
    upper, lower = split_value(folded)
    at = 0
    for j, (low, high, part) in enumerate(plan.forward):
        window = lambda v: jnp.concatenate([v[:, low:high], v[:, plan.block + low:plan.block + high]], axis=1)
        u, l = window(upper), window(lower)
        th, tl = fh[at:at + part.shape[0], :], fl[at:at + part.shape[0], :]
        at += part.shape[0]
        result = dot(u, th) + dot(l, th) + dot(u, tl)
        for b in range(outer):
            for o in range(2):
                y = b * inner + 2 * j + o
                mid[y * half:(y + 1) * half, :] = result[b * half:(b + 1) * half, o * lanes:(o + 1) * lanes]
    for k in range(0, half, 2):
        value = jnp.concatenate([mid[pl.ds(k + o, edge, stride=half), :] for o in range(2)], axis=1)
        value = dot(left_all, three(value))
        value = value * jnp.concatenate([weights[k], weights[k + 1]], axis=1)
        value = dot(left_all, three(value))
        for o in range(2):
            mid[pl.ds(k + o, edge, stride=half), :] = value[:, o * lanes:(o + 1) * lanes]
    value = jnp.concatenate([
        jnp.concatenate([mid[(b * inner + y) * half:(b * inner + y + 1) * half, :] for y in range(inner)], axis=1)
        for b in range(outer)], axis=0)
    upper, lower = split_value(value)
    at = 0
    pieces = []
    for low, high, part in plan.backward:
        u, l = upper[:, low:high], lower[:, low:high]
        th, tl = bh[at:at + part.shape[0], :], bl[at:at + part.shape[0], :]
        at += part.shape[0]
        pieces.append(dot(u, th) + dot(l, th) + dot(u, tl))
    value = jnp.concatenate([
        jnp.concatenate([pieces[c][b * half:(b + 1) * half, :lanes], pieces[c][b * half:(b + 1) * half, lanes:]], axis=0)
        for b in range(outer) for c in range(plan.block_rows)], axis=1)
    value = dot(left_all, three(value))
    for c in range(plan.plane_rows):
        cube[pl.ds(c, edge, stride=plan.plane_rows), :] = value[:, c * lanes:(c + 1) * lanes]


def params(mebibytes):
    return pltpu.CompilerParams(vmem_limit_bytes=mebibytes * 1024 * 1024)


whole = pl.BlockSpec(memory_space=pltpu.VMEM)
scalars = pl.BlockSpec(memory_space=pltpu.SMEM)
anywhere = pl.BlockSpec(memory_space=pl.ANY)


def iota(shape, axis):
    return lax.broadcasted_iota(jnp.int32, shape, axis)


def read_points(orbitals, points):
    occupied, shard_len = orbitals.shape
    group = points.shape[0]

    def kernel(points_ref, orbitals_ref, out_ref, tiles, sems):
        base = lax.axis_index("grid") * shard_len
        rows, columns = iota((8, group * lanes), 0), iota((8, group * lanes), 1)
        chosen = jnp.zeros((8, group * lanes), f32)
        copies = []
        for m in range(group):
            local = points_ref[m] - base
            inside = (local >= 0) & (local < shard_len)
            local = jnp.clip(local, 0, shard_len - 1)
            first = pl.multiple_of(local // lanes * lanes, lanes)
            copy = pltpu.make_async_copy(
                orbitals_ref.at[:, pl.ds(first, lanes)], tiles.at[:, pl.ds(m * lanes, lanes)], sems.at[m])
            copy.start()
            copies.append(copy)
            column = jnp.where(inside, local - first + m * lanes, -1)
            chosen = jnp.where((rows == m) & (columns == column), 1.0, chosen)
        for copy in copies:
            copy.wait()
        chosen = jnp.concatenate([chosen, jnp.zeros_like(chosen)], axis=0).astype(bf16)
        out = lax.dot_general(chosen, tiles[...], contract_last, preferred_element_type=f32)
        out_ref[...] = jnp.concatenate([out[:8], jnp.zeros((8, lanes - occupied), f32)], axis=1)

    return pl.pallas_call(
        kernel,
        out_shape=jax.ShapeDtypeStruct((8, lanes), f32),
        in_specs=[scalars, anywhere],
        out_specs=whole,
        scratch_shapes=[pltpu.VMEM((occupied, group * lanes), bf16), pltpu.SemaphoreType.DMA((group,))],
        compiler_params=params(4),
        name="read_points",
    )(points, orbitals)


def fit_pairs(orbitals, targets, fit, shares):
    occupied, shard_len = orbitals.shape
    count, group = targets.shape[0], fit.shape[0]
    shard_rows = shard_len // lanes
    step = shard_rows // 8
    scale = 1.0 / math.sqrt(occupied) / math.sqrt(count)

    def kernel(targets_ref, fit_ref, orbitals_ref, *refs):
        share_refs, out_refs, at_ref, mid = refs[:group], refs[group:2 * group], refs[2 * group], refs[2 * group + 1]
        me = lax.axis_index("grid")
        at = share_refs[0][...]
        for ref in share_refs[1:]:
            at = at + ref[...]
        at_ref[...] = at
        rows, columns = iota((8, lanes), 0), iota((8, lanes), 1)
        counts = jnp.zeros((8, lanes), f32)
        for k in range(count):
            counts = counts + jnp.where(columns == targets_ref[k], 1.0, 0.0)
        twice = jnp.where(rows < group, at, pltpu.roll(at, group, 0))
        weighted = counts * twice
        upper = weighted.astype(bf16).astype(f32)
        left = jnp.concatenate([twice, upper, weighted - upper, jnp.zeros((8, lanes), f32)], axis=0)
        left = left.astype(bf16)[:, :occupied]
        coefficients = []
        for j in range(group):
            value = jnp.zeros((8, lanes), f32)
            for r in range(8):
                d = r % group
                value = jnp.where(rows == r, fit_ref[(d + j) % group, jnp.bitwise_xor(me, d)], value)
            coefficients.append(value * scale)
        for c in range(0, shard_rows, step):
            product = jnp.dot(left, orbitals_ref[:, c * lanes:(c + step) * lanes], preferred_element_type=f32)
            for r in range(step):
                part = product[:, r * lanes:(r + 1) * lanes]
                pair = part[:8] * (part[8:16] + part[16:24])
                value = pair * coefficients[0]
                for j in range(1, group):
                    value = value + pltpu.roll(pair, 8 - j, 0) * coefficients[j]
                mid[(c + r) * 8:(c + r + 1) * 8, :] = value
        for d in range(group):
            out_refs[d][...] = mid[pl.ds(d, shard_rows, stride=8), :].astype(bf16)

    piece = jax.ShapeDtypeStruct((shard_rows, lanes), bf16)
    return pl.pallas_call(
        kernel,
        out_shape=[piece] * group + [jax.ShapeDtypeStruct((8, lanes), f32)],
        in_specs=[scalars, scalars, whole] + [whole] * group,
        out_specs=[whole] * (group + 1),
        scratch_shapes=[pltpu.VMEM((shard_rows * 8, lanes), f32)],
        compiler_params=params(16),
        name="fit_pairs",
    )(targets, fit, orbitals, *shares)


def potentials(plan, pieces, at, slab_count):
    grid_count, piece_rows = len(pieces), pieces[0].shape[0]
    part = piece_rows // slab_count
    tables = plan.tables()

    def kernel(at_ref, *refs):
        piece_refs, refs = refs[:grid_count], refs[grid_count:]
        table_refs, (out_ref, cube, mid) = refs[:len(tables)], refs[len(tables):]
        me = lax.axis_index("grid")
        for d, ref in enumerate(piece_refs):
            start = pl.multiple_of(jnp.bitwise_xor(me, d) * piece_rows, 8)
            cube[pl.ds(start, piece_rows), :] = ref[...].astype(f32)
        solve(plan, cube, *table_refs, mid)
        own = jnp.broadcast_to(at_ref[pl.ds(me, 1), :], (part + 1, lanes))
        last = iota((part + 1, lanes), 0) == part
        for g in range(grid_count):
            for s in range(slab_count):
                first = g * piece_rows + s * part
                out_ref[s * grid_count + g] = jnp.where(last, own, cube[first:first + part + 1, :]).astype(bf16)

    return pl.pallas_call(
        kernel,
        out_shape=jax.ShapeDtypeStruct((slab_count * grid_count, part + 1, lanes), bf16),
        in_specs=[whole] * (1 + grid_count + len(tables)),
        out_specs=whole,
        scratch_shapes=[
            pltpu.VMEM((plan.rows + 8, lanes), f32),
            pltpu.VMEM((plan.edge * plan.half, lanes), f32),
        ],
        compiler_params=params(24),
        name="potentials",
    )(at, *pieces, *tables)


def apply_part(orbitals, targets, received, slab_count):
    occupied, shard_len = orbitals.shape
    count = targets.shape[0]
    points, part = received.shape[0], received.shape[1] - 1
    keep = count // slab_count
    pitch = -(-(part + 1) // 8) * 8
    prefactor = -1.0 / math.sqrt(points)

    def kernel(targets_ref, orbitals_ref, received_ref, out_ref, spread, mid):
        for m in range(points):
            spread[m * pitch:m * pitch + part + 1, :] = received_ref[m].astype(f32)
        at = spread[pl.ds(part, points, stride=pitch), :][:, :occupied].astype(bf16)
        first = pl.multiple_of(lax.axis_index("slab") * (part * lanes), lanes)
        density = jnp.dot(at, orbitals_ref[:, pl.ds(first, part * lanes)], preferred_element_type=f32)
        rows, columns = iota((count, occupied), 0), iota((count, occupied), 1)
        chosen = jnp.zeros((count, occupied), f32)
        for k in range(count):
            chosen = jnp.where((rows == k) & (columns == targets_ref[k]), 1.0, chosen)
        target_points = lax.dot_general(
            chosen.astype(bf16), at, contract_last, preferred_element_type=f32).astype(bf16)
        potential = jnp.concatenate([spread[pl.ds(r, points, stride=pitch), :] for r in range(part)], axis=1)
        weighted = (potential * (density * (1.0 / math.sqrt(occupied)))).astype(bf16)
        applied = jnp.dot(target_points, weighted, preferred_element_type=f32) * prefactor
        for r in range(part):
            mid[r * count:(r + 1) * count, :] = applied[:, r * lanes:(r + 1) * lanes]
        for s in range(slab_count):
            for k in range(keep):
                out_ref[s, pl.ds(k, part, stride=keep), :] = mid[pl.ds(s * keep + k, part, stride=count), :]

    return pl.pallas_call(
        kernel,
        out_shape=jax.ShapeDtypeStruct((slab_count, part * keep, lanes), f32),
        in_specs=[scalars, whole, whole],
        out_specs=whole,
        scratch_shapes=[pltpu.VMEM((points * pitch, lanes), f32), pltpu.VMEM((part * count, lanes), f32)],
        compiler_params=params(16),
        name="apply_part",
    )(targets, orbitals, received)


def exchange(value, grid_count, offset):
    return lax.ppermute(value, "grid", [(i, i ^ offset) for i in range(grid_count)])


def quick_body(orbitals, targets, points, fit):
    grid_count, slab_count = lax.axis_size("grid"), lax.axis_size("slab")
    shard_len = orbitals.shape[1]
    edge = round((shard_len * grid_count) ** (1 / 3))
    keep = targets.shape[0] // slab_count
    plan = Plan(edge)
    share = read_points(orbitals, points)
    shares = [share] + [exchange(share, grid_count, d) for d in range(1, grid_count)]
    *pieces, at = fit_pairs(orbitals, targets, fit, shares)
    pieces = pieces[:1] + [exchange(pieces[d], grid_count, d) for d in range(1, grid_count)]
    sent = potentials(plan, pieces, at, slab_count)
    received = lax.all_to_all(sent, everyone, 0, 0)
    blocks = apply_part(orbitals, targets, received, slab_count)
    kept = lax.all_to_all(blocks, "slab", 0, 0)
    kept = kept.reshape(-1, keep, lanes)
    return jnp.transpose(kept, (1, 0, 2)).reshape(keep, shard_len)


def quick_fits(mesh, orbitals, targets, points, fit):
    grid_count, slab_count = mesh.shape["grid"], mesh.shape["slab"]
    occupied, cells = orbitals.shape
    group, edge = fit.shape[1], round(cells ** (1 / 3))
    shard_rows = cells // grid_count // lanes
    return (
        group == grid_count
        and 2 * group == 8
        and occupied <= lanes
        and occupied % 16 == 0
        and edge ** 3 == cells
        and edge % 16 == 0
        and edge <= lanes // 2
        and cells % (grid_count * lanes) == 0
        and shard_rows % 8 == 0
        and shard_rows % slab_count == 0
        and targets.shape[0] % slab_count == 0
        and targets.shape[0] % 8 == 0
    )


def solution(mesh):
    in_specs = (P(None, "grid"), P(), P("slab"), P("slab", None))
    out_specs = P("slab", "grid")

    def run(*arrays):
        body = quick_body if quick_fits(mesh, *arrays) else plain_body
        return jax.shard_map(body, mesh=mesh, in_specs=in_specs, out_specs=out_specs, check_vma=False)(*arrays)

    return run
```

```python
import math

import jax
import jax.numpy as jnp
import ml_dtypes
import numpy as np
from jax import lax
from jax.experimental import pallas as pl
from jax.experimental.pallas import tpu as pltpu
from jax.sharding import PartitionSpec as P

NG = 48


screening = 4.0
careful = lax.Precision.HIGH
lanes = 128
f32 = jnp.float32
bf16 = jnp.bfloat16
everyone = ("slab", "grid")
contract_last = (((1,), (1,)), ((), ()))


def dft_tables(length):
    positions = jnp.arange(length, dtype=jnp.int32)
    product = positions[:, None] * positions[None, :] % length
    angles = product.astype(jnp.float32) * (2.0 * math.pi / length)
    return (jnp.cos(angles), jnp.sin(angles))


def kernel_table():
    full_index = jnp.arange(NG, dtype=jnp.int32)
    wrapped = jnp.where(full_index > NG // 2, full_index - NG, full_index).astype(jnp.float32)
    half_index = jnp.arange(NG // 2 + 1, dtype=jnp.int32).astype(jnp.float32)
    step_size = 2.0 * math.pi / NG
    full_sq = wrapped * step_size * (wrapped * step_size)
    half_sq = half_index * step_size * (half_index * step_size)
    summed = full_sq[:, None, None] + full_sq[None, :, None] + half_sq[None, None, :]
    return screening / (screening + summed)


def apply_axis(values, matrix, pattern):
    return jnp.einsum(
        pattern, values, matrix, precision=careful, preferred_element_type=jnp.float32
    )


def split_apply(values, matrix, pattern):
    upper = matrix.astype(jnp.bfloat16)
    lower = (matrix - upper.astype(jnp.float32)).astype(jnp.bfloat16)
    first = jnp.einsum(pattern, values, upper, preferred_element_type=jnp.float32)
    return first + jnp.einsum(pattern, values, lower, preferred_element_type=jnp.float32)


def solve_one(vector_row):
    half_len = NG // 2 + 1
    cosine, sin_table = dft_tables(NG)
    cos_half = cosine[:, :half_len]
    sin_half = sin_table[:, :half_len]
    cube_vals = vector_row.reshape(NG, NG, NG)
    real_part = split_apply(cube_vals, cos_half, "xyz,zm->xym")
    imag_part = -split_apply(cube_vals, sin_half, "xyz,zm->xym")
    for pattern in ("xym,yb->xbm", "xym,xb->bym"):
        real_next = apply_axis(real_part, cosine, pattern) + apply_axis(
            imag_part, sin_table, pattern
        )
        imag_part = apply_axis(imag_part, cosine, pattern) - apply_axis(
            real_part, sin_table, pattern
        )
        real_part = real_next
    weights = kernel_table()
    real_part = real_part * weights
    imag_part = imag_part * weights
    for pattern in ("xym,xb->bym", "xym,yb->xbm"):
        real_next = apply_axis(real_part, cosine, pattern) - apply_axis(
            imag_part, sin_table, pattern
        )
        imag_part = apply_axis(real_part, sin_table, pattern) + apply_axis(
            imag_part, cosine, pattern
        )
        real_part = real_next
    frequency = jnp.arange(half_len, dtype=jnp.int32)
    fold_weight = jnp.where((frequency == 0) | (frequency == NG // 2), 1.0, 2.0).astype(jnp.float32)
    result = apply_axis(real_part * fold_weight, cos_half, "xym,zm->xyz") - apply_axis(
        imag_part * fold_weight, sin_half, "xym,zm->xyz"
    )
    return (result * (1.0 / (NG * NG * NG))).reshape(-1).astype(jnp.bfloat16)


def plain_body(orbitals, targets, points, fit):
    occupied, shard_len = orbitals.shape
    target_count = targets.shape[0]
    group_size = points.shape[0]
    slab_count = lax.axis_size("slab")
    offsets = points - lax.axis_index("grid") * shard_len
    cell_ids = lax.broadcasted_iota(jnp.int32, (group_size, shard_len), 1)
    one_hot = (cell_ids == offsets[:, None]).astype(jnp.bfloat16)
    point_terms = lax.dot_general(
        orbitals, one_hot, (((1,), (1,)), ((), ())), preferred_element_type=jnp.float32
    )
    at_points = lax.psum(point_terms, "grid").astype(jnp.bfloat16)
    chosen = jnp.take(orbitals, targets, axis=0)
    target_points = jnp.take(at_points, targets, axis=0)
    contract_first = (((0,), (0,)), ((), ()))
    density = lax.dot_general(
        at_points, orbitals, contract_first, preferred_element_type=jnp.float32
    ) * (1.0 / math.sqrt(occupied))
    target_density = lax.dot_general(
        target_points, chosen, contract_first, preferred_element_type=jnp.float32
    ) * (1.0 / math.sqrt(target_count))
    pairs = density * target_density
    fitted = lax.dot_general(
        fit,
        pairs,
        contract_first,
        precision=lax.Precision.HIGHEST,
        preferred_element_type=jnp.float32,
    ).astype(jnp.bfloat16)
    vectors = lax.all_to_all(fitted, "grid", split_axis=0, concat_axis=1, tiled=True)
    potential = lax.map(solve_one, vectors)
    returned = lax.all_to_all(potential, "grid", split_axis=1, concat_axis=0, tiled=True)
    weighted = (returned.astype(jnp.float32) * density).astype(jnp.bfloat16)
    prefactor = -1.0 / math.sqrt(group_size * slab_count)
    regrouped = lax.all_to_all(weighted, "slab", split_axis=1, concat_axis=0, tiled=True)
    all_targets = lax.all_gather(target_points, "slab", axis=1, tiled=True)
    block_out = jnp.dot(all_targets, regrouped, preferred_element_type=jnp.float32)
    summed = lax.all_to_all(block_out, "slab", split_axis=0, concat_axis=1, tiled=True)
    return summed * prefactor


def hartley(length):
    product = np.outer(np.arange(length), np.arange(length)) % length
    angles = product * (2.0 * math.pi / length)
    return (np.cos(angles) + np.sin(angles)) / math.sqrt(length)


def split_table(table):
    upper = table.astype(ml_dtypes.bfloat16)
    lower = (table - upper.astype(np.float64)).astype(ml_dtypes.bfloat16)
    return upper, lower


def split_value(value):
    upper = value.astype(bf16)
    return upper, (value - upper.astype(jnp.float32)).astype(bf16)


class Plan:
    def __init__(self, edge):
        self.edge = edge
        self.half = edge // 2
        self.slot = lanes // 2
        self.inner = lanes // math.gcd(edge, lanes)
        self.outer = edge // self.inner
        self.block = self.inner * edge
        self.block_rows = self.block // lanes
        self.plane_rows = edge * edge // lanes
        self.rows = edge * self.plane_rows
        matrix = hartley(edge)
        pairs = self.inner // 2
        wide = np.zeros((2, self.inner, edge, self.inner, 2, self.slot))
        for h in range(2):
            for y in range(self.inner):
                wide[h, y, :, y, h, :edge] = matrix
        wide = wide.reshape(2, self.block, self.inner * lanes)
        self.forward = []
        for j in range(pairs):
            low = 2 * j * edge // lanes * lanes
            high = -(-(2 * j + 2) * edge // lanes) * lanes
            part = wide[:, low:high, 2 * j * lanes:(2 * j + 2) * lanes].reshape(2 * (high - low), 2 * lanes)
            self.forward.append((low, high, part))
        back = np.transpose(wide, (2, 0, 1))
        self.backward = []
        for c in range(self.block_rows):
            low = c * lanes // edge * lanes
            high = -(-(c + 1) * lanes // edge) * lanes
            part = back[low:high, :, c * lanes:(c + 1) * lanes].reshape(high - low, 2 * lanes)
            self.backward.append((low, high, part))
        step = 2.0 * math.pi / edge
        index = np.arange(edge)
        square = (np.where(index > edge // 2, index - edge, index) * step) ** 2
        weights = screening / (screening + square[:, None, None] + square[None, :, None] + square[None, None, :])
        weights = weights.reshape(2, self.half, edge, edge)
        table = np.zeros((self.half, edge, 2, self.slot))
        table[..., :edge] = np.transpose(weights, (1, 2, 0, 3))
        self.weights = table.reshape(self.half, edge, lanes).astype(np.float32)
        self.left = np.concatenate([*split_table(matrix), split_table(matrix)[0]], axis=1)

    def tables(self):
        fh, fl = split_table(np.concatenate([p for _, _, p in self.forward]))
        bh, bl = split_table(np.concatenate([p for _, _, p in self.backward]))
        return [self.left, fh, fl, bh, bl, self.weights]


def three(value):
    upper, lower = split_value(value)
    return jnp.concatenate([upper, upper, lower], axis=0)


def dot(a, b):
    return jnp.dot(a, b, preferred_element_type=jnp.float32)


def solve(plan, cube, left, fh, fl, bh, bl, weights, mid):
    edge, half, inner, outer = plan.edge, plan.half, plan.inner, plan.outer
    left_all = left[...]
    values = jnp.concatenate(
        [cube[pl.ds(c, edge, stride=plan.plane_rows), :].astype(bf16) for c in range(plan.plane_rows)], axis=1)
    spectrum = dot(left_all[:, :2 * edge], jnp.concatenate([values, values], axis=0))
    folded = jnp.concatenate([
        jnp.concatenate([spectrum[:half, b * plan.block:(b + 1) * plan.block],
                         spectrum[half:, b * plan.block:(b + 1) * plan.block]], axis=1)
        for b in range(outer)], axis=0)
    upper, lower = split_value(folded)
    at = 0
    for j, (low, high, part) in enumerate(plan.forward):
        window = lambda v: jnp.concatenate([v[:, low:high], v[:, plan.block + low:plan.block + high]], axis=1)
        u, l = window(upper), window(lower)
        th, tl = fh[at:at + part.shape[0], :], fl[at:at + part.shape[0], :]
        at += part.shape[0]
        result = dot(u, th) + dot(l, th) + dot(u, tl)
        for b in range(outer):
            for o in range(2):
                y = b * inner + 2 * j + o
                mid[y * half:(y + 1) * half, :] = result[b * half:(b + 1) * half, o * lanes:(o + 1) * lanes]
    for k in range(0, half, 2):
        value = jnp.concatenate([mid[pl.ds(k + o, edge, stride=half), :] for o in range(2)], axis=1)
        value = dot(left_all, three(value))
        value = value * jnp.concatenate([weights[k], weights[k + 1]], axis=1)
        value = dot(left_all, three(value))
        for o in range(2):
            mid[pl.ds(k + o, edge, stride=half), :] = value[:, o * lanes:(o + 1) * lanes]
    value = jnp.concatenate([
        jnp.concatenate([mid[(b * inner + y) * half:(b * inner + y + 1) * half, :] for y in range(inner)], axis=1)
        for b in range(outer)], axis=0)
    upper, lower = split_value(value)
    at = 0
    pieces = []
    for low, high, part in plan.backward:
        u, l = upper[:, low:high], lower[:, low:high]
        th, tl = bh[at:at + part.shape[0], :], bl[at:at + part.shape[0], :]
        at += part.shape[0]
        pieces.append(dot(u, th) + dot(l, th) + dot(u, tl))
    value = jnp.concatenate([
        jnp.concatenate([pieces[c][b * half:(b + 1) * half, :lanes], pieces[c][b * half:(b + 1) * half, lanes:]], axis=0)
        for b in range(outer) for c in range(plan.block_rows)], axis=1)
    value = dot(left_all, three(value))
    for c in range(plan.plane_rows):
        cube[pl.ds(c, edge, stride=plan.plane_rows), :] = value[:, c * lanes:(c + 1) * lanes]


def params(mebibytes):
    return pltpu.CompilerParams(vmem_limit_bytes=mebibytes * 1024 * 1024)


whole = pl.BlockSpec(memory_space=pltpu.VMEM)
far = pl.BlockSpec(memory_space=pltpu.HBM)


def iota(shape, axis):
    return lax.broadcasted_iota(jnp.int32, shape, axis)


def read_points(orbitals, targets, points, fit):
    occupied, shard_len = orbitals.shape
    count, group = targets.shape[0], points.shape[0]
    scale = 1.0 / math.sqrt(occupied) / math.sqrt(count)

    def kernel(points_hbm, targets_hbm, fit_hbm, orbitals_ref, out_ref, notes_ref, points_ref, targets_ref, fit_ref, tiles, sems):
        small = [
            pltpu.make_async_copy(source, place, sems.at[group + i])
            for i, (source, place) in enumerate(
                ((points_hbm, points_ref), (targets_hbm, targets_ref), (fit_hbm, fit_ref)))
        ]
        for copy in small:
            copy.start()
        me = lax.axis_index("grid")
        base = me * shard_len
        rows, columns = iota((8, group * lanes), 0), iota((8, group * lanes), 1)
        chosen = jnp.zeros((8, group * lanes), f32)
        copies = []
        small[0].wait()
        for m in range(group):
            local = points_ref[m] - base
            inside = (local >= 0) & (local < shard_len)
            local = jnp.clip(local, 0, shard_len - 1)
            first = pl.multiple_of(local // lanes * lanes, lanes)
            copy = pltpu.make_async_copy(
                orbitals_ref.at[:, pl.ds(first, lanes)], tiles.at[:, pl.ds(m * lanes, lanes)], sems.at[m])
            copy.start()
            copies.append(copy)
            column = jnp.where(inside, local - first + m * lanes, -1)
            chosen = jnp.where((rows == m) & (columns == column), 1.0, chosen)
        chosen = jnp.concatenate([chosen, jnp.zeros_like(chosen)], axis=0).astype(bf16)
        small[1].wait()
        small[2].wait()
        rows, columns = iota((8, lanes), 0), iota((8, lanes), 1)
        counts = jnp.zeros((8, lanes), f32)
        for k in range(count):
            counts = counts + jnp.where(columns == targets_ref[k], 1.0, 0.0)
        notes_ref[:8, :] = counts
        for j in range(group):
            value = jnp.zeros((8, lanes), f32)
            for r in range(8):
                d = r % group
                value = jnp.where(rows == r, fit_ref[(d + j) % group, jnp.bitwise_xor(me, d)], value)
            notes_ref[8 + 8 * j:16 + 8 * j, :] = value * scale
        rows, columns = iota((count, lanes), 0), iota((count, lanes), 1)
        ones = jnp.zeros((count, lanes), f32)
        for k in range(count):
            ones = jnp.where((rows == k) & (columns == targets_ref[k]), 1.0, ones)
        notes_ref[8 + 8 * group:, :] = ones
        for copy in copies:
            copy.wait()
        out = lax.dot_general(chosen, tiles[...], contract_last, preferred_element_type=f32)
        out_ref[...] = jnp.concatenate([out[:8], jnp.zeros((8, lanes - occupied), f32)], axis=1)

    return pl.pallas_call(
        kernel,
        out_shape=[
            jax.ShapeDtypeStruct((8, lanes), f32),
            jax.ShapeDtypeStruct((8 + 8 * group + count, lanes), f32),
        ],
        in_specs=[far] * 4,
        out_specs=[whole] * 2,
        scratch_shapes=[
            pltpu.SMEM(points.shape, jnp.int32),
            pltpu.SMEM(targets.shape, jnp.int32),
            pltpu.SMEM(fit.shape, f32),
            pltpu.VMEM((occupied, group * lanes), bf16),
            pltpu.SemaphoreType.DMA((group + 3,)),
        ],
        compiler_params=params(60),
        name="read_points",
    )(points, targets, fit, orbitals)


def fit_pairs(orbitals, notes, shares):
    occupied, shard_len = orbitals.shape
    group = len(shares)
    shard_rows = shard_len // lanes
    step = shard_rows // 8

    def kernel(notes_ref, orbitals_ref, *refs):
        share_refs, out_refs, at_ref, mid = refs[:group], refs[group:2 * group], refs[2 * group], refs[2 * group + 1]
        at = share_refs[0][...]
        for ref in share_refs[1:]:
            at = at + ref[...]
        at_ref[...] = at
        rows = iota((8, lanes), 0)
        twice = jnp.where(rows < group, at, pltpu.roll(at, group, 0))
        weighted = notes_ref[:8, :] * twice
        upper = weighted.astype(bf16).astype(f32)
        left = jnp.concatenate([twice, upper, weighted - upper, jnp.zeros((8, lanes), f32)], axis=0)
        left = left.astype(bf16)[:, :occupied]
        coefficients = [notes_ref[8 + 8 * j:16 + 8 * j, :] for j in range(group)]
        for c in range(0, shard_rows, step):
            product = jnp.dot(left, orbitals_ref[:, c * lanes:(c + step) * lanes], preferred_element_type=f32)
            for r in range(step):
                part = product[:, r * lanes:(r + 1) * lanes]
                pair = part[:8] * (part[8:16] + part[16:24])
                value = pair * coefficients[0]
                for j in range(1, group):
                    value = value + pltpu.roll(pair, 8 - j, 0) * coefficients[j]
                mid[(c + r) * 8:(c + r + 1) * 8, :] = value
        for d in range(group):
            out_refs[d][...] = mid[pl.ds(d, shard_rows, stride=8), :].astype(bf16)

    piece = jax.ShapeDtypeStruct((shard_rows, lanes), bf16)
    return pl.pallas_call(
        kernel,
        out_shape=[piece] * group + [jax.ShapeDtypeStruct((8, lanes), f32)],
        in_specs=[whole] * (2 + group),
        out_specs=[whole] * (group + 1),
        scratch_shapes=[pltpu.VMEM((shard_rows * 8, lanes), f32)],
        compiler_params=params(16),
        name="fit_pairs",
    )(notes, orbitals, *shares)


def potentials(plan, pieces, at, slab_count):
    grid_count, piece_rows = len(pieces), pieces[0].shape[0]
    part = piece_rows // slab_count
    tables = plan.tables()

    def kernel(at_ref, *refs):
        piece_refs, refs = refs[:grid_count], refs[grid_count:]
        table_refs, (out_ref, cube, mid) = refs[:len(tables)], refs[len(tables):]
        me = lax.axis_index("grid")
        for d, ref in enumerate(piece_refs):
            start = pl.multiple_of(jnp.bitwise_xor(me, d) * piece_rows, 8)
            cube[pl.ds(start, piece_rows), :] = ref[...].astype(f32)
        solve(plan, cube, *table_refs, mid)
        own = jnp.broadcast_to(at_ref[pl.ds(me, 1), :], (part + 1, lanes))
        last = iota((part + 1, lanes), 0) == part
        for g in range(grid_count):
            for s in range(slab_count):
                first = g * piece_rows + s * part
                out_ref[s * grid_count + g] = jnp.where(last, own, cube[first:first + part + 1, :]).astype(bf16)

    return pl.pallas_call(
        kernel,
        out_shape=jax.ShapeDtypeStruct((slab_count * grid_count, part + 1, lanes), bf16),
        in_specs=[whole] * (1 + grid_count + len(tables)),
        out_specs=whole,
        scratch_shapes=[
            pltpu.VMEM((plan.rows + 8, lanes), f32),
            pltpu.VMEM((plan.edge * plan.half, lanes), f32),
        ],
        compiler_params=params(24),
        name="potentials",
    )(at, *pieces, *tables)


def apply_part(orbitals, notes, received, count, slab_count):
    occupied, shard_len = orbitals.shape
    points, part = received.shape[0], received.shape[1] - 1
    keep = count // slab_count
    pitch = -(-(part + 1) // 8) * 8
    prefactor = -1.0 / math.sqrt(points)

    def kernel(notes_ref, orbitals_ref, received_ref, out_ref, spread, mid, stage):
        for m in range(points):
            spread[m * pitch:m * pitch + part + 1, :] = received_ref[m].astype(f32)
        at = spread[pl.ds(part, points, stride=pitch), :][:, :occupied].astype(bf16)
        first = pl.multiple_of(lax.axis_index("slab") * (part * lanes), lanes)
        density = jnp.dot(at, orbitals_ref[:, pl.ds(first, part * lanes)], preferred_element_type=f32)
        chosen = notes_ref[notes_ref.shape[0] - count:, :][:, :occupied].astype(bf16)
        target_points = lax.dot_general(chosen, at, contract_last, preferred_element_type=f32).astype(bf16)
        potential = jnp.concatenate([spread[pl.ds(r, points, stride=pitch), :] for r in range(part)], axis=1)
        weighted = (potential * (density * (1.0 / math.sqrt(occupied)))).astype(bf16)
        applied = jnp.dot(target_points, weighted, preferred_element_type=f32) * prefactor
        for r in range(part):
            mid[r * count:(r + 1) * count, :] = applied[:, r * lanes:(r + 1) * lanes]
        for s in range(slab_count):
            for k in range(keep):
                stage[s, k * part:(k + 1) * part, :] = mid[pl.ds(s * keep + k, part, stride=count), :]
            out_ref[s] = stage[s].astype(bf16)

    return pl.pallas_call(
        kernel,
        out_shape=jax.ShapeDtypeStruct((slab_count, keep * part, lanes), bf16),
        in_specs=[whole] * 3,
        out_specs=whole,
        scratch_shapes=[
            pltpu.VMEM((points * pitch, lanes), f32),
            pltpu.VMEM((part * count, lanes), f32),
            pltpu.VMEM((slab_count, keep * part, lanes), f32),
        ],
        compiler_params=params(16),
        name="apply_part",
    )(notes, orbitals, received)


def settle(kept, keep):
    slab_count, part = kept.shape[0], kept.shape[1] // keep

    def kernel(kept_ref, out_ref, stage):
        for s in range(slab_count):
            stage[s] = kept_ref[s].astype(f32)
            for k in range(keep):
                out_ref[s * part:(s + 1) * part, k, :] = stage[s, k * part:(k + 1) * part, :]

    return pl.pallas_call(
        kernel,
        out_shape=jax.ShapeDtypeStruct((slab_count * part, keep, lanes), f32),
        in_specs=[whole],
        out_specs=whole,
        scratch_shapes=[pltpu.VMEM(kept.shape, f32)],
        compiler_params=params(4),
        name="settle",
    )(kept)


def exchange(value, grid_count, offset):
    return lax.ppermute(value, "grid", [(i, i ^ offset) for i in range(grid_count)])


def quick_body(orbitals, targets, points, fit):
    grid_count, slab_count = lax.axis_size("grid"), lax.axis_size("slab")
    shard_len = orbitals.shape[1]
    edge = round((shard_len * grid_count) ** (1 / 3))
    keep = targets.shape[0] // slab_count
    plan = Plan(edge)
    share, notes = read_points(orbitals, targets, points, fit)
    shares = [share] + [exchange(share, grid_count, d) for d in range(1, grid_count)]
    *pieces, at = fit_pairs(orbitals, notes, shares)
    pieces = pieces[:1] + [exchange(pieces[d], grid_count, d) for d in range(1, grid_count)]
    sent = potentials(plan, pieces, at, slab_count)
    received = lax.all_to_all(sent, everyone, 0, 0)
    blocks = apply_part(orbitals, notes, received, targets.shape[0], slab_count)
    kept = lax.all_to_all(blocks, "slab", 0, 0)
    return jnp.transpose(settle(kept, keep), (1, 0, 2)).reshape(keep, shard_len)


def quick_fits(mesh, orbitals, targets, points, fit):
    grid_count, slab_count = mesh.shape["grid"], mesh.shape["slab"]
    occupied, cells = orbitals.shape
    group, edge = fit.shape[1], round(cells ** (1 / 3))
    shard_rows = cells // grid_count // lanes
    return (
        group == grid_count
        and 2 * group == 8
        and occupied <= lanes
        and occupied % 16 == 0
        and edge ** 3 == cells
        and edge % 16 == 0
        and edge <= lanes // 2
        and cells % (grid_count * lanes) == 0
        and shard_rows % 8 == 0
        and shard_rows % slab_count == 0
        and targets.shape[0] % slab_count == 0
        and targets.shape[0] % 8 == 0
    )


def solution(mesh):
    in_specs = (P(None, "grid"), P(), P("slab"), P("slab", None))
    out_specs = P("slab", "grid")

    def run(*arrays):
        body = quick_body if quick_fits(mesh, *arrays) else plain_body
        return jax.shard_map(body, mesh=mesh, in_specs=in_specs, out_specs=out_specs, check_vma=False)(*arrays)

    return run
```

```python
import math

import jax
import jax.numpy as jnp
import ml_dtypes
import numpy as np
from jax import lax
from jax.experimental import pallas as pl
from jax.experimental.pallas import tpu as pltpu
from jax.sharding import PartitionSpec as P

NG = 48


screening = 4.0
careful = lax.Precision.HIGH
lanes = 128
f32 = jnp.float32
bf16 = jnp.bfloat16
everyone = ("slab", "grid")
contract_last = (((1,), (1,)), ((), ()))


def dft_tables(length):
    positions = jnp.arange(length, dtype=jnp.int32)
    product = positions[:, None] * positions[None, :] % length
    angles = product.astype(jnp.float32) * (2.0 * math.pi / length)
    return (jnp.cos(angles), jnp.sin(angles))


def kernel_table():
    full_index = jnp.arange(NG, dtype=jnp.int32)
    wrapped = jnp.where(full_index > NG // 2, full_index - NG, full_index).astype(jnp.float32)
    half_index = jnp.arange(NG // 2 + 1, dtype=jnp.int32).astype(jnp.float32)
    step_size = 2.0 * math.pi / NG
    full_sq = wrapped * step_size * (wrapped * step_size)
    half_sq = half_index * step_size * (half_index * step_size)
    summed = full_sq[:, None, None] + full_sq[None, :, None] + half_sq[None, None, :]
    return screening / (screening + summed)


def apply_axis(values, matrix, pattern):
    return jnp.einsum(
        pattern, values, matrix, precision=careful, preferred_element_type=jnp.float32
    )


def split_apply(values, matrix, pattern):
    upper = matrix.astype(jnp.bfloat16)
    lower = (matrix - upper.astype(jnp.float32)).astype(jnp.bfloat16)
    first = jnp.einsum(pattern, values, upper, preferred_element_type=jnp.float32)
    return first + jnp.einsum(pattern, values, lower, preferred_element_type=jnp.float32)


def solve_one(vector_row):
    half_len = NG // 2 + 1
    cosine, sin_table = dft_tables(NG)
    cos_half = cosine[:, :half_len]
    sin_half = sin_table[:, :half_len]
    cube_vals = vector_row.reshape(NG, NG, NG)
    real_part = split_apply(cube_vals, cos_half, "xyz,zm->xym")
    imag_part = -split_apply(cube_vals, sin_half, "xyz,zm->xym")
    for pattern in ("xym,yb->xbm", "xym,xb->bym"):
        real_next = apply_axis(real_part, cosine, pattern) + apply_axis(
            imag_part, sin_table, pattern
        )
        imag_part = apply_axis(imag_part, cosine, pattern) - apply_axis(
            real_part, sin_table, pattern
        )
        real_part = real_next
    weights = kernel_table()
    real_part = real_part * weights
    imag_part = imag_part * weights
    for pattern in ("xym,xb->bym", "xym,yb->xbm"):
        real_next = apply_axis(real_part, cosine, pattern) - apply_axis(
            imag_part, sin_table, pattern
        )
        imag_part = apply_axis(real_part, sin_table, pattern) + apply_axis(
            imag_part, cosine, pattern
        )
        real_part = real_next
    frequency = jnp.arange(half_len, dtype=jnp.int32)
    fold_weight = jnp.where((frequency == 0) | (frequency == NG // 2), 1.0, 2.0).astype(jnp.float32)
    result = apply_axis(real_part * fold_weight, cos_half, "xym,zm->xyz") - apply_axis(
        imag_part * fold_weight, sin_half, "xym,zm->xyz"
    )
    return (result * (1.0 / (NG * NG * NG))).reshape(-1).astype(jnp.bfloat16)


def plain_body(orbitals, targets, points, fit):
    occupied, shard_len = orbitals.shape
    target_count = targets.shape[0]
    group_size = points.shape[0]
    slab_count = lax.axis_size("slab")
    offsets = points - lax.axis_index("grid") * shard_len
    cell_ids = lax.broadcasted_iota(jnp.int32, (group_size, shard_len), 1)
    one_hot = (cell_ids == offsets[:, None]).astype(jnp.bfloat16)
    point_terms = lax.dot_general(
        orbitals, one_hot, (((1,), (1,)), ((), ())), preferred_element_type=jnp.float32
    )
    at_points = lax.psum(point_terms, "grid").astype(jnp.bfloat16)
    chosen = jnp.take(orbitals, targets, axis=0)
    target_points = jnp.take(at_points, targets, axis=0)
    contract_first = (((0,), (0,)), ((), ()))
    density = lax.dot_general(
        at_points, orbitals, contract_first, preferred_element_type=jnp.float32
    ) * (1.0 / math.sqrt(occupied))
    target_density = lax.dot_general(
        target_points, chosen, contract_first, preferred_element_type=jnp.float32
    ) * (1.0 / math.sqrt(target_count))
    pairs = density * target_density
    fitted = lax.dot_general(
        fit,
        pairs,
        contract_first,
        precision=lax.Precision.HIGHEST,
        preferred_element_type=jnp.float32,
    ).astype(jnp.bfloat16)
    vectors = lax.all_to_all(fitted, "grid", split_axis=0, concat_axis=1, tiled=True)
    potential = lax.map(solve_one, vectors)
    returned = lax.all_to_all(potential, "grid", split_axis=1, concat_axis=0, tiled=True)
    weighted = (returned.astype(jnp.float32) * density).astype(jnp.bfloat16)
    prefactor = -1.0 / math.sqrt(group_size * slab_count)
    regrouped = lax.all_to_all(weighted, "slab", split_axis=1, concat_axis=0, tiled=True)
    all_targets = lax.all_gather(target_points, "slab", axis=1, tiled=True)
    block_out = jnp.dot(all_targets, regrouped, preferred_element_type=jnp.float32)
    summed = lax.all_to_all(block_out, "slab", split_axis=0, concat_axis=1, tiled=True)
    return summed * prefactor


def hartley(length):
    product = np.outer(np.arange(length), np.arange(length)) % length
    angles = product * (2.0 * math.pi / length)
    return (np.cos(angles) + np.sin(angles)) / math.sqrt(length)


def split_table(table):
    upper = table.astype(ml_dtypes.bfloat16)
    lower = (table - upper.astype(np.float64)).astype(ml_dtypes.bfloat16)
    return upper, lower


def split_value(value):
    upper = value.astype(bf16)
    return upper, (value - upper.astype(jnp.float32)).astype(bf16)


class Plan:
    def __init__(self, edge):
        self.edge = edge
        self.half = edge // 2
        self.slot = lanes // 2
        self.inner = lanes // math.gcd(edge, lanes)
        self.outer = edge // self.inner
        self.block = self.inner * edge
        self.block_rows = self.block // lanes
        self.plane_rows = edge * edge // lanes
        self.rows = edge * self.plane_rows
        matrix = hartley(edge)
        pairs = self.inner // 2
        wide = np.zeros((2, self.inner, edge, self.inner, 2, self.slot))
        for h in range(2):
            for y in range(self.inner):
                wide[h, y, :, y, h, :edge] = matrix
        wide = wide.reshape(2, self.block, self.inner * lanes)
        self.forward = []
        for j in range(pairs):
            low = 2 * j * edge // lanes * lanes
            high = -(-(2 * j + 2) * edge // lanes) * lanes
            part = wide[:, low:high, 2 * j * lanes:(2 * j + 2) * lanes].reshape(2 * (high - low), 2 * lanes)
            self.forward.append((low, high, part))
        back = np.transpose(wide, (2, 0, 1))
        self.backward = []
        for c in range(self.block_rows):
            low = c * lanes // edge * lanes
            high = -(-(c + 1) * lanes // edge) * lanes
            part = back[low:high, :, c * lanes:(c + 1) * lanes].reshape(high - low, 2 * lanes)
            self.backward.append((low, high, part))
        step = 2.0 * math.pi / edge
        index = np.arange(edge)
        square = (np.where(index > edge // 2, index - edge, index) * step) ** 2
        weights = screening / (screening + square[:, None, None] + square[None, :, None] + square[None, None, :])
        weights = weights.reshape(2, self.half, edge, edge)
        table = np.zeros((self.half, edge, 2, self.slot))
        table[..., :edge] = np.transpose(weights, (1, 2, 0, 3))
        self.weights = table.reshape(self.half, edge, lanes).astype(np.float32)
        self.left = np.concatenate([*split_table(matrix), split_table(matrix)[0]], axis=1)

    def tables(self):
        fh, fl = split_table(np.concatenate([p for _, _, p in self.forward]))
        bh, bl = split_table(np.concatenate([p for _, _, p in self.backward]))
        return [self.left, fh, fl, bh, bl, self.weights]


def three(value):
    upper, lower = split_value(value)
    return jnp.concatenate([upper, upper, lower], axis=0)


def dot(a, b):
    return jnp.dot(a, b, preferred_element_type=jnp.float32)


def solve(plan, cube, left, fh, fl, bh, bl, weights, mid):
    edge, half, inner, outer = plan.edge, plan.half, plan.inner, plan.outer
    left_all = left[...]
    values = jnp.concatenate(
        [cube[pl.ds(c, edge, stride=plan.plane_rows), :].astype(bf16) for c in range(plan.plane_rows)], axis=1)
    spectrum = dot(left_all[:, :2 * edge], jnp.concatenate([values, values], axis=0))
    folded = jnp.concatenate([
        jnp.concatenate([spectrum[:half, b * plan.block:(b + 1) * plan.block],
                         spectrum[half:, b * plan.block:(b + 1) * plan.block]], axis=1)
        for b in range(outer)], axis=0)
    upper, lower = split_value(folded)
    at = 0
    for j, (low, high, part) in enumerate(plan.forward):
        window = lambda v: jnp.concatenate([v[:, low:high], v[:, plan.block + low:plan.block + high]], axis=1)
        u, l = window(upper), window(lower)
        th, tl = fh[at:at + part.shape[0], :], fl[at:at + part.shape[0], :]
        at += part.shape[0]
        result = dot(u, th) + dot(l, th) + dot(u, tl)
        for b in range(outer):
            for o in range(2):
                y = b * inner + 2 * j + o
                mid[y * half:(y + 1) * half, :] = result[b * half:(b + 1) * half, o * lanes:(o + 1) * lanes]
    for k in range(0, half, 2):
        value = jnp.concatenate([mid[pl.ds(k + o, edge, stride=half), :] for o in range(2)], axis=1)
        value = dot(left_all, three(value))
        value = value * jnp.concatenate([weights[k], weights[k + 1]], axis=1)
        value = dot(left_all, three(value))
        for o in range(2):
            mid[pl.ds(k + o, edge, stride=half), :] = value[:, o * lanes:(o + 1) * lanes]
    value = jnp.concatenate([
        jnp.concatenate([mid[(b * inner + y) * half:(b * inner + y + 1) * half, :] for y in range(inner)], axis=1)
        for b in range(outer)], axis=0)
    upper, lower = split_value(value)
    at = 0
    pieces = []
    for low, high, part in plan.backward:
        u, l = upper[:, low:high], lower[:, low:high]
        th, tl = bh[at:at + part.shape[0], :], bl[at:at + part.shape[0], :]
        at += part.shape[0]
        pieces.append(dot(u, th) + dot(l, th) + dot(u, tl))
    value = jnp.concatenate([
        jnp.concatenate([pieces[c][b * half:(b + 1) * half, :lanes], pieces[c][b * half:(b + 1) * half, lanes:]], axis=0)
        for b in range(outer) for c in range(plan.block_rows)], axis=1)
    value = dot(left_all, three(value))
    for c in range(plan.plane_rows):
        cube[pl.ds(c, edge, stride=plan.plane_rows), :] = value[:, c * lanes:(c + 1) * lanes]


def params(mebibytes):
    return pltpu.CompilerParams(vmem_limit_bytes=mebibytes * 1024 * 1024)


whole = pl.BlockSpec(memory_space=pltpu.VMEM)
far = pl.BlockSpec(memory_space=pltpu.HBM)


def iota(shape, axis):
    return lax.broadcasted_iota(jnp.int32, shape, axis)


def read_points(orbitals, targets, points, fit):
    occupied, shard_len = orbitals.shape
    count, group = targets.shape[0], points.shape[0]
    scale = 1.0 / math.sqrt(occupied) / math.sqrt(count)

    def kernel(points_hbm, targets_hbm, fit_hbm, orbitals_ref, out_ref, notes_ref, points_ref, targets_ref, fit_ref, tiles, sems):
        small = [
            pltpu.make_async_copy(source, place, sems.at[group + i])
            for i, (source, place) in enumerate(
                ((points_hbm, points_ref), (targets_hbm, targets_ref), (fit_hbm, fit_ref)))
        ]
        for copy in small:
            copy.start()
        me = lax.axis_index("grid")
        base = me * shard_len
        rows, columns = iota((8, group * lanes), 0), iota((8, group * lanes), 1)
        chosen = jnp.zeros((8, group * lanes), f32)
        copies = []
        small[0].wait()
        for m in range(group):
            local = points_ref[m] - base
            inside = (local >= 0) & (local < shard_len)
            local = jnp.clip(local, 0, shard_len - 1)
            first = pl.multiple_of(local // lanes * lanes, lanes)
            copy = pltpu.make_async_copy(
                orbitals_ref.at[:, pl.ds(first, lanes)], tiles.at[:, pl.ds(m * lanes, lanes)], sems.at[m])
            copy.start()
            copies.append(copy)
            column = jnp.where(inside, local - first + m * lanes, -1)
            chosen = jnp.where((rows == m) & (columns == column), 1.0, chosen)
        chosen = jnp.concatenate([chosen, jnp.zeros_like(chosen)], axis=0).astype(bf16)
        small[1].wait()
        small[2].wait()
        rows, columns = iota((8, lanes), 0), iota((8, lanes), 1)
        counts = jnp.zeros((8, lanes), f32)
        for k in range(count):
            counts = counts + jnp.where(columns == targets_ref[k], 1.0, 0.0)
        notes_ref[:8, :] = counts
        for j in range(group):
            value = jnp.zeros((8, lanes), f32)
            for r in range(8):
                d = r % group
                value = jnp.where(rows == r, fit_ref[(d + j) % group, jnp.bitwise_xor(me, d)], value)
            notes_ref[8 + 8 * j:16 + 8 * j, :] = value * scale
        rows, columns = iota((count, lanes), 0), iota((count, lanes), 1)
        ones = jnp.zeros((count, lanes), f32)
        for k in range(count):
            ones = jnp.where((rows == k) & (columns == targets_ref[k]), 1.0, ones)
        notes_ref[8 + 8 * group:, :] = ones
        for copy in copies:
            copy.wait()
        out = lax.dot_general(chosen, tiles[...], contract_last, preferred_element_type=f32)
        out_ref[...] = jnp.concatenate([out[:8], jnp.zeros((8, lanes - occupied), f32)], axis=1)

    return pl.pallas_call(
        kernel,
        out_shape=[
            pltpu.VMEM((8, lanes), f32),
            pltpu.VMEM((8 + 8 * group + count, lanes), f32),
        ],
        in_specs=[far] * 4,
        out_specs=[whole] * 2,
        scratch_shapes=[
            pltpu.SMEM(points.shape, jnp.int32),
            pltpu.SMEM(targets.shape, jnp.int32),
            pltpu.SMEM(fit.shape, f32),
            pltpu.VMEM((occupied, group * lanes), bf16),
            pltpu.SemaphoreType.DMA((group + 3,)),
        ],
        compiler_params=params(4),
        name="read_points",
    )(*[pltpu.with_memory_space_constraint(value, pltpu.HBM) for value in (points, targets, fit, orbitals)])


def fit_pairs(orbitals, notes, shares):
    occupied, shard_len = orbitals.shape
    group = len(shares)
    shard_rows = shard_len // lanes
    step = shard_rows // 8

    def kernel(notes_ref, orbitals_ref, *refs):
        share_refs, out_refs, at_ref, mid = refs[:group], refs[group:2 * group], refs[2 * group], refs[2 * group + 1]
        at = share_refs[0][...]
        for ref in share_refs[1:]:
            at = at + ref[...]
        at_ref[...] = at
        rows = iota((8, lanes), 0)
        twice = jnp.where(rows < group, at, pltpu.roll(at, group, 0))
        weighted = notes_ref[:8, :] * twice
        upper = weighted.astype(bf16).astype(f32)
        left = jnp.concatenate([twice, upper, weighted - upper, jnp.zeros((8, lanes), f32)], axis=0)
        left = left.astype(bf16)[:, :occupied]
        coefficients = [notes_ref[8 + 8 * j:16 + 8 * j, :] for j in range(group)]
        for c in range(0, shard_rows, step):
            product = jnp.dot(left, orbitals_ref[:, c * lanes:(c + step) * lanes], preferred_element_type=f32)
            for r in range(step):
                part = product[:, r * lanes:(r + 1) * lanes]
                pair = part[:8] * (part[8:16] + part[16:24])
                value = pair * coefficients[0]
                for j in range(1, group):
                    value = value + pltpu.roll(pair, 8 - j, 0) * coefficients[j]
                mid[(c + r) * 8:(c + r + 1) * 8, :] = value
        for d in range(group):
            out_refs[d][...] = mid[pl.ds(d, shard_rows, stride=8), :].astype(bf16)

    piece = jax.ShapeDtypeStruct((shard_rows, lanes), bf16)
    return pl.pallas_call(
        kernel,
        out_shape=[piece] * group + [jax.ShapeDtypeStruct((8, lanes), f32)],
        in_specs=[whole] * (2 + group),
        out_specs=[whole] * (group + 1),
        scratch_shapes=[pltpu.VMEM((shard_rows * 8, lanes), f32)],
        compiler_params=params(16),
        name="fit_pairs",
    )(notes, orbitals, *shares)


def potentials(plan, pieces, at, slab_count):
    grid_count, piece_rows = len(pieces), pieces[0].shape[0]
    part = piece_rows // slab_count
    tables = plan.tables()

    def kernel(at_ref, *refs):
        piece_refs, refs = refs[:grid_count], refs[grid_count:]
        table_refs, (out_ref, cube, mid) = refs[:len(tables)], refs[len(tables):]
        me = lax.axis_index("grid")
        for d, ref in enumerate(piece_refs):
            start = pl.multiple_of(jnp.bitwise_xor(me, d) * piece_rows, 8)
            cube[pl.ds(start, piece_rows), :] = ref[...].astype(f32)
        solve(plan, cube, *table_refs, mid)
        own = jnp.broadcast_to(at_ref[pl.ds(me, 1), :], (part + 1, lanes))
        last = iota((part + 1, lanes), 0) == part
        for g in range(grid_count):
            for s in range(slab_count):
                first = g * piece_rows + s * part
                out_ref[s * grid_count + g] = jnp.where(last, own, cube[first:first + part + 1, :]).astype(bf16)

    return pl.pallas_call(
        kernel,
        out_shape=jax.ShapeDtypeStruct((slab_count * grid_count, part + 1, lanes), bf16),
        in_specs=[whole] * (1 + grid_count + len(tables)),
        out_specs=whole,
        scratch_shapes=[
            pltpu.VMEM((plan.rows + 8, lanes), f32),
            pltpu.VMEM((plan.edge * plan.half, lanes), f32),
        ],
        compiler_params=params(24),
        name="potentials",
    )(at, *pieces, *tables)


def apply_part(orbitals, notes, received, count, slab_count):
    occupied, shard_len = orbitals.shape
    points, part = received.shape[0], received.shape[1] - 1
    keep = count // slab_count
    pitch = -(-(part + 1) // 8) * 8
    prefactor = -1.0 / math.sqrt(points)

    def kernel(notes_ref, orbitals_ref, received_ref, out_ref, spread, mid, stage):
        for m in range(points):
            spread[m * pitch:m * pitch + part + 1, :] = received_ref[m].astype(f32)
        at = spread[pl.ds(part, points, stride=pitch), :][:, :occupied].astype(bf16)
        first = pl.multiple_of(lax.axis_index("slab") * (part * lanes), lanes)
        density = jnp.dot(at, orbitals_ref[:, pl.ds(first, part * lanes)], preferred_element_type=f32)
        chosen = notes_ref[notes_ref.shape[0] - count:, :][:, :occupied].astype(bf16)
        target_points = lax.dot_general(chosen, at, contract_last, preferred_element_type=f32).astype(bf16)
        potential = jnp.concatenate([spread[pl.ds(r, points, stride=pitch), :] for r in range(part)], axis=1)
        weighted = (potential * (density * (1.0 / math.sqrt(occupied)))).astype(bf16)
        applied = jnp.dot(target_points, weighted, preferred_element_type=f32) * prefactor
        for r in range(part):
            mid[r * count:(r + 1) * count, :] = applied[:, r * lanes:(r + 1) * lanes]
        for s in range(slab_count):
            for k in range(keep):
                stage[s, k * part:(k + 1) * part, :] = mid[pl.ds(s * keep + k, part, stride=count), :]
            out_ref[s] = stage[s].astype(bf16)

    return pl.pallas_call(
        kernel,
        out_shape=jax.ShapeDtypeStruct((slab_count, keep * part, lanes), bf16),
        in_specs=[whole] * 3,
        out_specs=whole,
        scratch_shapes=[
            pltpu.VMEM((points * pitch, lanes), f32),
            pltpu.VMEM((part * count, lanes), f32),
            pltpu.VMEM((slab_count, keep * part, lanes), f32),
        ],
        compiler_params=params(16),
        name="apply_part",
    )(notes, orbitals, received)


def settle(kept, keep):
    slab_count, part = kept.shape[0], kept.shape[1] // keep

    def kernel(kept_ref, out_ref, stage):
        for s in range(slab_count):
            stage[s] = kept_ref[s].astype(f32)
            for k in range(keep):
                out_ref[s * part:(s + 1) * part, k, :] = stage[s, k * part:(k + 1) * part, :]

    return pl.pallas_call(
        kernel,
        out_shape=jax.ShapeDtypeStruct((slab_count * part, keep, lanes), f32),
        in_specs=[whole],
        out_specs=whole,
        scratch_shapes=[pltpu.VMEM(kept.shape, f32)],
        compiler_params=params(4),
        name="settle",
    )(kept)


def exchange(value, grid_count, offset):
    return lax.ppermute(value, "grid", [(i, i ^ offset) for i in range(grid_count)])


def quick_body(orbitals, targets, points, fit):
    grid_count, slab_count = lax.axis_size("grid"), lax.axis_size("slab")
    shard_len = orbitals.shape[1]
    edge = round((shard_len * grid_count) ** (1 / 3))
    keep = targets.shape[0] // slab_count
    plan = Plan(edge)
    share, notes = read_points(orbitals, targets, points, fit)
    shares = [share] + [exchange(share, grid_count, d) for d in range(1, grid_count)]
    *pieces, at = fit_pairs(orbitals, notes, shares)
    pieces = pieces[:1] + [exchange(pieces[d], grid_count, d) for d in range(1, grid_count)]
    sent = potentials(plan, pieces, at, slab_count)
    received = lax.all_to_all(sent, everyone, 0, 0)
    blocks = apply_part(orbitals, notes, received, targets.shape[0], slab_count)
    kept = lax.all_to_all(blocks, "slab", 0, 0)
    return jnp.transpose(settle(kept, keep), (1, 0, 2)).reshape(keep, shard_len)


def quick_fits(mesh, orbitals, targets, points, fit):
    grid_count, slab_count = mesh.shape["grid"], mesh.shape["slab"]
    occupied, cells = orbitals.shape
    group, edge = fit.shape[1], round(cells ** (1 / 3))
    shard_rows = cells // grid_count // lanes
    return (
        group == grid_count
        and 2 * group == 8
        and occupied <= lanes
        and occupied % 16 == 0
        and edge ** 3 == cells
        and edge % 16 == 0
        and edge <= lanes // 2
        and cells % (grid_count * lanes) == 0
        and shard_rows % 8 == 0
        and shard_rows % slab_count == 0
        and targets.shape[0] % slab_count == 0
        and targets.shape[0] % 8 == 0
    )


def solution(mesh):
    in_specs = (P(None, "grid"), P(), P("slab"), P("slab", None))
    out_specs = P("slab", "grid")

    def run(*arrays):
        body = quick_body if quick_fits(mesh, *arrays) else plain_body
        return jax.shard_map(body, mesh=mesh, in_specs=in_specs, out_specs=out_specs, check_vma=False)(*arrays)

    return run
```

```python
import math

import jax
import jax.numpy as jnp
import ml_dtypes
import numpy as np
from jax import lax
from jax.experimental import pallas as pl
from jax.experimental.pallas import tpu as pltpu
from jax.sharding import PartitionSpec as P

NG = 48


screening = 4.0
careful = lax.Precision.HIGH
lanes = 128
f32 = jnp.float32
bf16 = jnp.bfloat16
everyone = ("slab", "grid")
contract_last = (((1,), (1,)), ((), ()))


def dft_tables(length):
    positions = jnp.arange(length, dtype=jnp.int32)
    product = positions[:, None] * positions[None, :] % length
    angles = product.astype(jnp.float32) * (2.0 * math.pi / length)
    return (jnp.cos(angles), jnp.sin(angles))


def kernel_table():
    full_index = jnp.arange(NG, dtype=jnp.int32)
    wrapped = jnp.where(full_index > NG // 2, full_index - NG, full_index).astype(jnp.float32)
    half_index = jnp.arange(NG // 2 + 1, dtype=jnp.int32).astype(jnp.float32)
    step_size = 2.0 * math.pi / NG
    full_sq = wrapped * step_size * (wrapped * step_size)
    half_sq = half_index * step_size * (half_index * step_size)
    summed = full_sq[:, None, None] + full_sq[None, :, None] + half_sq[None, None, :]
    return screening / (screening + summed)


def apply_axis(values, matrix, pattern):
    return jnp.einsum(
        pattern, values, matrix, precision=careful, preferred_element_type=jnp.float32
    )


def split_apply(values, matrix, pattern):
    upper = matrix.astype(jnp.bfloat16)
    lower = (matrix - upper.astype(jnp.float32)).astype(jnp.bfloat16)
    first = jnp.einsum(pattern, values, upper, preferred_element_type=jnp.float32)
    return first + jnp.einsum(pattern, values, lower, preferred_element_type=jnp.float32)


def solve_one(vector_row):
    half_len = NG // 2 + 1
    cosine, sin_table = dft_tables(NG)
    cos_half = cosine[:, :half_len]
    sin_half = sin_table[:, :half_len]
    cube_vals = vector_row.reshape(NG, NG, NG)
    real_part = split_apply(cube_vals, cos_half, "xyz,zm->xym")
    imag_part = -split_apply(cube_vals, sin_half, "xyz,zm->xym")
    for pattern in ("xym,yb->xbm", "xym,xb->bym"):
        real_next = apply_axis(real_part, cosine, pattern) + apply_axis(
            imag_part, sin_table, pattern
        )
        imag_part = apply_axis(imag_part, cosine, pattern) - apply_axis(
            real_part, sin_table, pattern
        )
        real_part = real_next
    weights = kernel_table()
    real_part = real_part * weights
    imag_part = imag_part * weights
    for pattern in ("xym,xb->bym", "xym,yb->xbm"):
        real_next = apply_axis(real_part, cosine, pattern) - apply_axis(
            imag_part, sin_table, pattern
        )
        imag_part = apply_axis(real_part, sin_table, pattern) + apply_axis(
            imag_part, cosine, pattern
        )
        real_part = real_next
    frequency = jnp.arange(half_len, dtype=jnp.int32)
    fold_weight = jnp.where((frequency == 0) | (frequency == NG // 2), 1.0, 2.0).astype(jnp.float32)
    result = apply_axis(real_part * fold_weight, cos_half, "xym,zm->xyz") - apply_axis(
        imag_part * fold_weight, sin_half, "xym,zm->xyz"
    )
    return (result * (1.0 / (NG * NG * NG))).reshape(-1).astype(jnp.bfloat16)


def plain_body(orbitals, targets, points, fit):
    occupied, shard_len = orbitals.shape
    target_count = targets.shape[0]
    group_size = points.shape[0]
    slab_count = lax.axis_size("slab")
    offsets = points - lax.axis_index("grid") * shard_len
    cell_ids = lax.broadcasted_iota(jnp.int32, (group_size, shard_len), 1)
    one_hot = (cell_ids == offsets[:, None]).astype(jnp.bfloat16)
    point_terms = lax.dot_general(
        orbitals, one_hot, (((1,), (1,)), ((), ())), preferred_element_type=jnp.float32
    )
    at_points = lax.psum(point_terms, "grid").astype(jnp.bfloat16)
    chosen = jnp.take(orbitals, targets, axis=0)
    target_points = jnp.take(at_points, targets, axis=0)
    contract_first = (((0,), (0,)), ((), ()))
    density = lax.dot_general(
        at_points, orbitals, contract_first, preferred_element_type=jnp.float32
    ) * (1.0 / math.sqrt(occupied))
    target_density = lax.dot_general(
        target_points, chosen, contract_first, preferred_element_type=jnp.float32
    ) * (1.0 / math.sqrt(target_count))
    pairs = density * target_density
    fitted = lax.dot_general(
        fit,
        pairs,
        contract_first,
        precision=lax.Precision.HIGHEST,
        preferred_element_type=jnp.float32,
    ).astype(jnp.bfloat16)
    vectors = lax.all_to_all(fitted, "grid", split_axis=0, concat_axis=1, tiled=True)
    potential = lax.map(solve_one, vectors)
    returned = lax.all_to_all(potential, "grid", split_axis=1, concat_axis=0, tiled=True)
    weighted = (returned.astype(jnp.float32) * density).astype(jnp.bfloat16)
    prefactor = -1.0 / math.sqrt(group_size * slab_count)
    regrouped = lax.all_to_all(weighted, "slab", split_axis=1, concat_axis=0, tiled=True)
    all_targets = lax.all_gather(target_points, "slab", axis=1, tiled=True)
    block_out = jnp.dot(all_targets, regrouped, preferred_element_type=jnp.float32)
    summed = lax.all_to_all(block_out, "slab", split_axis=0, concat_axis=1, tiled=True)
    return summed * prefactor


def hartley(length):
    product = np.outer(np.arange(length), np.arange(length)) % length
    angles = product * (2.0 * math.pi / length)
    return (np.cos(angles) + np.sin(angles)) / math.sqrt(length)


def split_table(table):
    upper = table.astype(ml_dtypes.bfloat16)
    lower = (table - upper.astype(np.float64)).astype(ml_dtypes.bfloat16)
    return upper, lower


def split_value(value):
    upper = value.astype(bf16)
    return upper, (value - upper.astype(jnp.float32)).astype(bf16)


class Plan:
    def __init__(self, edge):
        self.edge = edge
        self.half = edge // 2
        self.slot = lanes // 2
        self.inner = lanes // math.gcd(edge, lanes)
        self.outer = edge // self.inner
        self.block = self.inner * edge
        self.block_rows = self.block // lanes
        self.plane_rows = edge * edge // lanes
        self.rows = edge * self.plane_rows
        matrix = hartley(edge)
        self.windows = []
        tables = []
        for j in range(self.inner // 2):
            low, high = 2 * j * edge, (2 * j + 2) * edge
            base = low // lanes * lanes
            self.windows.append((low, high, base))
            table = np.zeros((2 * lanes, 2, 2, self.slot))
            for h in range(2):
                for y in range(2):
                    for z in range(edge):
                        table[(low + y * edge + z - base + h * lanes) % (2 * lanes), y, h, :edge] = matrix[z]
            tables.append(table.reshape(2 * lanes, 2 * lanes))
        self.forward = np.concatenate(tables)
        self.backward = np.concatenate([table.T for table in tables])
        step = 2.0 * math.pi / edge
        index = np.arange(edge)
        square = (np.where(index > edge // 2, index - edge, index) * step) ** 2
        weights = screening / (screening + square[:, None, None] + square[None, :, None] + square[None, None, :])
        weights = weights.reshape(2, self.half, edge, edge)
        table = np.zeros((self.half, edge, 2, self.slot))
        table[..., :edge] = np.transpose(weights, (1, 2, 0, 3))
        self.weights = table.reshape(self.half, edge, lanes).astype(np.float32)
        self.left = np.concatenate([*split_table(matrix), split_table(matrix)[0]], axis=1)

    def tables(self):
        fh, fl = split_table(self.forward)
        bh, bl = split_table(self.backward)
        return [self.left, fh, fl, bh, bl, self.weights]


def three(value):
    upper, lower = split_value(value)
    return jnp.concatenate([upper, upper, lower], axis=0)


def dot(a, b):
    return jnp.dot(a, b, preferred_element_type=jnp.float32)


def product(value, upper_table, lower_table):
    rows = value.shape[0]
    upper, lower = split_value(value)
    both = dot(jnp.concatenate([upper, lower], axis=0), upper_table)
    return both[:rows] + both[rows:] + dot(upper, lower_table)


def solve(plan, cube, left, fh, fl, bh, bl, weights, mid):
    edge, half, inner, outer, block = plan.edge, plan.half, plan.inner, plan.outer, plan.block
    left_all = left[...]
    values = jnp.concatenate(
        [cube[pl.ds(c, edge, stride=plan.plane_rows), :].astype(bf16) for c in range(plan.plane_rows)], axis=1)
    spectrum = dot(left_all[:, :2 * edge], jnp.concatenate([values, values], axis=0))

    def tile(h, c):
        return jnp.concatenate([
            spectrum[h * half:(h + 1) * half, b * block + c * lanes:b * block + (c + 1) * lanes] for b in range(outer)], axis=0)

    lane = lax.broadcasted_iota(jnp.int32, (outer * half, lanes), 1)
    tiles = [[tile(h, c) for c in range(plan.block_rows)] for h in range(2)]
    for j, (low, high, base) in enumerate(plan.windows):
        c = base // lanes
        if high - base <= lanes:
            window = [tiles[0][c], tiles[1][c]]
        else:
            window = [jnp.where(lane >= low - base, tiles[0][c], tiles[1][c + 1]),
                      jnp.where(lane < high - base - lanes, tiles[0][c + 1], tiles[1][c])]
        rows = slice(2 * lanes * j, 2 * lanes * (j + 1))
        result = product(jnp.concatenate(window, axis=1), fh[rows, :], fl[rows, :])
        for b in range(outer):
            for o in range(2):
                y = b * inner + 2 * j + o
                mid[y * half:(y + 1) * half, :] = result[b * half:(b + 1) * half, o * lanes:(o + 1) * lanes]
    for k in range(0, half, 2):
        value = jnp.concatenate([mid[pl.ds(k + o, edge, stride=half), :] for o in range(2)], axis=1)
        value = dot(left_all, three(value))
        value = value * jnp.concatenate([weights[k], weights[k + 1]], axis=1)
        value = dot(left_all, three(value))
        for o in range(2):
            mid[pl.ds(k + o, edge, stride=half), :] = value[:, o * lanes:(o + 1) * lanes]
    results = []
    for j in range(len(plan.windows)):
        rows = slice(2 * lanes * j, 2 * lanes * (j + 1))
        value = jnp.concatenate([
            jnp.concatenate([mid[(b * inner + 2 * j + o) * half:(b * inner + 2 * j + o + 1) * half, :] for b in range(outer)], axis=0)
            for o in range(2)], axis=1)
        results.append(product(value, bh[rows, :], bl[rows, :]))

    def gathered(h, c):
        value = None
        for (low, high, base), result in zip(plan.windows, results):
            if low < (c + 1) * lanes and high > c * lanes:
                place = (c * lanes - base + h * lanes) % (2 * lanes)
                part = result[:, place:place + lanes]
                value = part if value is None else jnp.where(lane >= low - c * lanes, part, value)
        return value

    tiles = [[gathered(h, c) for c in range(plan.block_rows)] for h in range(2)]
    value = jnp.concatenate([
        jnp.concatenate([tiles[h][c][b * half:(b + 1) * half] for h in range(2)], axis=0)
        for b in range(outer) for c in range(plan.block_rows)], axis=1)
    value = dot(left_all, three(value))
    for c in range(plan.plane_rows):
        cube[pl.ds(c, edge, stride=plan.plane_rows), :] = value[:, c * lanes:(c + 1) * lanes]


def params(mebibytes):
    return pltpu.CompilerParams(vmem_limit_bytes=mebibytes * 1024 * 1024)


whole = pl.BlockSpec(memory_space=pltpu.VMEM)
far = pl.BlockSpec(memory_space=pltpu.HBM)


def iota(shape, axis):
    return lax.broadcasted_iota(jnp.int32, shape, axis)


def read_points(orbitals, targets, points, fit):
    occupied, shard_len = orbitals.shape
    count, group = targets.shape[0], points.shape[0]
    scale = 1.0 / math.sqrt(occupied) / math.sqrt(count)

    def kernel(points_hbm, targets_hbm, fit_hbm, orbitals_ref, out_ref, notes_ref, points_ref, targets_ref, fit_ref, tiles, sems):
        small = [
            pltpu.make_async_copy(source, place, sems.at[group + i])
            for i, (source, place) in enumerate(
                ((points_hbm, points_ref), (targets_hbm, targets_ref), (fit_hbm, fit_ref)))
        ]
        for copy in small:
            copy.start()
        me = lax.axis_index("grid")
        base = me * shard_len
        rows, columns = iota((8, group * lanes), 0), iota((8, group * lanes), 1)
        chosen = jnp.zeros((8, group * lanes), f32)
        copies = []
        small[0].wait()
        for m in range(group):
            local = points_ref[m] - base
            inside = (local >= 0) & (local < shard_len)
            local = jnp.clip(local, 0, shard_len - 1)
            first = pl.multiple_of(local // lanes * lanes, lanes)
            copy = pltpu.make_async_copy(
                orbitals_ref.at[:, pl.ds(first, lanes)], tiles.at[:, pl.ds(m * lanes, lanes)], sems.at[m])
            copy.start()
            copies.append(copy)
            column = jnp.where(inside, local - first + m * lanes, -1)
            chosen = jnp.where((rows == m) & (columns == column), 1.0, chosen)
        chosen = jnp.concatenate([chosen, jnp.zeros_like(chosen)], axis=0).astype(bf16)
        small[1].wait()
        small[2].wait()
        rows, columns = iota((8, lanes), 0), iota((8, lanes), 1)
        counts = jnp.zeros((8, lanes), f32)
        for k in range(count):
            counts = counts + jnp.where(columns == targets_ref[k], 1.0, 0.0)
        notes_ref[:8, :] = counts
        for j in range(group):
            value = jnp.zeros((8, lanes), f32)
            for r in range(8):
                d = r % group
                value = jnp.where(rows == r, fit_ref[(d + j) % group, jnp.bitwise_xor(me, d)], value)
            notes_ref[8 + 8 * j:16 + 8 * j, :] = value * scale
        rows, columns = iota((count, lanes), 0), iota((count, lanes), 1)
        ones = jnp.zeros((count, lanes), f32)
        for k in range(count):
            ones = jnp.where((rows == k) & (columns == targets_ref[k]), 1.0, ones)
        notes_ref[8 + 8 * group:, :] = ones
        for copy in copies:
            copy.wait()
        out = lax.dot_general(chosen, tiles[...], contract_last, preferred_element_type=f32)
        out_ref[...] = jnp.concatenate([out[:8], jnp.zeros((8, lanes - occupied), f32)], axis=1)

    return pl.pallas_call(
        kernel,
        out_shape=[
            pltpu.VMEM((8, lanes), f32),
            pltpu.VMEM((8 + 8 * group + count, lanes), f32),
        ],
        in_specs=[far] * 4,
        out_specs=[whole] * 2,
        scratch_shapes=[
            pltpu.SMEM(points.shape, jnp.int32),
            pltpu.SMEM(targets.shape, jnp.int32),
            pltpu.SMEM(fit.shape, f32),
            pltpu.VMEM((occupied, group * lanes), bf16),
            pltpu.SemaphoreType.DMA((group + 3,)),
        ],
        compiler_params=params(4),
        name="read_points",
    )(*[pltpu.with_memory_space_constraint(value, pltpu.HBM) for value in (points, targets, fit, orbitals)])


def fit_pairs(orbitals, notes, shares):
    occupied, shard_len = orbitals.shape
    group = len(shares)
    shard_rows = shard_len // lanes
    step = shard_rows // 8

    def kernel(notes_ref, orbitals_ref, *refs):
        share_refs, out_refs, at_ref, mid = refs[:group], refs[group:2 * group], refs[2 * group], refs[2 * group + 1]
        at = share_refs[0][...]
        for ref in share_refs[1:]:
            at = at + ref[...]
        at_ref[...] = at
        rows = iota((8, lanes), 0)
        twice = jnp.where(rows < group, at, pltpu.roll(at, group, 0))
        weighted = notes_ref[:8, :] * twice
        upper = weighted.astype(bf16).astype(f32)
        left = jnp.concatenate([twice, upper, weighted - upper, jnp.zeros((8, lanes), f32)], axis=0)
        left = left.astype(bf16)[:, :occupied]
        coefficients = [notes_ref[8 + 8 * j:16 + 8 * j, :] for j in range(group)]
        for c in range(0, shard_rows, step):
            product = jnp.dot(left, orbitals_ref[:, c * lanes:(c + step) * lanes], preferred_element_type=f32)
            for r in range(step):
                part = product[:, r * lanes:(r + 1) * lanes]
                pair = part[:8] * (part[8:16] + part[16:24])
                value = pair * coefficients[0]
                for j in range(1, group):
                    value = value + pltpu.roll(pair, 8 - j, 0) * coefficients[j]
                mid[(c + r) * 8:(c + r + 1) * 8, :] = value
        for d in range(group):
            out_refs[d][...] = mid[pl.ds(d, shard_rows, stride=8), :].astype(bf16)

    piece = jax.ShapeDtypeStruct((shard_rows, lanes), bf16)
    return pl.pallas_call(
        kernel,
        out_shape=[piece] * group + [jax.ShapeDtypeStruct((8, lanes), f32)],
        in_specs=[whole] * (2 + group),
        out_specs=[whole] * (group + 1),
        scratch_shapes=[pltpu.VMEM((shard_rows * 8, lanes), f32)],
        compiler_params=params(16),
        name="fit_pairs",
    )(notes, orbitals, *shares)


def potentials(plan, pieces, at, slab_count):
    grid_count, piece_rows = len(pieces), pieces[0].shape[0]
    part = piece_rows // slab_count
    sent = 2 * (part // 2 + 1)
    tables = plan.tables()

    def kernel(at_ref, *refs):
        piece_refs, refs = refs[:grid_count], refs[grid_count:]
        table_refs, (out_ref, cube, mid) = refs[:len(tables)], refs[len(tables):]
        me = lax.axis_index("grid")
        for d, ref in enumerate(piece_refs):
            start = pl.multiple_of(jnp.bitwise_xor(me, d) * piece_rows, 8)
            cube[pl.ds(start, piece_rows), :] = ref[...].astype(f32)
        solve(plan, cube, *table_refs, mid)
        own = jnp.broadcast_to(at_ref[pl.ds(me, 1), :], (sent, lanes))
        last = iota((sent, lanes), 0) >= part
        for g in range(grid_count):
            for s in range(slab_count):
                first = g * piece_rows + s * part
                value = jnp.where(last, own, cube[first:first + sent, :]).astype(bf16)
                out_ref[s * grid_count + g] = value.reshape(sent // 2, 2, lanes)

    return pl.pallas_call(
        kernel,
        out_shape=jax.ShapeDtypeStruct((slab_count * grid_count, sent // 2, 2, lanes), bf16),
        in_specs=[whole] * (1 + grid_count + len(tables)),
        out_specs=whole,
        scratch_shapes=[
            pltpu.VMEM((plan.rows + 8, lanes), f32),
            pltpu.VMEM((plan.edge * plan.half, lanes), f32),
        ],
        compiler_params=params(24),
        name="potentials",
    )(at, *pieces, *tables)


def apply_part(orbitals, notes, received, part, count, slab_count):
    occupied, shard_len = orbitals.shape
    points, sent = received.shape[0], 2 * received.shape[1]
    keep = count // slab_count
    pitch = -(-sent // 8) * 8
    prefactor = -1.0 / math.sqrt(points)

    def kernel(notes_ref, orbitals_ref, received_ref, out_ref, spread, mid, stage):
        for m in range(points):
            spread[m * pitch:m * pitch + sent, :] = received_ref[m].reshape(sent, lanes).astype(f32)
        at = spread[pl.ds(part, points, stride=pitch), :][:, :occupied].astype(bf16)
        first = pl.multiple_of(lax.axis_index("slab") * (part * lanes), lanes)
        density = jnp.dot(at, orbitals_ref[:, pl.ds(first, part * lanes)], preferred_element_type=f32)
        chosen = notes_ref[notes_ref.shape[0] - count:, :][:, :occupied].astype(bf16)
        target_points = lax.dot_general(chosen, at, contract_last, preferred_element_type=f32).astype(bf16)
        potential = jnp.concatenate([spread[pl.ds(r, points, stride=pitch), :] for r in range(part)], axis=1)
        weighted = (potential * (density * (1.0 / math.sqrt(occupied)))).astype(bf16)
        applied = jnp.dot(target_points, weighted, preferred_element_type=f32) * prefactor
        for r in range(part):
            mid[r * count:(r + 1) * count, :] = applied[:, r * lanes:(r + 1) * lanes]
        for s in range(slab_count):
            for k in range(keep):
                stage[s, k * part:(k + 1) * part, :] = mid[pl.ds(s * keep + k, part, stride=count), :]
            out_ref[s] = stage[s].astype(bf16)

    return pl.pallas_call(
        kernel,
        out_shape=jax.ShapeDtypeStruct((slab_count, keep * part, lanes), bf16),
        in_specs=[whole] * 3,
        out_specs=whole,
        scratch_shapes=[
            pltpu.VMEM((points * pitch, lanes), f32),
            pltpu.VMEM((part * count, lanes), f32),
            pltpu.VMEM((slab_count, keep * part, lanes), f32),
        ],
        compiler_params=params(16),
        name="apply_part",
    )(notes, orbitals, received)


def settle(kept, keep):
    slab_count, part = kept.shape[0], kept.shape[1] // keep

    def kernel(kept_ref, out_ref, stage):
        for s in range(slab_count):
            stage[s] = kept_ref[s].astype(f32)
            for k in range(keep):
                out_ref[s * part:(s + 1) * part, k, :] = stage[s, k * part:(k + 1) * part, :]

    return pl.pallas_call(
        kernel,
        out_shape=jax.ShapeDtypeStruct((slab_count * part, keep, lanes), f32),
        in_specs=[whole],
        out_specs=whole,
        scratch_shapes=[pltpu.VMEM(kept.shape, f32)],
        compiler_params=params(4),
        name="settle",
    )(kept)


def exchange(value, grid_count, offset):
    return lax.ppermute(value, "grid", [(i, i ^ offset) for i in range(grid_count)])


def quick_body(orbitals, targets, points, fit):
    grid_count, slab_count = lax.axis_size("grid"), lax.axis_size("slab")
    shard_len = orbitals.shape[1]
    edge = round((shard_len * grid_count) ** (1 / 3))
    keep = targets.shape[0] // slab_count
    plan = Plan(edge)
    share, notes = read_points(orbitals, targets, points, fit)
    shares = [share] + [exchange(share, grid_count, d) for d in range(1, grid_count)]
    *pieces, at = fit_pairs(orbitals, notes, shares)
    pieces = pieces[:1] + [exchange(pieces[d], grid_count, d) for d in range(1, grid_count)]
    sent = potentials(plan, pieces, at, slab_count)
    received = lax.all_to_all(sent, everyone, 0, 0)
    blocks = apply_part(orbitals, notes, received, shard_len // lanes // slab_count, targets.shape[0], slab_count)
    kept = lax.all_to_all(blocks, "slab", 0, 0)
    return jnp.transpose(settle(kept, keep), (1, 0, 2)).reshape(keep, shard_len)


def quick_fits(mesh, orbitals, targets, points, fit):
    grid_count, slab_count = mesh.shape["grid"], mesh.shape["slab"]
    occupied, cells = orbitals.shape
    group, edge = fit.shape[1], round(cells ** (1 / 3))
    shard_rows = cells // grid_count // lanes
    return (
        group == grid_count
        and 2 * group == 8
        and occupied <= lanes
        and occupied % 16 == 0
        and edge ** 3 == cells
        and edge % 16 == 0
        and edge <= lanes // 2
        and cells % (grid_count * lanes) == 0
        and shard_rows % 8 == 0
        and shard_rows % slab_count == 0
        and targets.shape[0] % slab_count == 0
        and targets.shape[0] % 8 == 0
    )


def solution(mesh):
    in_specs = (P(None, "grid"), P(), P("slab"), P("slab", None))
    out_specs = P("slab", "grid")

    def run(*arrays):
        body = quick_body if quick_fits(mesh, *arrays) else plain_body
        return jax.shard_map(body, mesh=mesh, in_specs=in_specs, out_specs=out_specs, check_vma=False)(*arrays)

    return run
```

```python
import math

import jax
import jax.numpy as jnp
import ml_dtypes
import numpy as np
from jax import lax
from jax.experimental import pallas as pl
from jax.experimental.pallas import tpu as pltpu
from jax.sharding import Mesh
from jax.sharding import PartitionSpec as P

NG = 48


screening = 4.0
careful = lax.Precision.HIGH
lanes = 128
f32 = jnp.float32
bf16 = jnp.bfloat16
contract_last = (((1,), (1,)), ((), ()))


def dft_tables(length):
    positions = jnp.arange(length, dtype=jnp.int32)
    product = positions[:, None] * positions[None, :] % length
    angles = product.astype(jnp.float32) * (2.0 * math.pi / length)
    return (jnp.cos(angles), jnp.sin(angles))


def kernel_table():
    full_index = jnp.arange(NG, dtype=jnp.int32)
    wrapped = jnp.where(full_index > NG // 2, full_index - NG, full_index).astype(jnp.float32)
    half_index = jnp.arange(NG // 2 + 1, dtype=jnp.int32).astype(jnp.float32)
    step_size = 2.0 * math.pi / NG
    full_sq = wrapped * step_size * (wrapped * step_size)
    half_sq = half_index * step_size * (half_index * step_size)
    summed = full_sq[:, None, None] + full_sq[None, :, None] + half_sq[None, None, :]
    return screening / (screening + summed)


def apply_axis(values, matrix, pattern):
    return jnp.einsum(
        pattern, values, matrix, precision=careful, preferred_element_type=jnp.float32
    )


def split_apply(values, matrix, pattern):
    upper = matrix.astype(jnp.bfloat16)
    lower = (matrix - upper.astype(jnp.float32)).astype(jnp.bfloat16)
    first = jnp.einsum(pattern, values, upper, preferred_element_type=jnp.float32)
    return first + jnp.einsum(pattern, values, lower, preferred_element_type=jnp.float32)


def solve_one(vector_row):
    half_len = NG // 2 + 1
    cosine, sin_table = dft_tables(NG)
    cos_half = cosine[:, :half_len]
    sin_half = sin_table[:, :half_len]
    cube_vals = vector_row.reshape(NG, NG, NG)
    real_part = split_apply(cube_vals, cos_half, "xyz,zm->xym")
    imag_part = -split_apply(cube_vals, sin_half, "xyz,zm->xym")
    for pattern in ("xym,yb->xbm", "xym,xb->bym"):
        real_next = apply_axis(real_part, cosine, pattern) + apply_axis(
            imag_part, sin_table, pattern
        )
        imag_part = apply_axis(imag_part, cosine, pattern) - apply_axis(
            real_part, sin_table, pattern
        )
        real_part = real_next
    weights = kernel_table()
    real_part = real_part * weights
    imag_part = imag_part * weights
    for pattern in ("xym,xb->bym", "xym,yb->xbm"):
        real_next = apply_axis(real_part, cosine, pattern) - apply_axis(
            imag_part, sin_table, pattern
        )
        imag_part = apply_axis(real_part, sin_table, pattern) + apply_axis(
            imag_part, cosine, pattern
        )
        real_part = real_next
    frequency = jnp.arange(half_len, dtype=jnp.int32)
    fold_weight = jnp.where((frequency == 0) | (frequency == NG // 2), 1.0, 2.0).astype(jnp.float32)
    result = apply_axis(real_part * fold_weight, cos_half, "xym,zm->xyz") - apply_axis(
        imag_part * fold_weight, sin_half, "xym,zm->xyz"
    )
    return (result * (1.0 / (NG * NG * NG))).reshape(-1).astype(jnp.bfloat16)


def plain_body(orbitals, targets, points, fit):
    occupied, shard_len = orbitals.shape
    target_count = targets.shape[0]
    group_size = points.shape[0]
    slab_count = lax.axis_size("slab")
    offsets = points - lax.axis_index("grid") * shard_len
    cell_ids = lax.broadcasted_iota(jnp.int32, (group_size, shard_len), 1)
    one_hot = (cell_ids == offsets[:, None]).astype(jnp.bfloat16)
    point_terms = lax.dot_general(
        orbitals, one_hot, (((1,), (1,)), ((), ())), preferred_element_type=jnp.float32
    )
    at_points = lax.psum(point_terms, "grid").astype(jnp.bfloat16)
    chosen = jnp.take(orbitals, targets, axis=0)
    target_points = jnp.take(at_points, targets, axis=0)
    contract_first = (((0,), (0,)), ((), ()))
    density = lax.dot_general(
        at_points, orbitals, contract_first, preferred_element_type=jnp.float32
    ) * (1.0 / math.sqrt(occupied))
    target_density = lax.dot_general(
        target_points, chosen, contract_first, preferred_element_type=jnp.float32
    ) * (1.0 / math.sqrt(target_count))
    pairs = density * target_density
    fitted = lax.dot_general(
        fit,
        pairs,
        contract_first,
        precision=lax.Precision.HIGHEST,
        preferred_element_type=jnp.float32,
    ).astype(jnp.bfloat16)
    vectors = lax.all_to_all(fitted, "grid", split_axis=0, concat_axis=1, tiled=True)
    potential = lax.map(solve_one, vectors)
    returned = lax.all_to_all(potential, "grid", split_axis=1, concat_axis=0, tiled=True)
    weighted = (returned.astype(jnp.float32) * density).astype(jnp.bfloat16)
    prefactor = -1.0 / math.sqrt(group_size * slab_count)
    regrouped = lax.all_to_all(weighted, "slab", split_axis=1, concat_axis=0, tiled=True)
    all_targets = lax.all_gather(target_points, "slab", axis=1, tiled=True)
    block_out = jnp.dot(all_targets, regrouped, preferred_element_type=jnp.float32)
    summed = lax.all_to_all(block_out, "slab", split_axis=0, concat_axis=1, tiled=True)
    return summed * prefactor


def hartley(length):
    product = np.outer(np.arange(length), np.arange(length)) % length
    angles = product * (2.0 * math.pi / length)
    return (np.cos(angles) + np.sin(angles)) / math.sqrt(length)


def split_table(table):
    upper = table.astype(ml_dtypes.bfloat16)
    lower = (table - upper.astype(np.float64)).astype(ml_dtypes.bfloat16)
    return upper, lower


def split_value(value):
    upper = value.astype(bf16)
    return upper, (value - upper.astype(jnp.float32)).astype(bf16)


class Plan:
    def __init__(self, edge):
        self.edge = edge
        self.half = edge // 2
        self.slot = lanes // 2
        self.inner = lanes // math.gcd(edge, lanes)
        self.outer = edge // self.inner
        self.block = self.inner * edge
        self.block_rows = self.block // lanes
        self.plane_rows = edge * edge // lanes
        self.rows = edge * self.plane_rows
        matrix = hartley(edge)
        self.windows = []
        tables = []
        for j in range(self.inner // 2):
            low, high = 2 * j * edge, (2 * j + 2) * edge
            base = low // lanes * lanes
            self.windows.append((low, high, base))
            table = np.zeros((2 * lanes, 2, 2, self.slot))
            for h in range(2):
                for y in range(2):
                    for z in range(edge):
                        table[(low + y * edge + z - base + h * lanes) % (2 * lanes), y, h, :edge] = matrix[z]
            tables.append(table.reshape(2 * lanes, 2 * lanes))
        self.forward = np.concatenate(tables)
        self.backward = np.concatenate([table.T for table in tables])
        step = 2.0 * math.pi / edge
        index = np.arange(edge)
        square = (np.where(index > edge // 2, index - edge, index) * step) ** 2
        weights = screening / (screening + square[:, None, None] + square[None, :, None] + square[None, None, :])
        weights = weights.reshape(2, self.half, edge, edge)
        table = np.zeros((self.half, edge, 2, self.slot))
        table[..., :edge] = np.transpose(weights, (1, 2, 0, 3))
        self.weights = table.reshape(self.half, edge, lanes).astype(np.float32)
        self.left = np.concatenate([*split_table(matrix), split_table(matrix)[0]], axis=1)

    def tables(self):
        fh, fl = split_table(self.forward)
        bh, bl = split_table(self.backward)
        return [self.left, fh, fl, bh, bl, self.weights]


def three(value):
    upper, lower = split_value(value)
    return jnp.concatenate([upper, upper, lower], axis=0)


def dot(a, b):
    return jnp.dot(a, b, preferred_element_type=jnp.float32)


def product(value, upper_table, lower_table):
    rows = value.shape[0]
    upper, lower = split_value(value)
    both = dot(jnp.concatenate([upper, lower], axis=0), upper_table)
    return both[:rows] + both[rows:] + dot(upper, lower_table)


def solve(plan, cube, left, fh, fl, bh, bl, weights, mid):
    edge, half, inner, outer, block = plan.edge, plan.half, plan.inner, plan.outer, plan.block
    left_all = left[...]
    values = jnp.concatenate(
        [cube[pl.ds(c, edge, stride=plan.plane_rows), :].astype(bf16) for c in range(plan.plane_rows)], axis=1)
    spectrum = dot(left_all[:, :2 * edge], jnp.concatenate([values, values], axis=0))

    def tile(h, c):
        return jnp.concatenate([
            spectrum[h * half:(h + 1) * half, b * block + c * lanes:b * block + (c + 1) * lanes] for b in range(outer)], axis=0)

    lane = lax.broadcasted_iota(jnp.int32, (outer * half, lanes), 1)
    tiles = [[tile(h, c) for c in range(plan.block_rows)] for h in range(2)]
    for j, (low, high, base) in enumerate(plan.windows):
        c = base // lanes
        if high - base <= lanes:
            window = [tiles[0][c], tiles[1][c]]
        else:
            window = [jnp.where(lane >= low - base, tiles[0][c], tiles[1][c + 1]),
                      jnp.where(lane < high - base - lanes, tiles[0][c + 1], tiles[1][c])]
        rows = slice(2 * lanes * j, 2 * lanes * (j + 1))
        result = product(jnp.concatenate(window, axis=1), fh[rows, :], fl[rows, :])
        for b in range(outer):
            for o in range(2):
                y = b * inner + 2 * j + o
                mid[y * half:(y + 1) * half, :] = result[b * half:(b + 1) * half, o * lanes:(o + 1) * lanes]
    for k in range(0, half, 2):
        value = jnp.concatenate([mid[pl.ds(k + o, edge, stride=half), :] for o in range(2)], axis=1)
        value = dot(left_all, three(value))
        value = value * jnp.concatenate([weights[k], weights[k + 1]], axis=1)
        value = dot(left_all, three(value))
        for o in range(2):
            mid[pl.ds(k + o, edge, stride=half), :] = value[:, o * lanes:(o + 1) * lanes]
    results = []
    for j in range(len(plan.windows)):
        rows = slice(2 * lanes * j, 2 * lanes * (j + 1))
        value = jnp.concatenate([
            jnp.concatenate([mid[(b * inner + 2 * j + o) * half:(b * inner + 2 * j + o + 1) * half, :] for b in range(outer)], axis=0)
            for o in range(2)], axis=1)
        results.append(product(value, bh[rows, :], bl[rows, :]))

    def gathered(h, c):
        value = None
        for (low, high, base), result in zip(plan.windows, results):
            if low < (c + 1) * lanes and high > c * lanes:
                place = (c * lanes - base + h * lanes) % (2 * lanes)
                part = result[:, place:place + lanes]
                value = part if value is None else jnp.where(lane >= low - c * lanes, part, value)
        return value

    tiles = [[gathered(h, c) for c in range(plan.block_rows)] for h in range(2)]
    value = jnp.concatenate([
        jnp.concatenate([tiles[h][c][b * half:(b + 1) * half] for h in range(2)], axis=0)
        for b in range(outer) for c in range(plan.block_rows)], axis=1)
    value = dot(left_all, three(value))
    for c in range(plan.plane_rows):
        cube[pl.ds(c, edge, stride=plan.plane_rows), :] = value[:, c * lanes:(c + 1) * lanes]


def params(mebibytes):
    return pltpu.CompilerParams(vmem_limit_bytes=mebibytes * 1024 * 1024)


whole = pl.BlockSpec(memory_space=pltpu.VMEM)
far = pl.BlockSpec(memory_space=pltpu.HBM)


def iota(shape, axis):
    return lax.broadcasted_iota(jnp.int32, shape, axis)


def read_points(orbitals, targets, points, fit):
    occupied, shard_len = orbitals.shape
    count, group = targets.shape[0], points.shape[0]
    scale = 1.0 / math.sqrt(occupied) / math.sqrt(count)

    def kernel(points_hbm, targets_hbm, fit_hbm, orbitals_ref, out_ref, notes_ref, points_ref, targets_ref, fit_ref, tiles, sems):
        small = [
            pltpu.make_async_copy(source, place, sems.at[group + i])
            for i, (source, place) in enumerate(
                ((points_hbm, points_ref), (targets_hbm, targets_ref), (fit_hbm, fit_ref)))
        ]
        for copy in small:
            copy.start()
        me = lax.axis_index("grid")
        base = me * shard_len
        rows, columns = iota((8, group * lanes), 0), iota((8, group * lanes), 1)
        chosen = jnp.zeros((8, group * lanes), f32)
        copies = []
        small[0].wait()
        for m in range(group):
            local = points_ref[m] - base
            inside = (local >= 0) & (local < shard_len)
            local = jnp.clip(local, 0, shard_len - 1)
            first = pl.multiple_of(local // lanes * lanes, lanes)
            copy = pltpu.make_async_copy(
                orbitals_ref.at[:, pl.ds(first, lanes)], tiles.at[:, pl.ds(m * lanes, lanes)], sems.at[m])
            copy.start()
            copies.append(copy)
            column = jnp.where(inside, local - first + m * lanes, -1)
            chosen = jnp.where((rows == m) & (columns == column), 1.0, chosen)
        chosen = jnp.concatenate([chosen, jnp.zeros_like(chosen)], axis=0).astype(bf16)
        small[1].wait()
        small[2].wait()
        rows, columns = iota((8, lanes), 0), iota((8, lanes), 1)
        counts = jnp.zeros((8, lanes), f32)
        for k in range(count):
            counts = counts + jnp.where(columns == targets_ref[k], 1.0, 0.0)
        notes_ref[:8, :] = counts
        for j in range(group):
            value = jnp.zeros((8, lanes), f32)
            for r in range(8):
                d = r % group
                value = jnp.where(rows == r, fit_ref[(d + j) % group, jnp.bitwise_xor(me, d)], value)
            notes_ref[8 + 8 * j:16 + 8 * j, :] = value * scale
        rows, columns = iota((count, lanes), 0), iota((count, lanes), 1)
        ones = jnp.zeros((count, lanes), f32)
        for k in range(count):
            ones = jnp.where((rows == k) & (columns == targets_ref[k]), 1.0, ones)
        notes_ref[8 + 8 * group:, :] = ones
        for copy in copies:
            copy.wait()
        out = lax.dot_general(chosen, tiles[...], contract_last, preferred_element_type=f32)
        out_ref[...] = jnp.concatenate([out[:8], jnp.zeros((8, lanes - occupied), f32)], axis=1)

    return pl.pallas_call(
        kernel,
        out_shape=[
            pltpu.VMEM((8, lanes), f32),
            pltpu.VMEM((8 + 8 * group + count, lanes), f32),
        ],
        in_specs=[far] * 4,
        out_specs=[whole] * 2,
        scratch_shapes=[
            pltpu.SMEM(points.shape, jnp.int32),
            pltpu.SMEM(targets.shape, jnp.int32),
            pltpu.SMEM(fit.shape, f32),
            pltpu.VMEM((occupied, group * lanes), bf16),
            pltpu.SemaphoreType.DMA((group + 3,)),
        ],
        compiler_params=params(4),
        name="read_points",
    )(*[pltpu.with_memory_space_constraint(value, pltpu.HBM) for value in (points, targets, fit, orbitals)])


def fit_pairs(orbitals, notes, shares):
    occupied, shard_len = orbitals.shape
    group = len(shares)
    shard_rows = shard_len // lanes
    step = shard_rows // 8

    def kernel(notes_ref, orbitals_ref, *refs):
        share_refs, out_refs, at_ref, mid = refs[:group], refs[group:2 * group], refs[2 * group], refs[2 * group + 1]
        at = share_refs[0][...]
        for ref in share_refs[1:]:
            at = at + ref[...]
        at_ref[...] = at
        rows = iota((8, lanes), 0)
        twice = jnp.where(rows < group, at, pltpu.roll(at, group, 0))
        weighted = notes_ref[:8, :] * twice
        upper = weighted.astype(bf16).astype(f32)
        left = jnp.concatenate([twice, upper, weighted - upper, jnp.zeros((8, lanes), f32)], axis=0)
        left = left.astype(bf16)[:, :occupied]
        coefficients = [notes_ref[8 + 8 * j:16 + 8 * j, :] for j in range(group)]
        for c in range(0, shard_rows, step):
            product = jnp.dot(left, orbitals_ref[:, c * lanes:(c + step) * lanes], preferred_element_type=f32)
            for r in range(step):
                part = product[:, r * lanes:(r + 1) * lanes]
                pair = part[:8] * (part[8:16] + part[16:24])
                value = pair * coefficients[0]
                for j in range(1, group):
                    value = value + pltpu.roll(pair, 8 - j, 0) * coefficients[j]
                mid[(c + r) * 8:(c + r + 1) * 8, :] = value
        for d in range(group):
            out_refs[d][...] = mid[pl.ds(d, shard_rows, stride=8), :].astype(bf16)

    piece = jax.ShapeDtypeStruct((shard_rows, lanes), bf16)
    return pl.pallas_call(
        kernel,
        out_shape=[piece] * group + [jax.ShapeDtypeStruct((8, lanes), f32)],
        in_specs=[whole] * (2 + group),
        out_specs=[whole] * (group + 1),
        scratch_shapes=[pltpu.VMEM((shard_rows * 8, lanes), f32)],
        compiler_params=params(16),
        name="fit_pairs",
    )(notes, orbitals, *shares)


def potentials(plan, pieces, at, parts):
    grid_count, piece_rows = len(pieces), pieces[0].shape[0]
    part = piece_rows // parts
    sent = -(-(part + 1) // 8) * 8
    tables = plan.tables()

    def kernel(at_ref, *refs):
        piece_refs, refs = refs[:grid_count], refs[grid_count:]
        table_refs, (out_ref, cube, mid) = refs[:len(tables)], refs[len(tables):]
        me = lax.axis_index("grid")
        for d, ref in enumerate(piece_refs):
            start = pl.multiple_of(jnp.bitwise_xor(me, d) * piece_rows, 8)
            cube[pl.ds(start, piece_rows), :] = ref[...].astype(f32)
        solve(plan, cube, *table_refs, mid)
        own = jnp.broadcast_to(at_ref[pl.ds(me, 1), :], (sent, lanes))
        last = iota((sent, lanes), 0) >= part
        for g in range(grid_count):
            for q in range(parts):
                first = g * piece_rows + q * part
                out_ref[q * grid_count + g] = jnp.where(last, own, cube[first:first + sent, :]).astype(bf16)

    return pl.pallas_call(
        kernel,
        out_shape=jax.ShapeDtypeStruct((parts * grid_count, sent, lanes), bf16),
        in_specs=[whole] * (1 + grid_count + len(tables)),
        out_specs=whole,
        scratch_shapes=[
            pltpu.VMEM((plan.rows + 8, lanes), f32),
            pltpu.VMEM((plan.edge * plan.half, lanes), f32),
        ],
        compiler_params=params(24),
        name="potentials",
    )(at, *pieces, *tables)


def apply_part(orbitals, notes, received, part, count, slab_count, halves):
    occupied, shard_len = orbitals.shape
    points, pitch = received.shape[:2]
    keep = count // slab_count
    prefactor = -1.0 / math.sqrt(points * halves)

    def kernel(notes_ref, orbitals_ref, received_ref, out_ref, spread, mid, stage):
        for m in range(points):
            spread[m * pitch:(m + 1) * pitch, :] = received_ref[m].astype(f32)
        at = spread[pl.ds(part, points, stride=pitch), :][:, :occupied].astype(bf16)
        first = pl.multiple_of(lax.axis_index("part") * (part * lanes), lanes)
        density = jnp.dot(at, orbitals_ref[:, pl.ds(first, part * lanes)], preferred_element_type=f32)
        chosen = notes_ref[notes_ref.shape[0] - count:, :][:, :occupied].astype(bf16)
        target_points = lax.dot_general(chosen, at, contract_last, preferred_element_type=f32).astype(bf16)
        potential = jnp.concatenate([spread[pl.ds(r, points, stride=pitch), :] for r in range(part)], axis=1)
        weighted = (potential * (density * (1.0 / math.sqrt(occupied)))).astype(bf16)
        applied = jnp.dot(target_points, weighted, preferred_element_type=f32) * prefactor
        for r in range(part):
            mid[r * count:(r + 1) * count, :] = applied[:, r * lanes:(r + 1) * lanes]
        for s in range(slab_count):
            for k in range(keep):
                stage[s, k * part:(k + 1) * part, :] = mid[pl.ds(s * keep + k, part, stride=count), :]
            out_ref[s] = stage[s].astype(bf16)

    return pl.pallas_call(
        kernel,
        out_shape=jax.ShapeDtypeStruct((slab_count, keep * part, lanes), bf16),
        in_specs=[whole] * 3,
        out_specs=whole,
        scratch_shapes=[
            pltpu.VMEM((points * pitch, lanes), f32),
            pltpu.VMEM((part * count, lanes), f32),
            pltpu.VMEM((slab_count, keep * part, lanes), f32),
        ],
        compiler_params=params(16),
        name="apply_part",
    )(notes, orbitals, received)


def settle(kept, keep, halves):
    parts, rows = kept.shape[0] // halves, kept.shape[1]
    part = rows // keep

    def kernel(kept_ref, out_ref, stage):
        for q in range(parts):
            total = kept_ref[q].astype(f32)
            for h in range(1, halves):
                total = total + kept_ref[h * parts + q].astype(f32)
            stage[q] = total
            for k in range(keep):
                out_ref[q * part:(q + 1) * part, k, :] = stage[q, k * part:(k + 1) * part, :]

    return pl.pallas_call(
        kernel,
        out_shape=jax.ShapeDtypeStruct((parts * part, keep, lanes), f32),
        in_specs=[whole],
        out_specs=whole,
        scratch_shapes=[pltpu.VMEM((parts, rows, lanes), f32)],
        compiler_params=params(4),
        name="settle",
    )(kept)


def exchange(value, grid_count, offset):
    return lax.ppermute(value, "grid", [(i, i ^ offset) for i in range(grid_count)])


def quick_body(orbitals, targets, points, fit):
    grid_count, part_count, halves = (lax.axis_size(name) for name in ("grid", "part", "half"))
    shard_len, slab_count = orbitals.shape[1], part_count * halves
    count = targets.shape[0]
    keep = count // slab_count
    part = shard_len // lanes // part_count
    plan = Plan(round((shard_len * grid_count) ** (1 / 3)))
    share, notes = read_points(orbitals, targets, points, fit)
    shares = [share] + [exchange(share, grid_count, d) for d in range(1, grid_count)]
    *pieces, at = fit_pairs(orbitals, notes, shares)
    pieces = pieces[:1] + [exchange(pieces[d], grid_count, d) for d in range(1, grid_count)]
    sent = potentials(plan, pieces, at, part_count)
    received = lax.all_to_all(sent, ("part", "grid"), 0, 0)
    blocks = apply_part(orbitals, notes, received, part, count, slab_count, halves)
    kept = lax.all_to_all(blocks, ("half", "part"), 0, 0)
    return jnp.transpose(settle(kept, keep, halves), (1, 0, 2)).reshape(keep, shard_len)


def quick_fits(mesh, orbitals, targets, points, fit):
    grid_count, slab_count = mesh.shape["grid"], mesh.shape["slab"]
    occupied, cells = orbitals.shape
    group, edge = fit.shape[1], round(cells ** (1 / 3))
    shard_rows = cells // grid_count // lanes
    return (
        group == grid_count
        and 2 * group == 8
        and occupied <= lanes
        and occupied % 16 == 0
        and edge ** 3 == cells
        and edge % 16 == 0
        and edge <= lanes // 2
        and cells % (grid_count * lanes) == 0
        and shard_rows % 8 == 0
        and slab_count % 2 == 0
        and shard_rows % (slab_count // 2) == 0
        and targets.shape[0] % slab_count == 0
        and targets.shape[0] % 8 == 0
    )


def solution(mesh):
    grid_count, slab_count = mesh.shape["grid"], mesh.shape["slab"]
    out_specs = P("slab", "grid")

    def run(*arrays):
        if not quick_fits(mesh, *arrays):
            in_specs = (P(None, "grid"), P(), P("slab"), P("slab", None))
            return jax.shard_map(plain_body, mesh=mesh, in_specs=in_specs, out_specs=out_specs, check_vma=False)(*arrays)
        halved = Mesh(mesh.devices.reshape(2, slab_count // 2, grid_count), ("half", "part", "grid"))
        slab = ("half", "part")
        in_specs = (P(None, "grid"), P(), P(slab), P(slab, None))
        return jax.shard_map(
            quick_body, mesh=halved, in_specs=in_specs, out_specs=P(slab, "grid"), check_vma=False)(*arrays)

    return run
```

```python
import math

import jax
import jax.numpy as jnp
import ml_dtypes
import numpy as np
from jax import lax
from jax.experimental import pallas as pl
from jax.experimental.pallas import tpu as pltpu
from jax.sharding import Mesh
from jax.sharding import PartitionSpec as P

NG = 48


screening = 4.0
careful = lax.Precision.HIGH
lanes = 128
f32 = jnp.float32
bf16 = jnp.bfloat16
contract_last = (((1,), (1,)), ((), ()))


def dft_tables(length):
    positions = jnp.arange(length, dtype=jnp.int32)
    product = positions[:, None] * positions[None, :] % length
    angles = product.astype(jnp.float32) * (2.0 * math.pi / length)
    return (jnp.cos(angles), jnp.sin(angles))


def kernel_table():
    full_index = jnp.arange(NG, dtype=jnp.int32)
    wrapped = jnp.where(full_index > NG // 2, full_index - NG, full_index).astype(jnp.float32)
    half_index = jnp.arange(NG // 2 + 1, dtype=jnp.int32).astype(jnp.float32)
    step_size = 2.0 * math.pi / NG
    full_sq = wrapped * step_size * (wrapped * step_size)
    half_sq = half_index * step_size * (half_index * step_size)
    summed = full_sq[:, None, None] + full_sq[None, :, None] + half_sq[None, None, :]
    return screening / (screening + summed)


def apply_axis(values, matrix, pattern):
    return jnp.einsum(
        pattern, values, matrix, precision=careful, preferred_element_type=jnp.float32
    )


def split_apply(values, matrix, pattern):
    upper = matrix.astype(jnp.bfloat16)
    lower = (matrix - upper.astype(jnp.float32)).astype(jnp.bfloat16)
    first = jnp.einsum(pattern, values, upper, preferred_element_type=jnp.float32)
    return first + jnp.einsum(pattern, values, lower, preferred_element_type=jnp.float32)


def solve_one(vector_row):
    half_len = NG // 2 + 1
    cosine, sin_table = dft_tables(NG)
    cos_half = cosine[:, :half_len]
    sin_half = sin_table[:, :half_len]
    cube_vals = vector_row.reshape(NG, NG, NG)
    real_part = split_apply(cube_vals, cos_half, "xyz,zm->xym")
    imag_part = -split_apply(cube_vals, sin_half, "xyz,zm->xym")
    for pattern in ("xym,yb->xbm", "xym,xb->bym"):
        real_next = apply_axis(real_part, cosine, pattern) + apply_axis(
            imag_part, sin_table, pattern
        )
        imag_part = apply_axis(imag_part, cosine, pattern) - apply_axis(
            real_part, sin_table, pattern
        )
        real_part = real_next
    weights = kernel_table()
    real_part = real_part * weights
    imag_part = imag_part * weights
    for pattern in ("xym,xb->bym", "xym,yb->xbm"):
        real_next = apply_axis(real_part, cosine, pattern) - apply_axis(
            imag_part, sin_table, pattern
        )
        imag_part = apply_axis(real_part, sin_table, pattern) + apply_axis(
            imag_part, cosine, pattern
        )
        real_part = real_next
    frequency = jnp.arange(half_len, dtype=jnp.int32)
    fold_weight = jnp.where((frequency == 0) | (frequency == NG // 2), 1.0, 2.0).astype(jnp.float32)
    result = apply_axis(real_part * fold_weight, cos_half, "xym,zm->xyz") - apply_axis(
        imag_part * fold_weight, sin_half, "xym,zm->xyz"
    )
    return (result * (1.0 / (NG * NG * NG))).reshape(-1).astype(jnp.bfloat16)


def plain_body(orbitals, targets, points, fit):
    occupied, shard_len = orbitals.shape
    target_count = targets.shape[0]
    group_size = points.shape[0]
    slab_count = lax.axis_size("slab")
    offsets = points - lax.axis_index("grid") * shard_len
    cell_ids = lax.broadcasted_iota(jnp.int32, (group_size, shard_len), 1)
    one_hot = (cell_ids == offsets[:, None]).astype(jnp.bfloat16)
    point_terms = lax.dot_general(
        orbitals, one_hot, (((1,), (1,)), ((), ())), preferred_element_type=jnp.float32
    )
    at_points = lax.psum(point_terms, "grid").astype(jnp.bfloat16)
    chosen = jnp.take(orbitals, targets, axis=0)
    target_points = jnp.take(at_points, targets, axis=0)
    contract_first = (((0,), (0,)), ((), ()))
    density = lax.dot_general(
        at_points, orbitals, contract_first, preferred_element_type=jnp.float32
    ) * (1.0 / math.sqrt(occupied))
    target_density = lax.dot_general(
        target_points, chosen, contract_first, preferred_element_type=jnp.float32
    ) * (1.0 / math.sqrt(target_count))
    pairs = density * target_density
    fitted = lax.dot_general(
        fit,
        pairs,
        contract_first,
        precision=lax.Precision.HIGHEST,
        preferred_element_type=jnp.float32,
    ).astype(jnp.bfloat16)
    vectors = lax.all_to_all(fitted, "grid", split_axis=0, concat_axis=1, tiled=True)
    potential = lax.map(solve_one, vectors)
    returned = lax.all_to_all(potential, "grid", split_axis=1, concat_axis=0, tiled=True)
    weighted = (returned.astype(jnp.float32) * density).astype(jnp.bfloat16)
    prefactor = -1.0 / math.sqrt(group_size * slab_count)
    regrouped = lax.all_to_all(weighted, "slab", split_axis=1, concat_axis=0, tiled=True)
    all_targets = lax.all_gather(target_points, "slab", axis=1, tiled=True)
    block_out = jnp.dot(all_targets, regrouped, preferred_element_type=jnp.float32)
    summed = lax.all_to_all(block_out, "slab", split_axis=0, concat_axis=1, tiled=True)
    return summed * prefactor


def hartley(length):
    product = np.outer(np.arange(length), np.arange(length)) % length
    angles = product * (2.0 * math.pi / length)
    return (np.cos(angles) + np.sin(angles)) / math.sqrt(length)


def split_table(table):
    upper = table.astype(ml_dtypes.bfloat16)
    lower = (table - upper.astype(np.float64)).astype(ml_dtypes.bfloat16)
    return upper, lower


def split_value(value):
    upper = value.astype(bf16)
    return upper, (value - upper.astype(jnp.float32)).astype(bf16)


class Plan:
    def __init__(self, edge):
        self.edge = edge
        self.half = edge // 2
        self.slot = lanes // 2
        self.inner = lanes // math.gcd(edge, lanes)
        self.outer = edge // self.inner
        self.block = self.inner * edge
        self.block_rows = self.block // lanes
        self.plane_rows = edge * edge // lanes
        self.rows = edge * self.plane_rows
        matrix = hartley(edge)
        self.windows = []
        tables = []
        for j in range(self.inner // 2):
            low, high = 2 * j * edge, (2 * j + 2) * edge
            base = low // lanes * lanes
            self.windows.append((low, high, base))
            table = np.zeros((2 * lanes, 2, 2, self.slot))
            for h in range(2):
                for y in range(2):
                    for z in range(edge):
                        table[(low + y * edge + z - base + h * lanes) % (2 * lanes), y, h, :edge] = matrix[z]
            tables.append(table.reshape(2 * lanes, 2 * lanes))
        self.forward = np.concatenate(tables)
        self.backward = np.concatenate([table.T for table in tables])
        step = 2.0 * math.pi / edge
        index = np.arange(edge)
        square = (np.where(index > edge // 2, index - edge, index) * step) ** 2
        weights = screening / (screening + square[:, None, None] + square[None, :, None] + square[None, None, :])
        weights = weights.reshape(2, self.half, edge, edge)
        table = np.zeros((self.half, edge, 2, self.slot))
        table[..., :edge] = np.transpose(weights, (1, 2, 0, 3))
        self.weights = table.reshape(self.half, edge, lanes).astype(np.float32)
        self.left = np.concatenate([*split_table(matrix), split_table(matrix)[0]], axis=1)

    def tables(self):
        fh, fl = split_table(self.forward)
        bh, bl = split_table(self.backward)
        return [self.left, fh, fl, bh, bl, self.weights]


def three(value):
    upper, lower = split_value(value)
    return jnp.concatenate([upper, upper, lower], axis=0)


def dot(a, b):
    return jnp.dot(a, b, preferred_element_type=jnp.float32)


def product(value, upper_table, lower_table):
    rows = value.shape[0]
    upper, lower = split_value(value)
    both = dot(jnp.concatenate([upper, lower], axis=0), upper_table)
    return both[:rows] + both[rows:] + dot(upper, lower_table)


def solve(plan, cube, left, fh, fl, bh, bl, weights, mid):
    edge, half, inner, outer, block = plan.edge, plan.half, plan.inner, plan.outer, plan.block
    left_all = left[...]
    values = jnp.concatenate(
        [cube[pl.ds(c, edge, stride=plan.plane_rows), :].astype(bf16) for c in range(plan.plane_rows)], axis=1)
    spectrum = dot(left_all[:, :2 * edge], jnp.concatenate([values, values], axis=0))

    def tile(h, c):
        return jnp.concatenate([
            spectrum[h * half:(h + 1) * half, b * block + c * lanes:b * block + (c + 1) * lanes] for b in range(outer)], axis=0)

    lane = lax.broadcasted_iota(jnp.int32, (outer * half, lanes), 1)
    tiles = [[tile(h, c) for c in range(plan.block_rows)] for h in range(2)]
    for j, (low, high, base) in enumerate(plan.windows):
        c = base // lanes
        if high - base <= lanes:
            window = [tiles[0][c], tiles[1][c]]
        else:
            window = [jnp.where(lane >= low - base, tiles[0][c], tiles[1][c + 1]),
                      jnp.where(lane < high - base - lanes, tiles[0][c + 1], tiles[1][c])]
        rows = slice(2 * lanes * j, 2 * lanes * (j + 1))
        result = product(jnp.concatenate(window, axis=1), fh[rows, :], fl[rows, :])
        for b in range(outer):
            for o in range(2):
                y = b * inner + 2 * j + o
                mid[y * half:(y + 1) * half, :] = result[b * half:(b + 1) * half, o * lanes:(o + 1) * lanes]
    for k in range(0, half, 2):
        value = jnp.concatenate([mid[pl.ds(k + o, edge, stride=half), :] for o in range(2)], axis=1)
        value = dot(left_all, three(value))
        value = value * jnp.concatenate([weights[k], weights[k + 1]], axis=1)
        value = dot(left_all, three(value))
        for o in range(2):
            mid[pl.ds(k + o, edge, stride=half), :] = value[:, o * lanes:(o + 1) * lanes]
    results = []
    for j in range(len(plan.windows)):
        rows = slice(2 * lanes * j, 2 * lanes * (j + 1))
        value = jnp.concatenate([
            jnp.concatenate([mid[(b * inner + 2 * j + o) * half:(b * inner + 2 * j + o + 1) * half, :] for b in range(outer)], axis=0)
            for o in range(2)], axis=1)
        results.append(product(value, bh[rows, :], bl[rows, :]))

    def gathered(h, c):
        value = None
        for (low, high, base), result in zip(plan.windows, results):
            if low < (c + 1) * lanes and high > c * lanes:
                place = (c * lanes - base + h * lanes) % (2 * lanes)
                part = result[:, place:place + lanes]
                value = part if value is None else jnp.where(lane >= low - c * lanes, part, value)
        return value

    tiles = [[gathered(h, c) for c in range(plan.block_rows)] for h in range(2)]
    value = jnp.concatenate([
        jnp.concatenate([tiles[h][c][b * half:(b + 1) * half] for h in range(2)], axis=0)
        for b in range(outer) for c in range(plan.block_rows)], axis=1)
    value = dot(left_all, three(value))
    for c in range(plan.plane_rows):
        cube[pl.ds(c, edge, stride=plan.plane_rows), :] = value[:, c * lanes:(c + 1) * lanes]


def params(mebibytes):
    return pltpu.CompilerParams(vmem_limit_bytes=mebibytes * 1024 * 1024)


whole = pl.BlockSpec(memory_space=pltpu.VMEM)
far = pl.BlockSpec(memory_space=pltpu.HBM)


def iota(shape, axis):
    return lax.broadcasted_iota(jnp.int32, shape, axis)


def read_points(orbitals, targets, points, fit):
    occupied, shard_len = orbitals.shape
    count, group = targets.shape[0], points.shape[0]
    scale = 1.0 / math.sqrt(occupied) / math.sqrt(count)

    def kernel(points_hbm, targets_hbm, fit_hbm, orbitals_ref, out_ref, notes_ref, points_ref, targets_ref, fit_ref, tiles, sems):
        small = [
            pltpu.make_async_copy(source, place, sems.at[group + i])
            for i, (source, place) in enumerate(
                ((points_hbm, points_ref), (targets_hbm, targets_ref), (fit_hbm, fit_ref)))
        ]
        for copy in small:
            copy.start()
        me = lax.axis_index("grid")
        base = me * shard_len
        rows, columns = iota((8, group * lanes), 0), iota((8, group * lanes), 1)
        chosen = jnp.zeros((8, group * lanes), f32)
        copies = []
        small[0].wait()
        for m in range(group):
            local = points_ref[m] - base
            inside = (local >= 0) & (local < shard_len)
            local = jnp.clip(local, 0, shard_len - 1)
            first = pl.multiple_of(local // lanes * lanes, lanes)
            copy = pltpu.make_async_copy(
                orbitals_ref.at[:, pl.ds(first, lanes)], tiles.at[:, pl.ds(m * lanes, lanes)], sems.at[m])
            copy.start()
            copies.append(copy)
            column = jnp.where(inside, local - first + m * lanes, -1)
            chosen = jnp.where((rows == m) & (columns == column), 1.0, chosen)
        chosen = jnp.concatenate([chosen, jnp.zeros_like(chosen)], axis=0).astype(bf16)
        small[1].wait()
        small[2].wait()
        rows, columns = iota((8, lanes), 0), iota((8, lanes), 1)
        counts = jnp.zeros((8, lanes), f32)
        for k in range(count):
            counts = counts + jnp.where(columns == targets_ref[k], 1.0, 0.0)
        notes_ref[:8, :] = counts
        for j in range(group):
            value = jnp.zeros((8, lanes), f32)
            for r in range(8):
                d = r % group
                value = jnp.where(rows == r, fit_ref[(d + j) % group, jnp.bitwise_xor(me, d)], value)
            notes_ref[8 + 8 * j:16 + 8 * j, :] = value * scale
        rows, columns = iota((count, lanes), 0), iota((count, lanes), 1)
        ones = jnp.zeros((count, lanes), f32)
        for k in range(count):
            ones = jnp.where((rows == k) & (columns == targets_ref[k]), 1.0, ones)
        notes_ref[8 + 8 * group:, :] = ones
        for copy in copies:
            copy.wait()
        out = lax.dot_general(chosen, tiles[...], contract_last, preferred_element_type=f32)
        out_ref[...] = jnp.concatenate([out[:8], jnp.zeros((8, lanes - occupied), f32)], axis=1)

    return pl.pallas_call(
        kernel,
        out_shape=[
            pltpu.VMEM((8, lanes), f32),
            pltpu.VMEM((8 + 8 * group + count, lanes), f32),
        ],
        in_specs=[far] * 4,
        out_specs=[whole] * 2,
        scratch_shapes=[
            pltpu.SMEM(points.shape, jnp.int32),
            pltpu.SMEM(targets.shape, jnp.int32),
            pltpu.SMEM(fit.shape, f32),
            pltpu.VMEM((occupied, group * lanes), bf16),
            pltpu.SemaphoreType.DMA((group + 3,)),
        ],
        compiler_params=params(4),
        name="read_points",
    )(*[pltpu.with_memory_space_constraint(value, pltpu.HBM) for value in (points, targets, fit, orbitals)])


def fit_pairs(orbitals, notes, shares):
    occupied, shard_len = orbitals.shape
    group = len(shares)
    shard_rows = shard_len // lanes
    step = shard_rows // 8

    def kernel(notes_ref, orbitals_ref, *refs):
        share_refs, out_refs, at_ref, mid = refs[:group], refs[group:2 * group], refs[2 * group], refs[2 * group + 1]
        at = share_refs[0][...]
        for ref in share_refs[1:]:
            at = at + ref[...]
        at_ref[...] = at
        rows = iota((8, lanes), 0)
        twice = jnp.where(rows < group, at, pltpu.roll(at, group, 0))
        weighted = notes_ref[:8, :] * twice
        upper = weighted.astype(bf16).astype(f32)
        left = jnp.concatenate([twice, upper, weighted - upper, jnp.zeros((8, lanes), f32)], axis=0)
        left = left.astype(bf16)[:, :occupied]
        coefficients = [notes_ref[8 + 8 * j:16 + 8 * j, :] for j in range(group)]
        for c in range(0, shard_rows, step):
            product = jnp.dot(left, orbitals_ref[:, c * lanes:(c + step) * lanes], preferred_element_type=f32)
            for r in range(step):
                part = product[:, r * lanes:(r + 1) * lanes]
                pair = part[:8] * (part[8:16] + part[16:24])
                value = pair * coefficients[0]
                for j in range(1, group):
                    value = value + pltpu.roll(pair, 8 - j, 0) * coefficients[j]
                mid[(c + r) * 8:(c + r + 1) * 8, :] = value
        for d in range(group):
            out_refs[d][...] = mid[pl.ds(d, shard_rows, stride=8), :].astype(bf16)

    piece = jax.ShapeDtypeStruct((shard_rows, lanes), bf16)
    return pl.pallas_call(
        kernel,
        out_shape=[piece] * group + [jax.ShapeDtypeStruct((8, lanes), f32)],
        in_specs=[whole] * (2 + group),
        out_specs=[whole] * (group + 1),
        scratch_shapes=[pltpu.VMEM((shard_rows * 8, lanes), f32)],
        compiler_params=params(16),
        name="fit_pairs",
    )(notes, orbitals, *shares)


def potentials(plan, pieces, at, parts, place):
    grid_count, piece_rows = len(pieces), pieces[0].shape[0]
    part = piece_rows // parts
    sent = -(-(part + 1) // 8) * 8
    tables = plan.tables()

    def kernel(at_ref, *refs):
        piece_refs, refs = refs[:grid_count], refs[grid_count:]
        table_refs, (out_ref, cube, mid) = refs[:len(tables)], refs[len(tables):]
        me = lax.axis_index("grid")
        for d, ref in enumerate(piece_refs):
            start = pl.multiple_of(jnp.bitwise_xor(me, d) * piece_rows, 8)
            cube[pl.ds(start, piece_rows), :] = ref[...].astype(f32)
        solve(plan, cube, *table_refs, mid)
        own = jnp.broadcast_to(at_ref[pl.ds(me, 1), :], (sent, lanes))
        last = iota((sent, lanes), 0) >= part
        for g in range(grid_count):
            for q in range(parts):
                first = g * piece_rows + q * part
                out_ref[place[q * grid_count + g]] = jnp.where(last, own, cube[first:first + sent, :]).astype(bf16)

    return pl.pallas_call(
        kernel,
        out_shape=jax.ShapeDtypeStruct((parts * grid_count, sent, lanes), bf16),
        in_specs=[whole] * (1 + grid_count + len(tables)),
        out_specs=whole,
        scratch_shapes=[
            pltpu.VMEM((plan.rows + 8, lanes), f32),
            pltpu.VMEM((plan.edge * plan.half, lanes), f32),
        ],
        compiler_params=params(24),
        name="potentials",
    )(at, *pieces, *tables)


def apply_part(orbitals, notes, received, part, count, place, halves):
    occupied, shard_len = orbitals.shape
    points, pitch = received.shape[:2]
    slab_count = len(place)
    keep = count // slab_count
    prefactor = -1.0 / math.sqrt(points * halves)

    def kernel(notes_ref, orbitals_ref, received_ref, out_ref, spread, mid, stage):
        for m in range(points):
            spread[m * pitch:(m + 1) * pitch, :] = received_ref[m].astype(f32)
        at = spread[pl.ds(part, points, stride=pitch), :][:, :occupied].astype(bf16)
        first = pl.multiple_of(lax.axis_index("part") * (part * lanes), lanes)
        density = jnp.dot(at, orbitals_ref[:, pl.ds(first, part * lanes)], preferred_element_type=f32)
        chosen = notes_ref[notes_ref.shape[0] - count:, :][:, :occupied].astype(bf16)
        target_points = lax.dot_general(chosen, at, contract_last, preferred_element_type=f32).astype(bf16)
        potential = jnp.concatenate([spread[pl.ds(r, points, stride=pitch), :] for r in range(part)], axis=1)
        weighted = (potential * (density * (1.0 / math.sqrt(occupied)))).astype(bf16)
        applied = jnp.dot(target_points, weighted, preferred_element_type=f32) * prefactor
        for r in range(part):
            mid[r * count:(r + 1) * count, :] = applied[:, r * lanes:(r + 1) * lanes]
        for s in range(slab_count):
            for k in range(keep):
                stage[s, k * part:(k + 1) * part, :] = mid[pl.ds(s * keep + k, part, stride=count), :]
            out_ref[place[s]] = stage[s].astype(bf16)

    return pl.pallas_call(
        kernel,
        out_shape=jax.ShapeDtypeStruct((slab_count, keep * part, lanes), bf16),
        in_specs=[whole] * 3,
        out_specs=whole,
        scratch_shapes=[
            pltpu.VMEM((points * pitch, lanes), f32),
            pltpu.VMEM((part * count, lanes), f32),
            pltpu.VMEM((slab_count, keep * part, lanes), f32),
        ],
        compiler_params=params(16),
        name="apply_part",
    )(notes, orbitals, received)


def settle(kept, keep, halves, order):
    slab_count, rows = kept.shape[:2]
    parts = slab_count // halves
    part = rows // keep

    def kernel(kept_ref, out_ref, stage):
        for q in range(parts):
            stage[q] = sum(kept_ref[j].astype(f32) for j in range(slab_count) if order[j] % parts == q)
            for k in range(keep):
                out_ref[q * part:(q + 1) * part, k, :] = stage[q, k * part:(k + 1) * part, :]

    return pl.pallas_call(
        kernel,
        out_shape=jax.ShapeDtypeStruct((parts * part, keep, lanes), f32),
        in_specs=[whole],
        out_specs=whole,
        scratch_shapes=[pltpu.VMEM((parts, rows, lanes), f32)],
        compiler_params=params(4),
        name="settle",
    )(kept)


def places(order):
    return [order.index(i) for i in range(len(order))]


def exchange(value, grid_count, offset):
    return lax.ppermute(value, "grid", [(i, i ^ offset) for i in range(grid_count)])


def quick_body(orbitals, targets, points, fit):
    grid_count, part_count, halves = (lax.axis_size(name) for name in ("grid", "part", "half"))
    shard_len, slab_count = orbitals.shape[1], part_count * halves
    count = targets.shape[0]
    keep = count // slab_count
    part = shard_len // lanes // part_count
    plan = Plan(round((shard_len * grid_count) ** (1 / 3)))
    share, notes = read_points(orbitals, targets, points, fit)
    shares = [share] + [exchange(share, grid_count, d) for d in range(1, grid_count)]
    *pieces, at = fit_pairs(orbitals, notes, shares)
    pieces = pieces[:1] + [exchange(pieces[d], grid_count, d) for d in range(1, grid_count)]
    near = list(reversed(range(part_count * grid_count)))
    far = [s ^ (slab_count // 2 + 1) for s in range(slab_count)]
    sent = potentials(plan, pieces, at, part_count, places(near))
    received = lax.all_to_all(sent, ("part", "grid"), 0, 0, axis_index_groups=[near])
    blocks = apply_part(orbitals, notes, received, part, count, places(far), halves)
    kept = lax.all_to_all(blocks, ("half", "part"), 0, 0, axis_index_groups=[far])
    return jnp.transpose(settle(kept, keep, halves, far), (1, 0, 2)).reshape(keep, shard_len)


def quick_fits(mesh, orbitals, targets, points, fit):
    grid_count, slab_count = mesh.shape["grid"], mesh.shape["slab"]
    occupied, cells = orbitals.shape
    group, edge = fit.shape[1], round(cells ** (1 / 3))
    shard_rows = cells // grid_count // lanes
    return (
        group == grid_count
        and 2 * group == 8
        and occupied <= lanes
        and occupied % 16 == 0
        and edge ** 3 == cells
        and edge % 16 == 0
        and edge <= lanes // 2
        and cells % (grid_count * lanes) == 0
        and shard_rows % 8 == 0
        and slab_count % 2 == 0
        and shard_rows % (slab_count // 2) == 0
        and targets.shape[0] % slab_count == 0
        and targets.shape[0] % 8 == 0
    )


def solution(mesh):
    grid_count, slab_count = mesh.shape["grid"], mesh.shape["slab"]
    out_specs = P("slab", "grid")

    def run(*arrays):
        if not quick_fits(mesh, *arrays):
            in_specs = (P(None, "grid"), P(), P("slab"), P("slab", None))
            return jax.shard_map(plain_body, mesh=mesh, in_specs=in_specs, out_specs=out_specs, check_vma=False)(*arrays)
        halved = Mesh(mesh.devices.reshape(2, slab_count // 2, grid_count), ("half", "part", "grid"))
        slab = ("half", "part")
        in_specs = (P(None, "grid"), P(), P(slab), P(slab, None))
        return jax.shard_map(
            quick_body, mesh=halved, in_specs=in_specs, out_specs=P(slab, "grid"), check_vma=False)(*arrays)

    return run
```

```python
import math

import jax
import jax.numpy as jnp
import ml_dtypes
import numpy as np
from jax import lax
from jax.experimental import pallas as pl
from jax.experimental.pallas import tpu as pltpu
from jax.sharding import Mesh
from jax.sharding import PartitionSpec as P

NG = 48


screening = 4.0
careful = lax.Precision.HIGH
lanes = 128
f32 = jnp.float32
bf16 = jnp.bfloat16
contract_last = (((1,), (1,)), ((), ()))


def dft_tables(length):
    positions = jnp.arange(length, dtype=jnp.int32)
    product = positions[:, None] * positions[None, :] % length
    angles = product.astype(jnp.float32) * (2.0 * math.pi / length)
    return (jnp.cos(angles), jnp.sin(angles))


def kernel_table():
    full_index = jnp.arange(NG, dtype=jnp.int32)
    wrapped = jnp.where(full_index > NG // 2, full_index - NG, full_index).astype(jnp.float32)
    half_index = jnp.arange(NG // 2 + 1, dtype=jnp.int32).astype(jnp.float32)
    step_size = 2.0 * math.pi / NG
    full_sq = wrapped * step_size * (wrapped * step_size)
    half_sq = half_index * step_size * (half_index * step_size)
    summed = full_sq[:, None, None] + full_sq[None, :, None] + half_sq[None, None, :]
    return screening / (screening + summed)


def apply_axis(values, matrix, pattern):
    return jnp.einsum(
        pattern, values, matrix, precision=careful, preferred_element_type=jnp.float32
    )


def split_apply(values, matrix, pattern):
    upper = matrix.astype(jnp.bfloat16)
    lower = (matrix - upper.astype(jnp.float32)).astype(jnp.bfloat16)
    first = jnp.einsum(pattern, values, upper, preferred_element_type=jnp.float32)
    return first + jnp.einsum(pattern, values, lower, preferred_element_type=jnp.float32)


def solve_one(vector_row):
    half_len = NG // 2 + 1
    cosine, sin_table = dft_tables(NG)
    cos_half = cosine[:, :half_len]
    sin_half = sin_table[:, :half_len]
    cube_vals = vector_row.reshape(NG, NG, NG)
    real_part = split_apply(cube_vals, cos_half, "xyz,zm->xym")
    imag_part = -split_apply(cube_vals, sin_half, "xyz,zm->xym")
    for pattern in ("xym,yb->xbm", "xym,xb->bym"):
        real_next = apply_axis(real_part, cosine, pattern) + apply_axis(
            imag_part, sin_table, pattern
        )
        imag_part = apply_axis(imag_part, cosine, pattern) - apply_axis(
            real_part, sin_table, pattern
        )
        real_part = real_next
    weights = kernel_table()
    real_part = real_part * weights
    imag_part = imag_part * weights
    for pattern in ("xym,xb->bym", "xym,yb->xbm"):
        real_next = apply_axis(real_part, cosine, pattern) - apply_axis(
            imag_part, sin_table, pattern
        )
        imag_part = apply_axis(real_part, sin_table, pattern) + apply_axis(
            imag_part, cosine, pattern
        )
        real_part = real_next
    frequency = jnp.arange(half_len, dtype=jnp.int32)
    fold_weight = jnp.where((frequency == 0) | (frequency == NG // 2), 1.0, 2.0).astype(jnp.float32)
    result = apply_axis(real_part * fold_weight, cos_half, "xym,zm->xyz") - apply_axis(
        imag_part * fold_weight, sin_half, "xym,zm->xyz"
    )
    return (result * (1.0 / (NG * NG * NG))).reshape(-1).astype(jnp.bfloat16)


def plain_body(orbitals, targets, points, fit):
    occupied, shard_len = orbitals.shape
    target_count = targets.shape[0]
    group_size = points.shape[0]
    slab_count = lax.axis_size("slab")
    offsets = points - lax.axis_index("grid") * shard_len
    cell_ids = lax.broadcasted_iota(jnp.int32, (group_size, shard_len), 1)
    one_hot = (cell_ids == offsets[:, None]).astype(jnp.bfloat16)
    point_terms = lax.dot_general(
        orbitals, one_hot, (((1,), (1,)), ((), ())), preferred_element_type=jnp.float32
    )
    at_points = lax.psum(point_terms, "grid").astype(jnp.bfloat16)
    chosen = jnp.take(orbitals, targets, axis=0)
    target_points = jnp.take(at_points, targets, axis=0)
    contract_first = (((0,), (0,)), ((), ()))
    density = lax.dot_general(
        at_points, orbitals, contract_first, preferred_element_type=jnp.float32
    ) * (1.0 / math.sqrt(occupied))
    target_density = lax.dot_general(
        target_points, chosen, contract_first, preferred_element_type=jnp.float32
    ) * (1.0 / math.sqrt(target_count))
    pairs = density * target_density
    fitted = lax.dot_general(
        fit,
        pairs,
        contract_first,
        precision=lax.Precision.HIGHEST,
        preferred_element_type=jnp.float32,
    ).astype(jnp.bfloat16)
    vectors = lax.all_to_all(fitted, "grid", split_axis=0, concat_axis=1, tiled=True)
    potential = lax.map(solve_one, vectors)
    returned = lax.all_to_all(potential, "grid", split_axis=1, concat_axis=0, tiled=True)
    weighted = (returned.astype(jnp.float32) * density).astype(jnp.bfloat16)
    prefactor = -1.0 / math.sqrt(group_size * slab_count)
    regrouped = lax.all_to_all(weighted, "slab", split_axis=1, concat_axis=0, tiled=True)
    all_targets = lax.all_gather(target_points, "slab", axis=1, tiled=True)
    block_out = jnp.dot(all_targets, regrouped, preferred_element_type=jnp.float32)
    summed = lax.all_to_all(block_out, "slab", split_axis=0, concat_axis=1, tiled=True)
    return summed * prefactor


def hartley(length):
    product = np.outer(np.arange(length), np.arange(length)) % length
    angles = product * (2.0 * math.pi / length)
    return (np.cos(angles) + np.sin(angles)) / math.sqrt(length)


def split_table(table):
    upper = table.astype(ml_dtypes.bfloat16)
    lower = (table - upper.astype(np.float64)).astype(ml_dtypes.bfloat16)
    return upper, lower


def split_value(value):
    upper = value.astype(bf16)
    return upper, (value - upper.astype(jnp.float32)).astype(bf16)


class Plan:
    def __init__(self, edge):
        self.edge = edge
        self.half = edge // 2
        self.slot = lanes // 2
        self.inner = lanes // math.gcd(edge, lanes)
        self.outer = edge // self.inner
        self.block = self.inner * edge
        self.block_rows = self.block // lanes
        self.plane_rows = edge * edge // lanes
        self.rows = edge * self.plane_rows
        matrix = hartley(edge)
        self.windows = []
        tables = []
        for j in range(self.inner // 2):
            low, high = 2 * j * edge, (2 * j + 2) * edge
            base = low // lanes * lanes
            self.windows.append((low, high, base))
            table = np.zeros((2 * lanes, 2, 2, self.slot))
            for h in range(2):
                for y in range(2):
                    for z in range(edge):
                        table[(low + y * edge + z - base + h * lanes) % (2 * lanes), y, h, :edge] = matrix[z]
            tables.append(table.reshape(2 * lanes, 2 * lanes))
        self.forward = np.concatenate(tables)
        self.backward = np.concatenate([table.T for table in tables])
        step = 2.0 * math.pi / edge
        index = np.arange(edge)
        square = (np.where(index > edge // 2, index - edge, index) * step) ** 2
        weights = screening / (screening + square[:, None, None] + square[None, :, None] + square[None, None, :])
        weights = weights.reshape(2, self.half, edge, edge)
        table = np.zeros((self.half, edge, 2, self.slot))
        table[..., :edge] = np.transpose(weights, (1, 2, 0, 3))
        self.weights = table.reshape(self.half, edge, lanes).astype(np.float32)
        self.left = np.concatenate([*split_table(matrix), split_table(matrix)[0]], axis=1)

    def tables(self):
        fh, fl = split_table(self.forward)
        bh, bl = split_table(self.backward)
        return [self.left, fh, fl, bh, bl, self.weights]


def three(value):
    upper, lower = split_value(value)
    return jnp.concatenate([upper, upper, lower], axis=0)


def dot(a, b):
    return jnp.dot(a, b, preferred_element_type=jnp.float32)


def product(value, upper_table, lower_table):
    rows = value.shape[0]
    upper, lower = split_value(value)
    both = dot(jnp.concatenate([upper, lower], axis=0), upper_table)
    return both[:rows] + both[rows:] + dot(upper, lower_table)


def solve(plan, cube, left, fh, fl, bh, bl, weights, mid):
    edge, half, inner, outer, block = plan.edge, plan.half, plan.inner, plan.outer, plan.block
    left_all = left[...]
    values = jnp.concatenate(
        [cube[pl.ds(c, edge, stride=plan.plane_rows), :].astype(bf16) for c in range(plan.plane_rows)], axis=1)
    spectrum = dot(left_all[:, :2 * edge], jnp.concatenate([values, values], axis=0))

    def tile(h, c):
        return jnp.concatenate([
            spectrum[h * half:(h + 1) * half, b * block + c * lanes:b * block + (c + 1) * lanes] for b in range(outer)], axis=0)

    lane = lax.broadcasted_iota(jnp.int32, (outer * half, lanes), 1)
    tiles = [[tile(h, c) for c in range(plan.block_rows)] for h in range(2)]
    for j, (low, high, base) in enumerate(plan.windows):
        c = base // lanes
        if high - base <= lanes:
            window = [tiles[0][c], tiles[1][c]]
        else:
            window = [jnp.where(lane >= low - base, tiles[0][c], tiles[1][c + 1]),
                      jnp.where(lane < high - base - lanes, tiles[0][c + 1], tiles[1][c])]
        rows = slice(2 * lanes * j, 2 * lanes * (j + 1))
        result = product(jnp.concatenate(window, axis=1), fh[rows, :], fl[rows, :])
        for b in range(outer):
            for o in range(2):
                y = b * inner + 2 * j + o
                mid[y * half:(y + 1) * half, :] = result[b * half:(b + 1) * half, o * lanes:(o + 1) * lanes]
    for k in range(0, half, 2):
        value = jnp.concatenate([mid[pl.ds(k + o, edge, stride=half), :] for o in range(2)], axis=1)
        value = dot(left_all, three(value))
        value = value * jnp.concatenate([weights[k], weights[k + 1]], axis=1)
        value = dot(left_all, three(value))
        for o in range(2):
            mid[pl.ds(k + o, edge, stride=half), :] = value[:, o * lanes:(o + 1) * lanes]
    results = []
    for j in range(len(plan.windows)):
        rows = slice(2 * lanes * j, 2 * lanes * (j + 1))
        value = jnp.concatenate([
            jnp.concatenate([mid[(b * inner + 2 * j + o) * half:(b * inner + 2 * j + o + 1) * half, :] for b in range(outer)], axis=0)
            for o in range(2)], axis=1)
        results.append(product(value, bh[rows, :], bl[rows, :]))

    def gathered(h, c):
        value = None
        for (low, high, base), result in zip(plan.windows, results):
            if low < (c + 1) * lanes and high > c * lanes:
                place = (c * lanes - base + h * lanes) % (2 * lanes)
                part = result[:, place:place + lanes]
                value = part if value is None else jnp.where(lane >= low - c * lanes, part, value)
        return value

    tiles = [[gathered(h, c) for c in range(plan.block_rows)] for h in range(2)]
    value = jnp.concatenate([
        jnp.concatenate([tiles[h][c][b * half:(b + 1) * half] for h in range(2)], axis=0)
        for b in range(outer) for c in range(plan.block_rows)], axis=1)
    value = dot(left_all, three(value))
    for c in range(plan.plane_rows):
        cube[pl.ds(c, edge, stride=plan.plane_rows), :] = value[:, c * lanes:(c + 1) * lanes]


def params(mebibytes):
    return pltpu.CompilerParams(vmem_limit_bytes=mebibytes * 1024 * 1024)


whole = pl.BlockSpec(memory_space=pltpu.VMEM)
far = pl.BlockSpec(memory_space=pltpu.HBM)


def iota(shape, axis):
    return lax.broadcasted_iota(jnp.int32, shape, axis)


def read_points(orbitals, targets, points, fit):
    occupied, shard_len = orbitals.shape
    count, group = targets.shape[0], points.shape[0]
    scale = 1.0 / math.sqrt(occupied) / math.sqrt(count)

    def kernel(points_hbm, targets_hbm, fit_hbm, orbitals_ref, out_ref, notes_ref, points_ref, targets_ref, fit_ref, tiles, sems):
        small = [
            pltpu.make_async_copy(source, place, sems.at[group + i])
            for i, (source, place) in enumerate(
                ((points_hbm, points_ref), (targets_hbm, targets_ref), (fit_hbm, fit_ref)))
        ]
        for copy in small:
            copy.start()
        me = lax.axis_index("grid")
        base = me * shard_len
        rows, columns = iota((8, group * lanes), 0), iota((8, group * lanes), 1)
        chosen = jnp.zeros((8, group * lanes), f32)
        copies = []
        small[0].wait()
        for m in range(group):
            local = points_ref[m] - base
            inside = (local >= 0) & (local < shard_len)
            local = jnp.clip(local, 0, shard_len - 1)
            first = pl.multiple_of(local // lanes * lanes, lanes)
            copy = pltpu.make_async_copy(
                orbitals_ref.at[:, pl.ds(first, lanes)], tiles.at[:, pl.ds(m * lanes, lanes)], sems.at[m])
            copy.start()
            copies.append(copy)
            column = jnp.where(inside, local - first + m * lanes, -1)
            chosen = jnp.where((rows == m) & (columns == column), 1.0, chosen)
        chosen = jnp.concatenate([chosen, jnp.zeros_like(chosen)], axis=0).astype(bf16)
        small[1].wait()
        small[2].wait()
        rows, columns = iota((8, lanes), 0), iota((8, lanes), 1)
        counts = jnp.zeros((8, lanes), f32)
        for k in range(count):
            counts = counts + jnp.where(columns == targets_ref[k], 1.0, 0.0)
        notes_ref[:8, :] = counts
        for j in range(group):
            value = jnp.zeros((8, lanes), f32)
            for r in range(8):
                d = r % group
                value = jnp.where(rows == r, fit_ref[(d + j) % group, jnp.bitwise_xor(me, d)], value)
            notes_ref[8 + 8 * j:16 + 8 * j, :] = value * scale
        rows, columns = iota((count, lanes), 0), iota((count, lanes), 1)
        ones = jnp.zeros((count, lanes), f32)
        for k in range(count):
            ones = jnp.where((rows == k) & (columns == targets_ref[k]), 1.0, ones)
        notes_ref[8 + 8 * group:, :] = ones
        for copy in copies:
            copy.wait()
        out = lax.dot_general(chosen, tiles[...], contract_last, preferred_element_type=f32)
        out_ref[...] = jnp.concatenate([out[:8], jnp.zeros((8, lanes - occupied), f32)], axis=1)

    return pl.pallas_call(
        kernel,
        out_shape=[
            pltpu.VMEM((8, lanes), f32),
            pltpu.VMEM((8 + 8 * group + count, lanes), f32),
        ],
        in_specs=[far] * 4,
        out_specs=[whole] * 2,
        scratch_shapes=[
            pltpu.SMEM(points.shape, jnp.int32),
            pltpu.SMEM(targets.shape, jnp.int32),
            pltpu.SMEM(fit.shape, f32),
            pltpu.VMEM((occupied, group * lanes), bf16),
            pltpu.SemaphoreType.DMA((group + 3,)),
        ],
        compiler_params=params(4),
        name="read_points",
    )(*[pltpu.with_memory_space_constraint(value, pltpu.HBM) for value in (points, targets, fit, orbitals)])


def fit_pairs(orbitals, notes, shares):
    occupied, shard_len = orbitals.shape
    group = len(shares)
    shard_rows = shard_len // lanes
    step = shard_rows // 8

    def kernel(notes_ref, orbitals_ref, *refs):
        share_refs, out_refs, at_ref, mid = refs[:group], refs[group:2 * group], refs[2 * group], refs[2 * group + 1]
        at = share_refs[0][...]
        for ref in share_refs[1:]:
            at = at + ref[...]
        at_ref[...] = at
        rows = iota((8, lanes), 0)
        twice = jnp.where(rows < group, at, pltpu.roll(at, group, 0))
        weighted = notes_ref[:8, :] * twice
        upper = weighted.astype(bf16).astype(f32)
        left = jnp.concatenate([twice, upper, weighted - upper, jnp.zeros((8, lanes), f32)], axis=0)
        left = left.astype(bf16)[:, :occupied]
        coefficients = [notes_ref[8 + 8 * j:16 + 8 * j, :] for j in range(group)]
        for c in range(0, shard_rows, step):
            product = jnp.dot(left, orbitals_ref[:, c * lanes:(c + step) * lanes], preferred_element_type=f32)
            for r in range(step):
                part = product[:, r * lanes:(r + 1) * lanes]
                pair = part[:8] * (part[8:16] + part[16:24])
                value = pair * coefficients[0]
                for j in range(1, group):
                    value = value + pltpu.roll(pair, 8 - j, 0) * coefficients[j]
                mid[(c + r) * 8:(c + r + 1) * 8, :] = value
        for d in range(group):
            out_refs[d][...] = mid[pl.ds(d, shard_rows, stride=8), :].astype(bf16)

    piece = jax.ShapeDtypeStruct((shard_rows, lanes), bf16)
    return pl.pallas_call(
        kernel,
        out_shape=[piece] * group + [jax.ShapeDtypeStruct((8, lanes), f32)],
        in_specs=[whole] * (2 + group),
        out_specs=[whole] * (group + 1),
        scratch_shapes=[pltpu.VMEM((shard_rows * 8, lanes), f32)],
        compiler_params=params(16),
        name="fit_pairs",
    )(notes, orbitals, *shares)


def potentials(plan, pieces, offsets, at, parts, place):
    grid_count, piece_rows = len(pieces), pieces[0].shape[0]
    part = piece_rows // parts
    sent = -(-(part + 1) // 8) * 8
    tables = plan.tables()

    def kernel(at_ref, *refs):
        piece_refs, refs = refs[:grid_count], refs[grid_count:]
        table_refs, (out_ref, cube, mid) = refs[:len(tables)], refs[len(tables):]
        me = lax.axis_index("grid")
        for d, ref in zip(offsets, piece_refs):
            start = pl.multiple_of(jnp.bitwise_xor(me, d) * piece_rows, 8)
            cube[pl.ds(start, piece_rows), :] = ref[...].astype(f32)
        solve(plan, cube, *table_refs, mid)
        own = jnp.broadcast_to(at_ref[pl.ds(me, 1), :], (sent, lanes))
        last = iota((sent, lanes), 0) >= part
        for g in range(grid_count):
            for q in range(parts):
                first = g * piece_rows + q * part
                out_ref[place[q * grid_count + g]] = jnp.where(last, own, cube[first:first + sent, :]).astype(bf16)

    return pl.pallas_call(
        kernel,
        out_shape=jax.ShapeDtypeStruct((parts * grid_count, sent, lanes), bf16),
        in_specs=[whole] * (1 + grid_count + len(tables)),
        out_specs=whole,
        scratch_shapes=[
            pltpu.VMEM((plan.rows + 8, lanes), f32),
            pltpu.VMEM((plan.edge * plan.half, lanes), f32),
        ],
        compiler_params=params(24),
        name="potentials",
    )(at, *pieces, *tables)


def apply_part(orbitals, notes, received, part, count, place, halves):
    occupied, shard_len = orbitals.shape
    points, pitch = received.shape[:2]
    slab_count = len(place)
    keep = count // slab_count
    prefactor = -1.0 / math.sqrt(points * halves)

    def kernel(notes_ref, orbitals_ref, received_ref, out_ref, spread, mid, stage):
        for m in range(points):
            spread[m * pitch:(m + 1) * pitch, :] = received_ref[m].astype(f32)
        at = spread[pl.ds(part, points, stride=pitch), :][:, :occupied].astype(bf16)
        first = pl.multiple_of(lax.axis_index("part") * (part * lanes), lanes)
        density = jnp.dot(at, orbitals_ref[:, pl.ds(first, part * lanes)], preferred_element_type=f32)
        chosen = notes_ref[notes_ref.shape[0] - count:, :][:, :occupied].astype(bf16)
        target_points = lax.dot_general(chosen, at, contract_last, preferred_element_type=f32).astype(bf16)
        potential = jnp.concatenate([spread[pl.ds(r, points, stride=pitch), :] for r in range(part)], axis=1)
        weighted = (potential * (density * (1.0 / math.sqrt(occupied)))).astype(bf16)
        applied = jnp.dot(target_points, weighted, preferred_element_type=f32) * prefactor
        for r in range(part):
            mid[r * count:(r + 1) * count, :] = applied[:, r * lanes:(r + 1) * lanes]
        for s in range(slab_count):
            for k in range(keep):
                stage[s, k * part:(k + 1) * part, :] = mid[pl.ds(s * keep + k, part, stride=count), :]
            out_ref[place[s]] = stage[s].astype(bf16)

    return pl.pallas_call(
        kernel,
        out_shape=jax.ShapeDtypeStruct((slab_count, keep * part, lanes), bf16),
        in_specs=[whole] * 3,
        out_specs=whole,
        scratch_shapes=[
            pltpu.VMEM((points * pitch, lanes), f32),
            pltpu.VMEM((part * count, lanes), f32),
            pltpu.VMEM((slab_count, keep * part, lanes), f32),
        ],
        compiler_params=params(16),
        name="apply_part",
    )(notes, orbitals, received)


def settle(kept, keep, halves, order):
    slab_count, rows = kept.shape[:2]
    parts = slab_count // halves
    part = rows // keep

    def kernel(kept_ref, out_ref, stage):
        for q in range(parts):
            stage[q] = sum(kept_ref[j].astype(f32) for j in range(slab_count) if order[j] % parts == q)
            for k in range(keep):
                out_ref[q * part:(q + 1) * part, k, :] = stage[q, k * part:(k + 1) * part, :]

    return pl.pallas_call(
        kernel,
        out_shape=jax.ShapeDtypeStruct((parts * part, keep, lanes), f32),
        in_specs=[whole],
        out_specs=whole,
        scratch_shapes=[pltpu.VMEM((parts, rows, lanes), f32)],
        compiler_params=params(4),
        name="settle",
    )(kept)


def places(order):
    return [order.index(i) for i in range(len(order))]


def exchange(value, grid_count, offset):
    return lax.ppermute(value, "grid", [(i, i ^ offset) for i in range(grid_count)])


def quick_body(orbitals, targets, points, fit):
    grid_count, part_count, halves = (lax.axis_size(name) for name in ("grid", "part", "half"))
    shard_len, slab_count = orbitals.shape[1], part_count * halves
    count = targets.shape[0]
    keep = count // slab_count
    part = shard_len // lanes // part_count
    plan = Plan(round((shard_len * grid_count) ** (1 / 3)))
    share, notes = read_points(orbitals, targets, points, fit)
    shares = [share] + [exchange(share, grid_count, d) for d in range(1, grid_count)]
    *pieces, at = fit_pairs(orbitals, notes, shares)
    offsets = [0] + list(reversed(range(1, grid_count)))
    pieces = [exchange(pieces[d], grid_count, d) if d else pieces[d] for d in offsets]
    near = list(reversed(range(part_count * grid_count)))
    far = [s ^ (s >> 1) for s in reversed(range(slab_count))]
    sent = potentials(plan, pieces, offsets, at, part_count, places(near))
    received = lax.all_to_all(sent, ("part", "grid"), 0, 0, axis_index_groups=[near])
    blocks = apply_part(orbitals, notes, received, part, count, places(far), halves)
    kept = lax.all_to_all(blocks, ("half", "part"), 0, 0, axis_index_groups=[far])
    return jnp.transpose(settle(kept, keep, halves, far), (1, 0, 2)).reshape(keep, shard_len)


def quick_fits(mesh, orbitals, targets, points, fit):
    grid_count, slab_count = mesh.shape["grid"], mesh.shape["slab"]
    occupied, cells = orbitals.shape
    group, edge = fit.shape[1], round(cells ** (1 / 3))
    shard_rows = cells // grid_count // lanes
    return (
        group == grid_count
        and 2 * group == 8
        and occupied <= lanes
        and occupied % 16 == 0
        and edge ** 3 == cells
        and edge % 16 == 0
        and edge <= lanes // 2
        and cells % (grid_count * lanes) == 0
        and shard_rows % 8 == 0
        and slab_count % 2 == 0
        and shard_rows % (slab_count // 2) == 0
        and targets.shape[0] % slab_count == 0
        and targets.shape[0] % 8 == 0
    )


def solution(mesh):
    grid_count, slab_count = mesh.shape["grid"], mesh.shape["slab"]
    out_specs = P("slab", "grid")

    def run(*arrays):
        if not quick_fits(mesh, *arrays):
            in_specs = (P(None, "grid"), P(), P("slab"), P("slab", None))
            return jax.shard_map(plain_body, mesh=mesh, in_specs=in_specs, out_specs=out_specs, check_vma=False)(*arrays)
        halved = Mesh(mesh.devices.reshape(2, slab_count // 2, grid_count), ("half", "part", "grid"))
        slab = ("half", "part")
        in_specs = (P(None, "grid"), P(), P(slab), P(slab, None))
        return jax.shard_map(
            quick_body, mesh=halved, in_specs=in_specs, out_specs=P(slab, "grid"), check_vma=False)(*arrays)

    return run
```

```python
import math

import jax
import jax.numpy as jnp
import ml_dtypes
import numpy as np
from jax import lax
from jax.experimental import pallas as pl
from jax.experimental.pallas import tpu as pltpu
from jax.sharding import Mesh
from jax.sharding import PartitionSpec as P

NG = 48


screening = 4.0
careful = lax.Precision.HIGH
lanes = 128
f32 = jnp.float32
bf16 = jnp.bfloat16
contract_last = (((1,), (1,)), ((), ()))


def dft_tables(length):
    positions = jnp.arange(length, dtype=jnp.int32)
    product = positions[:, None] * positions[None, :] % length
    angles = product.astype(jnp.float32) * (2.0 * math.pi / length)
    return (jnp.cos(angles), jnp.sin(angles))


def kernel_table():
    full_index = jnp.arange(NG, dtype=jnp.int32)
    wrapped = jnp.where(full_index > NG // 2, full_index - NG, full_index).astype(jnp.float32)
    half_index = jnp.arange(NG // 2 + 1, dtype=jnp.int32).astype(jnp.float32)
    step_size = 2.0 * math.pi / NG
    full_sq = wrapped * step_size * (wrapped * step_size)
    half_sq = half_index * step_size * (half_index * step_size)
    summed = full_sq[:, None, None] + full_sq[None, :, None] + half_sq[None, None, :]
    return screening / (screening + summed)


def apply_axis(values, matrix, pattern):
    return jnp.einsum(
        pattern, values, matrix, precision=careful, preferred_element_type=jnp.float32
    )


def split_apply(values, matrix, pattern):
    upper = matrix.astype(jnp.bfloat16)
    lower = (matrix - upper.astype(jnp.float32)).astype(jnp.bfloat16)
    first = jnp.einsum(pattern, values, upper, preferred_element_type=jnp.float32)
    return first + jnp.einsum(pattern, values, lower, preferred_element_type=jnp.float32)


def solve_one(vector_row):
    half_len = NG // 2 + 1
    cosine, sin_table = dft_tables(NG)
    cos_half = cosine[:, :half_len]
    sin_half = sin_table[:, :half_len]
    cube_vals = vector_row.reshape(NG, NG, NG)
    real_part = split_apply(cube_vals, cos_half, "xyz,zm->xym")
    imag_part = -split_apply(cube_vals, sin_half, "xyz,zm->xym")
    for pattern in ("xym,yb->xbm", "xym,xb->bym"):
        real_next = apply_axis(real_part, cosine, pattern) + apply_axis(
            imag_part, sin_table, pattern
        )
        imag_part = apply_axis(imag_part, cosine, pattern) - apply_axis(
            real_part, sin_table, pattern
        )
        real_part = real_next
    weights = kernel_table()
    real_part = real_part * weights
    imag_part = imag_part * weights
    for pattern in ("xym,xb->bym", "xym,yb->xbm"):
        real_next = apply_axis(real_part, cosine, pattern) - apply_axis(
            imag_part, sin_table, pattern
        )
        imag_part = apply_axis(real_part, sin_table, pattern) + apply_axis(
            imag_part, cosine, pattern
        )
        real_part = real_next
    frequency = jnp.arange(half_len, dtype=jnp.int32)
    fold_weight = jnp.where((frequency == 0) | (frequency == NG // 2), 1.0, 2.0).astype(jnp.float32)
    result = apply_axis(real_part * fold_weight, cos_half, "xym,zm->xyz") - apply_axis(
        imag_part * fold_weight, sin_half, "xym,zm->xyz"
    )
    return (result * (1.0 / (NG * NG * NG))).reshape(-1).astype(jnp.bfloat16)


def plain_body(orbitals, targets, points, fit):
    occupied, shard_len = orbitals.shape
    target_count = targets.shape[0]
    group_size = points.shape[0]
    slab_count = lax.axis_size("slab")
    offsets = points - lax.axis_index("grid") * shard_len
    cell_ids = lax.broadcasted_iota(jnp.int32, (group_size, shard_len), 1)
    one_hot = (cell_ids == offsets[:, None]).astype(jnp.bfloat16)
    point_terms = lax.dot_general(
        orbitals, one_hot, (((1,), (1,)), ((), ())), preferred_element_type=jnp.float32
    )
    at_points = lax.psum(point_terms, "grid").astype(jnp.bfloat16)
    chosen = jnp.take(orbitals, targets, axis=0)
    target_points = jnp.take(at_points, targets, axis=0)
    contract_first = (((0,), (0,)), ((), ()))
    density = lax.dot_general(
        at_points, orbitals, contract_first, preferred_element_type=jnp.float32
    ) * (1.0 / math.sqrt(occupied))
    target_density = lax.dot_general(
        target_points, chosen, contract_first, preferred_element_type=jnp.float32
    ) * (1.0 / math.sqrt(target_count))
    pairs = density * target_density
    fitted = lax.dot_general(
        fit,
        pairs,
        contract_first,
        precision=lax.Precision.HIGHEST,
        preferred_element_type=jnp.float32,
    ).astype(jnp.bfloat16)
    vectors = lax.all_to_all(fitted, "grid", split_axis=0, concat_axis=1, tiled=True)
    potential = lax.map(solve_one, vectors)
    returned = lax.all_to_all(potential, "grid", split_axis=1, concat_axis=0, tiled=True)
    weighted = (returned.astype(jnp.float32) * density).astype(jnp.bfloat16)
    prefactor = -1.0 / math.sqrt(group_size * slab_count)
    regrouped = lax.all_to_all(weighted, "slab", split_axis=1, concat_axis=0, tiled=True)
    all_targets = lax.all_gather(target_points, "slab", axis=1, tiled=True)
    block_out = jnp.dot(all_targets, regrouped, preferred_element_type=jnp.float32)
    summed = lax.all_to_all(block_out, "slab", split_axis=0, concat_axis=1, tiled=True)
    return summed * prefactor


def hartley(length):
    angles = np.outer(np.arange(length), np.arange(length)) % length * (2.0 * math.pi / length)
    matrix = np.cos(angles) + np.sin(angles)
    values = np.unique(np.round(np.abs(matrix), 12))
    scales = 2.0 ** (np.arange(1 << 14) / (1 << 14))
    exact = scales[:, None] * values
    errors = ((exact.astype(ml_dtypes.bfloat16).astype(np.float64) - exact) / scales[:, None]) ** 2
    scale = scales[np.argmin(errors.sum(axis=1))]
    return (matrix * scale).astype(ml_dtypes.bfloat16), scale


def split_value(value):
    upper = value.astype(bf16)
    return upper, (value - upper.astype(jnp.float32)).astype(bf16)


class Plan:
    def __init__(self, edge):
        self.edge = edge
        self.half = edge // 2
        self.slot = lanes // 2
        self.inner = lanes // math.gcd(edge, lanes)
        self.outer = edge // self.inner
        self.block = self.inner * edge
        self.block_rows = self.block // lanes
        self.plane_rows = edge * edge // lanes
        self.rows = edge * self.plane_rows
        matrix, scale = hartley(edge)
        self.windows = []
        tables = []
        for j in range(self.inner // 2):
            low, high = 2 * j * edge, (2 * j + 2) * edge
            base = low // lanes * lanes
            self.windows.append((low, high, base))
            table = np.zeros((2 * lanes, 2, 2, self.slot), ml_dtypes.bfloat16)
            for h in range(2):
                for y in range(2):
                    for z in range(edge):
                        table[(low + y * edge + z - base + h * lanes) % (2 * lanes), y, h, :edge] = matrix[z]
            tables.append(table.reshape(2 * lanes, 2 * lanes))
        self.forward = np.concatenate(tables)
        self.backward = np.concatenate([table.T for table in tables])
        step = 2.0 * math.pi / edge
        index = np.arange(edge)
        square = (np.where(index > edge // 2, index - edge, index) * step) ** 2
        weights = screening / (screening + square[:, None, None] + square[None, :, None] + square[None, None, :])
        weights = weights.reshape(2, self.half, edge, edge)
        table = np.zeros((self.half, edge, 2, self.slot))
        table[..., :edge] = np.transpose(weights, (1, 2, 0, 3))
        self.weights = (table.reshape(self.half, edge, lanes) / (edge * scale ** 2) ** 3).astype(np.float32)
        self.left = np.concatenate([matrix, matrix], axis=1)

    def tables(self):
        return [self.left, self.forward, self.backward, self.weights]


def both_parts(value):
    return jnp.concatenate(split_value(value), axis=0)


def dot(a, b):
    return jnp.dot(a, b, preferred_element_type=jnp.float32)


def product(value, table):
    rows = value.shape[0]
    both = dot(both_parts(value), table)
    return both[:rows] + both[rows:]


def solve(plan, cube, left, forward, backward, weights, mid):
    edge, half, inner, outer, block = plan.edge, plan.half, plan.inner, plan.outer, plan.block
    left_all = left[...]
    values = jnp.concatenate(
        [cube[pl.ds(c, edge, stride=plan.plane_rows), :].astype(bf16) for c in range(plan.plane_rows)], axis=1)
    spectrum = dot(left_all[:, :edge], values)

    def tile(h, c):
        return jnp.concatenate([
            spectrum[h * half:(h + 1) * half, b * block + c * lanes:b * block + (c + 1) * lanes] for b in range(outer)], axis=0)

    lane = lax.broadcasted_iota(jnp.int32, (outer * half, lanes), 1)
    tiles = [[tile(h, c) for c in range(plan.block_rows)] for h in range(2)]
    for j, (low, high, base) in enumerate(plan.windows):
        c = base // lanes
        if high - base <= lanes:
            window = [tiles[0][c], tiles[1][c]]
        else:
            window = [jnp.where(lane >= low - base, tiles[0][c], tiles[1][c + 1]),
                      jnp.where(lane < high - base - lanes, tiles[0][c + 1], tiles[1][c])]
        rows = slice(2 * lanes * j, 2 * lanes * (j + 1))
        result = product(jnp.concatenate(window, axis=1), forward[rows, :])
        for b in range(outer):
            for o in range(2):
                y = b * inner + 2 * j + o
                mid[y * half:(y + 1) * half, :] = result[b * half:(b + 1) * half, o * lanes:(o + 1) * lanes]
    for k in range(0, half, 2):
        value = jnp.concatenate([mid[pl.ds(k + o, edge, stride=half), :] for o in range(2)], axis=1)
        value = dot(left_all, both_parts(value))
        value = value * jnp.concatenate([weights[k], weights[k + 1]], axis=1)
        value = dot(left_all, both_parts(value))
        for o in range(2):
            mid[pl.ds(k + o, edge, stride=half), :] = value[:, o * lanes:(o + 1) * lanes]
    results = []
    for j in range(len(plan.windows)):
        rows = slice(2 * lanes * j, 2 * lanes * (j + 1))
        value = jnp.concatenate([
            jnp.concatenate([mid[(b * inner + 2 * j + o) * half:(b * inner + 2 * j + o + 1) * half, :] for b in range(outer)], axis=0)
            for o in range(2)], axis=1)
        results.append(product(value, backward[rows, :]))

    def gathered(h, c):
        value = None
        for (low, high, base), result in zip(plan.windows, results):
            if low < (c + 1) * lanes and high > c * lanes:
                place = (c * lanes - base + h * lanes) % (2 * lanes)
                part = result[:, place:place + lanes]
                value = part if value is None else jnp.where(lane >= low - c * lanes, part, value)
        return value

    tiles = [[gathered(h, c) for c in range(plan.block_rows)] for h in range(2)]
    value = jnp.concatenate([
        jnp.concatenate([tiles[h][c][b * half:(b + 1) * half] for h in range(2)], axis=0)
        for b in range(outer) for c in range(plan.block_rows)], axis=1)
    value = dot(left_all, both_parts(value))
    for c in range(plan.plane_rows):
        cube[pl.ds(c, edge, stride=plan.plane_rows), :] = value[:, c * lanes:(c + 1) * lanes]


def params(mebibytes):
    return pltpu.CompilerParams(vmem_limit_bytes=mebibytes * 1024 * 1024)


whole = pl.BlockSpec(memory_space=pltpu.VMEM)
far = pl.BlockSpec(memory_space=pltpu.HBM)


def iota(shape, axis):
    return lax.broadcasted_iota(jnp.int32, shape, axis)


def read_points(orbitals, targets, points, fit):
    occupied, shard_len = orbitals.shape
    count, group = targets.shape[0], points.shape[0]
    scale = 1.0 / math.sqrt(occupied) / math.sqrt(count)

    def kernel(points_hbm, targets_hbm, fit_hbm, orbitals_ref, out_ref, notes_ref, points_ref, targets_ref, fit_ref, tiles, sems):
        small = [
            pltpu.make_async_copy(source, place, sems.at[group + i])
            for i, (source, place) in enumerate(
                ((points_hbm, points_ref), (targets_hbm, targets_ref), (fit_hbm, fit_ref)))
        ]
        for copy in small:
            copy.start()
        me = lax.axis_index("grid")
        base = me * shard_len
        rows, columns = iota((8, group * lanes), 0), iota((8, group * lanes), 1)
        chosen = jnp.zeros((8, group * lanes), f32)
        copies = []
        small[0].wait()
        for m in range(group):
            local = points_ref[m] - base
            inside = (local >= 0) & (local < shard_len)
            local = jnp.clip(local, 0, shard_len - 1)
            first = pl.multiple_of(local // lanes * lanes, lanes)
            copy = pltpu.make_async_copy(
                orbitals_ref.at[:, pl.ds(first, lanes)], tiles.at[:, pl.ds(m * lanes, lanes)], sems.at[m])
            copy.start()
            copies.append(copy)
            column = jnp.where(inside, local - first + m * lanes, -1)
            chosen = jnp.where((rows == m) & (columns == column), 1.0, chosen)
        chosen = jnp.concatenate([chosen, jnp.zeros_like(chosen)], axis=0).astype(bf16)
        small[1].wait()
        small[2].wait()
        rows, columns = iota((8, lanes), 0), iota((8, lanes), 1)
        counts = jnp.zeros((8, lanes), f32)
        for k in range(count):
            counts = counts + jnp.where(columns == targets_ref[k], 1.0, 0.0)
        notes_ref[:8, :] = counts
        for j in range(group):
            value = jnp.zeros((8, lanes), f32)
            for r in range(8):
                d = r % group
                value = jnp.where(rows == r, fit_ref[(d + j) % group, jnp.bitwise_xor(me, d)], value)
            notes_ref[8 + 8 * j:16 + 8 * j, :] = value * scale
        rows, columns = iota((count, lanes), 0), iota((count, lanes), 1)
        ones = jnp.zeros((count, lanes), f32)
        for k in range(count):
            ones = jnp.where((rows == k) & (columns == targets_ref[k]), 1.0, ones)
        notes_ref[8 + 8 * group:, :] = ones
        for copy in copies:
            copy.wait()
        out = lax.dot_general(chosen, tiles[...], contract_last, preferred_element_type=f32)
        out_ref[...] = jnp.concatenate([out[:8], jnp.zeros((8, lanes - occupied), f32)], axis=1)

    return pl.pallas_call(
        kernel,
        out_shape=[
            pltpu.VMEM((8, lanes), f32),
            pltpu.VMEM((8 + 8 * group + count, lanes), f32),
        ],
        in_specs=[far] * 4,
        out_specs=[whole] * 2,
        scratch_shapes=[
            pltpu.SMEM(points.shape, jnp.int32),
            pltpu.SMEM(targets.shape, jnp.int32),
            pltpu.SMEM(fit.shape, f32),
            pltpu.VMEM((occupied, group * lanes), bf16),
            pltpu.SemaphoreType.DMA((group + 3,)),
        ],
        compiler_params=params(4),
        name="read_points",
    )(*[pltpu.with_memory_space_constraint(value, pltpu.HBM) for value in (points, targets, fit, orbitals)])


def fit_pairs(orbitals, notes, shares):
    occupied, shard_len = orbitals.shape
    group = len(shares)
    shard_rows = shard_len // lanes
    step = shard_rows // 8

    def kernel(notes_ref, orbitals_ref, *refs):
        share_refs, out_refs, at_ref, mid = refs[:group], refs[group:2 * group], refs[2 * group], refs[2 * group + 1]
        at = share_refs[0][...]
        for ref in share_refs[1:]:
            at = at + ref[...]
        at_ref[...] = at
        rows = iota((8, lanes), 0)
        twice = jnp.where(rows < group, at, pltpu.roll(at, group, 0))
        weighted = notes_ref[:8, :] * twice
        upper = weighted.astype(bf16).astype(f32)
        left = jnp.concatenate([twice, upper, weighted - upper, jnp.zeros((8, lanes), f32)], axis=0)
        left = left.astype(bf16)[:, :occupied]
        coefficients = [notes_ref[8 + 8 * j:16 + 8 * j, :] for j in range(group)]
        for c in range(0, shard_rows, step):
            product = jnp.dot(left, orbitals_ref[:, c * lanes:(c + step) * lanes], preferred_element_type=f32)
            for r in range(step):
                part = product[:, r * lanes:(r + 1) * lanes]
                pair = part[:8] * (part[8:16] + part[16:24])
                value = pair * coefficients[0]
                for j in range(1, group):
                    value = value + pltpu.roll(pair, 8 - j, 0) * coefficients[j]
                mid[(c + r) * 8:(c + r + 1) * 8, :] = value
        for d in range(group):
            out_refs[d][...] = mid[pl.ds(d, shard_rows, stride=8), :].astype(bf16)

    piece = jax.ShapeDtypeStruct((shard_rows, lanes), bf16)
    return pl.pallas_call(
        kernel,
        out_shape=[piece] * group + [jax.ShapeDtypeStruct((8, lanes), f32)],
        in_specs=[whole] * (2 + group),
        out_specs=[whole] * (group + 1),
        scratch_shapes=[pltpu.VMEM((shard_rows * 8, lanes), f32)],
        compiler_params=params(16),
        name="fit_pairs",
    )(notes, orbitals, *shares)


def potentials(plan, pieces, offsets, at, parts, place):
    grid_count, piece_rows = len(pieces), pieces[0].shape[0]
    part = piece_rows // parts
    sent = -(-(part + 1) // 8) * 8
    tables = plan.tables()

    def kernel(at_ref, *refs):
        piece_refs, refs = refs[:grid_count], refs[grid_count:]
        table_refs, (out_ref, cube, mid) = refs[:len(tables)], refs[len(tables):]
        me = lax.axis_index("grid")
        for d, ref in zip(offsets, piece_refs):
            start = pl.multiple_of(jnp.bitwise_xor(me, d) * piece_rows, 8)
            cube[pl.ds(start, piece_rows), :] = ref[...].astype(f32)
        solve(plan, cube, *table_refs, mid)
        own = jnp.broadcast_to(at_ref[pl.ds(me, 1), :], (sent, lanes))
        last = iota((sent, lanes), 0) >= part
        for g in range(grid_count):
            for q in range(parts):
                first = g * piece_rows + q * part
                out_ref[place[q * grid_count + g]] = jnp.where(last, own, cube[first:first + sent, :]).astype(bf16)

    return pl.pallas_call(
        kernel,
        out_shape=jax.ShapeDtypeStruct((parts * grid_count, sent, lanes), bf16),
        in_specs=[whole] * (1 + grid_count + len(tables)),
        out_specs=whole,
        scratch_shapes=[
            pltpu.VMEM((plan.rows + 8, lanes), f32),
            pltpu.VMEM((plan.edge * plan.half, lanes), f32),
        ],
        compiler_params=params(24),
        name="potentials",
    )(at, *pieces, *tables)


def apply_part(orbitals, notes, received, part, count, place, halves):
    occupied, shard_len = orbitals.shape
    points, pitch = received.shape[:2]
    slab_count = len(place)
    keep = count // slab_count
    prefactor = -1.0 / math.sqrt(points * halves)

    def kernel(notes_ref, orbitals_ref, received_ref, out_ref, spread, mid, stage):
        for m in range(points):
            spread[m * pitch:(m + 1) * pitch, :] = received_ref[m].astype(f32)
        at = spread[pl.ds(part, points, stride=pitch), :][:, :occupied].astype(bf16)
        first = pl.multiple_of(lax.axis_index("part") * (part * lanes), lanes)
        density = jnp.dot(at, orbitals_ref[:, pl.ds(first, part * lanes)], preferred_element_type=f32)
        chosen = notes_ref[notes_ref.shape[0] - count:, :][:, :occupied].astype(bf16)
        target_points = lax.dot_general(chosen, at, contract_last, preferred_element_type=f32).astype(bf16)
        potential = jnp.concatenate([spread[pl.ds(r, points, stride=pitch), :] for r in range(part)], axis=1)
        weighted = (potential * (density * (1.0 / math.sqrt(occupied)))).astype(bf16)
        applied = jnp.dot(target_points, weighted, preferred_element_type=f32) * prefactor
        for r in range(part):
            mid[r * count:(r + 1) * count, :] = applied[:, r * lanes:(r + 1) * lanes]
        for s in range(slab_count):
            for k in range(keep):
                stage[s, k * part:(k + 1) * part, :] = mid[pl.ds(s * keep + k, part, stride=count), :]
            out_ref[place[s]] = stage[s].astype(bf16)

    return pl.pallas_call(
        kernel,
        out_shape=jax.ShapeDtypeStruct((slab_count, keep * part, lanes), bf16),
        in_specs=[whole] * 3,
        out_specs=whole,
        scratch_shapes=[
            pltpu.VMEM((points * pitch, lanes), f32),
            pltpu.VMEM((part * count, lanes), f32),
            pltpu.VMEM((slab_count, keep * part, lanes), f32),
        ],
        compiler_params=params(16),
        name="apply_part",
    )(notes, orbitals, received)


def settle(kept, keep, halves, order):
    slab_count, rows = kept.shape[:2]
    parts = slab_count // halves
    part = rows // keep

    def kernel(kept_ref, out_ref, stage):
        for q in range(parts):
            stage[q] = sum(kept_ref[j].astype(f32) for j in range(slab_count) if order[j] % parts == q)
            for k in range(keep):
                out_ref[q * part:(q + 1) * part, k, :] = stage[q, k * part:(k + 1) * part, :]

    return pl.pallas_call(
        kernel,
        out_shape=jax.ShapeDtypeStruct((parts * part, keep, lanes), f32),
        in_specs=[whole],
        out_specs=whole,
        scratch_shapes=[pltpu.VMEM((parts, rows, lanes), f32)],
        compiler_params=params(4),
        name="settle",
    )(kept)


def places(order):
    return [order.index(i) for i in range(len(order))]


def exchange(value, grid_count, offset):
    return lax.ppermute(value, "grid", [(i, i ^ offset) for i in range(grid_count)])


def quick_body(orbitals, targets, points, fit):
    grid_count, part_count, halves = (lax.axis_size(name) for name in ("grid", "part", "half"))
    shard_len, slab_count = orbitals.shape[1], part_count * halves
    count = targets.shape[0]
    keep = count // slab_count
    part = shard_len // lanes // part_count
    plan = Plan(round((shard_len * grid_count) ** (1 / 3)))
    share, notes = read_points(orbitals, targets, points, fit)
    shares = [share] + [exchange(share, grid_count, d) for d in range(1, grid_count)]
    *pieces, at = fit_pairs(orbitals, notes, shares)
    offsets = [0] + list(reversed(range(1, grid_count)))
    pieces = [exchange(pieces[d], grid_count, d) if d else pieces[d] for d in offsets]
    near = list(reversed(range(part_count * grid_count)))
    far = [s ^ (s >> 1) for s in reversed(range(slab_count))]
    sent = potentials(plan, pieces, offsets, at, part_count, places(near))
    received = lax.all_to_all(sent, ("part", "grid"), 0, 0, axis_index_groups=[near])
    blocks = apply_part(orbitals, notes, received, part, count, places(far), halves)
    kept = lax.all_to_all(blocks, ("half", "part"), 0, 0, axis_index_groups=[far])
    return jnp.transpose(settle(kept, keep, halves, far), (1, 0, 2)).reshape(keep, shard_len)


def quick_fits(mesh, orbitals, targets, points, fit):
    grid_count, slab_count = mesh.shape["grid"], mesh.shape["slab"]
    occupied, cells = orbitals.shape
    group, edge = fit.shape[1], round(cells ** (1 / 3))
    shard_rows = cells // grid_count // lanes
    return (
        group == grid_count
        and 2 * group == 8
        and occupied <= lanes
        and occupied % 16 == 0
        and edge ** 3 == cells
        and edge % 16 == 0
        and edge <= lanes // 2
        and cells % (grid_count * lanes) == 0
        and shard_rows % 8 == 0
        and slab_count % 2 == 0
        and shard_rows % (slab_count // 2) == 0
        and targets.shape[0] % slab_count == 0
        and targets.shape[0] % 8 == 0
    )


def solution(mesh):
    grid_count, slab_count = mesh.shape["grid"], mesh.shape["slab"]
    out_specs = P("slab", "grid")

    def run(*arrays):
        if not quick_fits(mesh, *arrays):
            in_specs = (P(None, "grid"), P(), P("slab"), P("slab", None))
            return jax.shard_map(plain_body, mesh=mesh, in_specs=in_specs, out_specs=out_specs, check_vma=False)(*arrays)
        halved = Mesh(mesh.devices.reshape(2, slab_count // 2, grid_count), ("half", "part", "grid"))
        slab = ("half", "part")
        in_specs = (P(None, "grid"), P(), P(slab), P(slab, None))
        return jax.shard_map(
            quick_body, mesh=halved, in_specs=in_specs, out_specs=P(slab, "grid"), check_vma=False)(*arrays)

    return run
```

```python
import math

import jax
import jax.numpy as jnp
import ml_dtypes
import numpy as np
from jax import lax
from jax.experimental import pallas as pl
from jax.experimental.pallas import tpu as pltpu
from jax.sharding import Mesh
from jax.sharding import PartitionSpec as P

NG = 48


screening = 4.0
careful = lax.Precision.HIGH
lanes = 128
f32 = jnp.float32
bf16 = jnp.bfloat16
contract_last = (((1,), (1,)), ((), ()))


def dft_tables(length):
    positions = jnp.arange(length, dtype=jnp.int32)
    product = positions[:, None] * positions[None, :] % length
    angles = product.astype(jnp.float32) * (2.0 * math.pi / length)
    return (jnp.cos(angles), jnp.sin(angles))


def kernel_table():
    full_index = jnp.arange(NG, dtype=jnp.int32)
    wrapped = jnp.where(full_index > NG // 2, full_index - NG, full_index).astype(jnp.float32)
    half_index = jnp.arange(NG // 2 + 1, dtype=jnp.int32).astype(jnp.float32)
    step_size = 2.0 * math.pi / NG
    full_sq = wrapped * step_size * (wrapped * step_size)
    half_sq = half_index * step_size * (half_index * step_size)
    summed = full_sq[:, None, None] + full_sq[None, :, None] + half_sq[None, None, :]
    return screening / (screening + summed)


def apply_axis(values, matrix, pattern):
    return jnp.einsum(
        pattern, values, matrix, precision=careful, preferred_element_type=jnp.float32
    )


def split_apply(values, matrix, pattern):
    upper = matrix.astype(jnp.bfloat16)
    lower = (matrix - upper.astype(jnp.float32)).astype(jnp.bfloat16)
    first = jnp.einsum(pattern, values, upper, preferred_element_type=jnp.float32)
    return first + jnp.einsum(pattern, values, lower, preferred_element_type=jnp.float32)


def solve_one(vector_row):
    half_len = NG // 2 + 1
    cosine, sin_table = dft_tables(NG)
    cos_half = cosine[:, :half_len]
    sin_half = sin_table[:, :half_len]
    cube_vals = vector_row.reshape(NG, NG, NG)
    real_part = split_apply(cube_vals, cos_half, "xyz,zm->xym")
    imag_part = -split_apply(cube_vals, sin_half, "xyz,zm->xym")
    for pattern in ("xym,yb->xbm", "xym,xb->bym"):
        real_next = apply_axis(real_part, cosine, pattern) + apply_axis(
            imag_part, sin_table, pattern
        )
        imag_part = apply_axis(imag_part, cosine, pattern) - apply_axis(
            real_part, sin_table, pattern
        )
        real_part = real_next
    weights = kernel_table()
    real_part = real_part * weights
    imag_part = imag_part * weights
    for pattern in ("xym,xb->bym", "xym,yb->xbm"):
        real_next = apply_axis(real_part, cosine, pattern) - apply_axis(
            imag_part, sin_table, pattern
        )
        imag_part = apply_axis(real_part, sin_table, pattern) + apply_axis(
            imag_part, cosine, pattern
        )
        real_part = real_next
    frequency = jnp.arange(half_len, dtype=jnp.int32)
    fold_weight = jnp.where((frequency == 0) | (frequency == NG // 2), 1.0, 2.0).astype(jnp.float32)
    result = apply_axis(real_part * fold_weight, cos_half, "xym,zm->xyz") - apply_axis(
        imag_part * fold_weight, sin_half, "xym,zm->xyz"
    )
    return (result * (1.0 / (NG * NG * NG))).reshape(-1).astype(jnp.bfloat16)


def plain_body(orbitals, targets, points, fit):
    occupied, shard_len = orbitals.shape
    target_count = targets.shape[0]
    group_size = points.shape[0]
    slab_count = lax.axis_size("slab")
    offsets = points - lax.axis_index("grid") * shard_len
    cell_ids = lax.broadcasted_iota(jnp.int32, (group_size, shard_len), 1)
    one_hot = (cell_ids == offsets[:, None]).astype(jnp.bfloat16)
    point_terms = lax.dot_general(
        orbitals, one_hot, (((1,), (1,)), ((), ())), preferred_element_type=jnp.float32
    )
    at_points = lax.psum(point_terms, "grid").astype(jnp.bfloat16)
    chosen = jnp.take(orbitals, targets, axis=0)
    target_points = jnp.take(at_points, targets, axis=0)
    contract_first = (((0,), (0,)), ((), ()))
    density = lax.dot_general(
        at_points, orbitals, contract_first, preferred_element_type=jnp.float32
    ) * (1.0 / math.sqrt(occupied))
    target_density = lax.dot_general(
        target_points, chosen, contract_first, preferred_element_type=jnp.float32
    ) * (1.0 / math.sqrt(target_count))
    pairs = density * target_density
    fitted = lax.dot_general(
        fit,
        pairs,
        contract_first,
        precision=lax.Precision.HIGHEST,
        preferred_element_type=jnp.float32,
    ).astype(jnp.bfloat16)
    vectors = lax.all_to_all(fitted, "grid", split_axis=0, concat_axis=1, tiled=True)
    potential = lax.map(solve_one, vectors)
    returned = lax.all_to_all(potential, "grid", split_axis=1, concat_axis=0, tiled=True)
    weighted = (returned.astype(jnp.float32) * density).astype(jnp.bfloat16)
    prefactor = -1.0 / math.sqrt(group_size * slab_count)
    regrouped = lax.all_to_all(weighted, "slab", split_axis=1, concat_axis=0, tiled=True)
    all_targets = lax.all_gather(target_points, "slab", axis=1, tiled=True)
    block_out = jnp.dot(all_targets, regrouped, preferred_element_type=jnp.float32)
    summed = lax.all_to_all(block_out, "slab", split_axis=0, concat_axis=1, tiled=True)
    return summed * prefactor


def hartley(length):
    angles = np.outer(np.arange(length), np.arange(length)) % length * (2.0 * math.pi / length)
    matrix = np.cos(angles) + np.sin(angles)
    values = np.unique(np.round(np.abs(matrix), 12))
    scales = 2.0 ** (np.arange(1 << 14) / (1 << 14))
    exact = scales[:, None] * values
    errors = ((exact.astype(ml_dtypes.bfloat16).astype(np.float64) - exact) / scales[:, None]) ** 2
    scale = scales[np.argmin(errors.sum(axis=1))]
    return (matrix * scale).astype(ml_dtypes.bfloat16), scale


def split_value(value):
    upper = value.astype(bf16)
    return upper, (value - upper.astype(jnp.float32)).astype(bf16)


class Plan:
    def __init__(self, edge):
        self.edge = edge
        self.half = edge // 2
        self.slot = lanes // 2
        self.inner = lanes // math.gcd(edge, lanes)
        self.outer = edge // self.inner
        self.block = self.inner * edge
        self.block_rows = self.block // lanes
        self.plane_rows = edge * edge // lanes
        self.rows = edge * self.plane_rows
        matrix, scale = hartley(edge)
        self.windows = []
        tables = []
        for j in range(self.inner // 2):
            low, high = 2 * j * edge, (2 * j + 2) * edge
            base = low // lanes * lanes
            self.windows.append((low, high, base))
            table = np.zeros((2 * lanes, 2, 2, self.slot), ml_dtypes.bfloat16)
            for h in range(2):
                for y in range(2):
                    for z in range(edge):
                        table[(low + y * edge + z - base + h * lanes) % (2 * lanes), y, h, :edge] = matrix[z]
            tables.append(table.reshape(2 * lanes, 2 * lanes))
        self.forward = np.concatenate(tables)
        self.backward = np.concatenate([table.T for table in tables])
        step = 2.0 * math.pi / edge
        index = np.arange(edge)
        square = (np.where(index > edge // 2, index - edge, index) * step) ** 2
        weights = screening / (screening + square[:, None, None] + square[None, :, None] + square[None, None, :])
        weights = weights.reshape(2, self.half, edge, edge)
        table = np.zeros((self.half, edge, 2, self.slot))
        table[..., :edge] = np.transpose(weights, (1, 2, 0, 3))
        self.weights = (table.reshape(self.half, edge, lanes) / (edge * scale ** 2) ** 3).astype(np.float32)
        self.left = np.concatenate([matrix, matrix], axis=1)

    def tables(self):
        return [self.left, self.forward, self.backward, self.weights]


def both_parts(value):
    return jnp.concatenate(split_value(value), axis=0)


def dot(a, b):
    return jnp.dot(a, b, preferred_element_type=jnp.float32)


def product(value, table):
    rows = value.shape[0]
    both = dot(both_parts(value), table)
    return both[:rows] + both[rows:]


def solve(plan, cube, left, forward, backward, weights, mid):
    edge, half, inner, outer, block = plan.edge, plan.half, plan.inner, plan.outer, plan.block
    left_all = left[...]
    values = jnp.concatenate(
        [cube[pl.ds(c, edge, stride=plan.plane_rows), :].astype(bf16) for c in range(plan.plane_rows)], axis=1)
    spectrum = dot(left_all[:, :edge], values)

    def tile(h, c):
        return jnp.concatenate([
            spectrum[h * half:(h + 1) * half, b * block + c * lanes:b * block + (c + 1) * lanes] for b in range(outer)], axis=0)

    lane = lax.broadcasted_iota(jnp.int32, (outer * half, lanes), 1)
    tiles = [[tile(h, c) for c in range(plan.block_rows)] for h in range(2)]
    for j, (low, high, base) in enumerate(plan.windows):
        c = base // lanes
        if high - base <= lanes:
            window = [tiles[0][c], tiles[1][c]]
        else:
            window = [jnp.where(lane >= low - base, tiles[0][c], tiles[1][c + 1]),
                      jnp.where(lane < high - base - lanes, tiles[0][c + 1], tiles[1][c])]
        rows = slice(2 * lanes * j, 2 * lanes * (j + 1))
        result = product(jnp.concatenate(window, axis=1), forward[rows, :])
        for b in range(outer):
            for o in range(2):
                y = b * inner + 2 * j + o
                mid[y * half:(y + 1) * half, :] = result[b * half:(b + 1) * half, o * lanes:(o + 1) * lanes]
    for k in range(0, half, 2):
        value = jnp.concatenate([mid[pl.ds(k + o, edge, stride=half), :] for o in range(2)], axis=1)
        value = dot(left_all, both_parts(value))
        value = value * jnp.concatenate([weights[k], weights[k + 1]], axis=1)
        value = dot(left_all, both_parts(value))
        for o in range(2):
            mid[pl.ds(k + o, edge, stride=half), :] = value[:, o * lanes:(o + 1) * lanes]
    results = []
    for j in range(len(plan.windows)):
        rows = slice(2 * lanes * j, 2 * lanes * (j + 1))
        value = jnp.concatenate([
            jnp.concatenate([mid[(b * inner + 2 * j + o) * half:(b * inner + 2 * j + o + 1) * half, :] for b in range(outer)], axis=0)
            for o in range(2)], axis=1)
        results.append(product(value, backward[rows, :]))

    def gathered(h, c):
        value = None
        for (low, high, base), result in zip(plan.windows, results):
            if low < (c + 1) * lanes and high > c * lanes:
                place = (c * lanes - base + h * lanes) % (2 * lanes)
                part = result[:, place:place + lanes]
                value = part if value is None else jnp.where(lane >= low - c * lanes, part, value)
        return value

    tiles = [[gathered(h, c) for c in range(plan.block_rows)] for h in range(2)]
    value = jnp.concatenate([
        jnp.concatenate([tiles[h][c][b * half:(b + 1) * half] for h in range(2)], axis=0)
        for b in range(outer) for c in range(plan.block_rows)], axis=1)
    value = dot(left_all, both_parts(value))
    for c in range(plan.plane_rows):
        cube[pl.ds(c, edge, stride=plan.plane_rows), :] = value[:, c * lanes:(c + 1) * lanes]


def params(mebibytes):
    return pltpu.CompilerParams(vmem_limit_bytes=mebibytes * 1024 * 1024)


whole = pl.BlockSpec(memory_space=pltpu.VMEM)
far = pl.BlockSpec(memory_space=pltpu.HBM)


def iota(shape, axis):
    return lax.broadcasted_iota(jnp.int32, shape, axis)


def read_points(orbitals, targets, points, fit):
    occupied, shard_len = orbitals.shape
    count, group = targets.shape[0], points.shape[0]
    scale = 1.0 / math.sqrt(occupied) / math.sqrt(count)

    def kernel(points_hbm, targets_hbm, fit_hbm, orbitals_ref, out_ref, notes_ref, points_ref, targets_ref, fit_ref, tiles, sems):
        small = [
            pltpu.make_async_copy(source, place, sems.at[group + i])
            for i, (source, place) in enumerate(
                ((points_hbm, points_ref), (targets_hbm, targets_ref), (fit_hbm, fit_ref)))
        ]
        for copy in small:
            copy.start()
        me = lax.axis_index("grid")
        base = me * shard_len
        rows, columns = iota((8, group * lanes), 0), iota((8, group * lanes), 1)
        chosen = jnp.zeros((8, group * lanes), f32)
        copies = []
        small[0].wait()
        for m in range(group):
            local = points_ref[m] - base
            inside = (local >= 0) & (local < shard_len)
            local = jnp.clip(local, 0, shard_len - 1)
            first = pl.multiple_of(local // lanes * lanes, lanes)
            copy = pltpu.make_async_copy(
                orbitals_ref.at[:, pl.ds(first, lanes)], tiles.at[:, pl.ds(m * lanes, lanes)], sems.at[m])
            copy.start()
            copies.append(copy)
            column = jnp.where(inside, local - first + m * lanes, -1)
            chosen = jnp.where((rows == m) & (columns == column), 1.0, chosen)
        chosen = jnp.concatenate([chosen, jnp.zeros_like(chosen)], axis=0).astype(bf16)
        small[1].wait()
        small[2].wait()
        rows, columns = iota((8, lanes), 0), iota((8, lanes), 1)
        counts = jnp.zeros((8, lanes), f32)
        for k in range(count):
            counts = counts + jnp.where(columns == targets_ref[k], 1.0, 0.0)
        notes_ref[:8, :] = counts
        for j in range(group):
            value = jnp.zeros((8, lanes), f32)
            for r in range(8):
                d = r % group
                value = jnp.where(rows == r, fit_ref[(d + j) % group, jnp.bitwise_xor(me, d)], value)
            notes_ref[8 + 8 * j:16 + 8 * j, :] = value * scale
        rows, columns = iota((count, lanes), 0), iota((count, lanes), 1)
        ones = jnp.zeros((count, lanes), f32)
        for k in range(count):
            ones = jnp.where((rows == k) & (columns == targets_ref[k]), 1.0, ones)
        notes_ref[8 + 8 * group:, :] = ones
        for copy in copies:
            copy.wait()
        out = lax.dot_general(chosen, tiles[...], contract_last, preferred_element_type=f32)
        out_ref[...] = jnp.concatenate([out[:8], jnp.zeros((8, lanes - occupied), f32)], axis=1)

    return pl.pallas_call(
        kernel,
        out_shape=[
            pltpu.VMEM((8, lanes), f32),
            pltpu.VMEM((8 + 8 * group + count, lanes), f32),
        ],
        in_specs=[far] * 4,
        out_specs=[whole] * 2,
        scratch_shapes=[
            pltpu.SMEM(points.shape, jnp.int32),
            pltpu.SMEM(targets.shape, jnp.int32),
            pltpu.SMEM(fit.shape, f32),
            pltpu.VMEM((occupied, group * lanes), bf16),
            pltpu.SemaphoreType.DMA((group + 3,)),
        ],
        compiler_params=params(4),
        name="read_points",
    )(*[pltpu.with_memory_space_constraint(value, pltpu.HBM) for value in (points, targets, fit, orbitals)])


def fit_pairs(orbitals, notes, shares):
    occupied, shard_len = orbitals.shape
    group = len(shares)
    shard_rows = shard_len // lanes
    step = shard_rows // 8

    def kernel(notes_ref, orbitals_ref, *refs):
        share_refs, out_refs, at_ref, mid = refs[:group], refs[group:2 * group], refs[2 * group], refs[2 * group + 1]
        at = share_refs[0][...]
        for ref in share_refs[1:]:
            at = at + ref[...]
        at_ref[...] = at
        rows = iota((8, lanes), 0)
        twice = jnp.where(rows < group, at, pltpu.roll(at, group, 0))
        weighted = notes_ref[:8, :] * twice
        upper = weighted.astype(bf16).astype(f32)
        left = jnp.concatenate([twice, upper, weighted - upper, jnp.zeros((8, lanes), f32)], axis=0)
        left = left.astype(bf16)[:, :occupied]
        coefficients = [notes_ref[8 + 8 * j:16 + 8 * j, :] for j in range(group)]
        for c in range(0, shard_rows, step):
            product = jnp.dot(left, orbitals_ref[:, c * lanes:(c + step) * lanes], preferred_element_type=f32)
            for r in range(step):
                part = product[:, r * lanes:(r + 1) * lanes]
                pair = part[:8] * (part[8:16] + part[16:24])
                value = pair * coefficients[0]
                for j in range(1, group):
                    value = value + pltpu.roll(pair, 8 - j, 0) * coefficients[j]
                mid[(c + r) * 8:(c + r + 1) * 8, :] = value
        for d in range(group):
            out_refs[d][...] = mid[pl.ds(d, shard_rows, stride=8), :].astype(bf16)

    piece = jax.ShapeDtypeStruct((shard_rows, lanes), bf16)
    return pl.pallas_call(
        kernel,
        out_shape=[piece] * group + [jax.ShapeDtypeStruct((8, lanes), f32)],
        in_specs=[whole] * (2 + group),
        out_specs=[whole] * (group + 1),
        scratch_shapes=[pltpu.VMEM((shard_rows * 8, lanes), f32)],
        compiler_params=params(16),
        name="fit_pairs",
    )(notes, orbitals, *shares)


def potentials(plan, pieces, offsets, at, parts, place):
    grid_count, piece_rows = len(pieces), pieces[0].shape[0]
    part = piece_rows // parts
    sent = -(-(part + 1) // 8) * 8
    tables = plan.tables()

    def kernel(at_ref, *refs):
        piece_refs, refs = refs[:grid_count], refs[grid_count:]
        table_refs, (out_ref, cube, mid) = refs[:len(tables)], refs[len(tables):]
        me = lax.axis_index("grid")
        for d, ref in zip(offsets, piece_refs):
            start = pl.multiple_of(jnp.bitwise_xor(me, d) * piece_rows, 8)
            cube[pl.ds(start, piece_rows), :] = ref[...].astype(f32)
        solve(plan, cube, *table_refs, mid)
        own = jnp.broadcast_to(at_ref[pl.ds(me, 1), :], (sent, lanes))
        last = iota((sent, lanes), 0) >= part
        for g in range(grid_count):
            for q in range(parts):
                first = g * piece_rows + q * part
                out_ref[place[q * grid_count + g]] = jnp.where(last, own, cube[first:first + sent, :]).astype(bf16)

    return pl.pallas_call(
        kernel,
        out_shape=jax.ShapeDtypeStruct((parts * grid_count, sent, lanes), bf16),
        in_specs=[whole] * (1 + grid_count + len(tables)),
        out_specs=whole,
        scratch_shapes=[
            pltpu.VMEM((plan.rows + 8, lanes), f32),
            pltpu.VMEM((plan.edge * plan.half, lanes), f32),
        ],
        compiler_params=params(24),
        name="potentials",
    )(at, *pieces, *tables)


def apply_part(orbitals, notes, received, part, count, place, halves):
    occupied, shard_len = orbitals.shape
    points, pitch = received.shape[:2]
    slab_count = len(place)
    keep = count // slab_count
    prefactor = -1.0 / math.sqrt(points * halves)

    def kernel(notes_ref, orbitals_ref, received_ref, out_ref, spread, mid, stage):
        for m in range(points):
            spread[m * pitch:(m + 1) * pitch, :] = received_ref[m].astype(f32)
        at = spread[pl.ds(part, points, stride=pitch), :][:, :occupied].astype(bf16)
        first = pl.multiple_of(lax.axis_index("part") * (part * lanes), lanes)
        density = jnp.dot(at, orbitals_ref[:, pl.ds(first, part * lanes)], preferred_element_type=f32)
        chosen = notes_ref[notes_ref.shape[0] - count:, :][:, :occupied].astype(bf16)
        target_points = lax.dot_general(chosen, at, contract_last, preferred_element_type=f32).astype(bf16)
        potential = jnp.concatenate([spread[pl.ds(r, points, stride=pitch), :] for r in range(part)], axis=1)
        weighted = (potential * (density * (1.0 / math.sqrt(occupied)))).astype(bf16)
        applied = jnp.dot(target_points, weighted, preferred_element_type=f32) * prefactor
        for r in range(part):
            mid[r * count:(r + 1) * count, :] = applied[:, r * lanes:(r + 1) * lanes]
        for s in range(slab_count):
            for k in range(keep):
                stage[s, k * part:(k + 1) * part, :] = mid[pl.ds(s * keep + k, part, stride=count), :]
            out_ref[place[s]] = stage[s].astype(bf16)

    return pl.pallas_call(
        kernel,
        out_shape=jax.ShapeDtypeStruct((slab_count, keep * part, lanes), bf16),
        in_specs=[whole] * 3,
        out_specs=whole,
        scratch_shapes=[
            pltpu.VMEM((points * pitch, lanes), f32),
            pltpu.VMEM((part * count, lanes), f32),
            pltpu.VMEM((slab_count, keep * part, lanes), f32),
        ],
        compiler_params=params(16),
        name="apply_part",
    )(notes, orbitals, received)


def settle(kept, keep, halves, order):
    slab_count, rows = kept.shape[:2]
    parts = slab_count // halves
    part = rows // keep

    def kernel(kept_ref, out_ref, stage):
        for q in range(parts):
            stage[q] = sum(kept_ref[j].astype(f32) for j in range(slab_count) if order[j] % parts == q)
            for k in range(keep):
                out_ref[q * part:(q + 1) * part, k, :] = stage[q, k * part:(k + 1) * part, :]

    return pl.pallas_call(
        kernel,
        out_shape=jax.ShapeDtypeStruct((parts * part, keep, lanes), f32),
        in_specs=[whole],
        out_specs=whole,
        scratch_shapes=[pltpu.VMEM((parts, rows, lanes), f32)],
        compiler_params=params(4),
        name="settle",
    )(kept)


def bits_reversed(count):
    order = [0]
    while len(order) < count:
        order = [2 * i for i in order] + [2 * i + 1 for i in order]
    return order


def places(order):
    return [order.index(i) for i in range(len(order))]


def exchange(value, grid_count, offset):
    return lax.ppermute(value, "grid", [(i, i ^ offset) for i in range(grid_count)])


def quick_body(orbitals, targets, points, fit):
    grid_count, part_count, halves = (lax.axis_size(name) for name in ("grid", "part", "half"))
    shard_len, slab_count = orbitals.shape[1], part_count * halves
    count = targets.shape[0]
    keep = count // slab_count
    part = shard_len // lanes // part_count
    plan = Plan(round((shard_len * grid_count) ** (1 / 3)))
    share, notes = read_points(orbitals, targets, points, fit)
    shares = [share] + [exchange(share, grid_count, d) for d in range(1, grid_count)]
    *pieces, at = fit_pairs(orbitals, notes, shares)
    offsets = [0] + list(reversed(range(1, grid_count)))
    pieces = [exchange(pieces[d], grid_count, d) if d else pieces[d] for d in offsets]
    near = bits_reversed(part_count * grid_count)[::-1]
    far = [s ^ (s >> 1) ^ 1 for s in reversed(range(slab_count))]
    sent = potentials(plan, pieces, offsets, at, part_count, places(near))
    received = lax.all_to_all(sent, ("part", "grid"), 0, 0, axis_index_groups=[near])
    blocks = apply_part(orbitals, notes, received, part, count, places(far), halves)
    kept = lax.all_to_all(blocks, ("half", "part"), 0, 0, axis_index_groups=[far])
    return jnp.transpose(settle(kept, keep, halves, far), (1, 0, 2)).reshape(keep, shard_len)


def quick_fits(mesh, orbitals, targets, points, fit):
    grid_count, slab_count = mesh.shape["grid"], mesh.shape["slab"]
    occupied, cells = orbitals.shape
    group, edge = fit.shape[1], round(cells ** (1 / 3))
    shard_rows = cells // grid_count // lanes
    return (
        group == grid_count
        and 2 * group == 8
        and occupied <= lanes
        and occupied % 16 == 0
        and edge ** 3 == cells
        and edge % 16 == 0
        and edge <= lanes // 2
        and cells % (grid_count * lanes) == 0
        and shard_rows % 8 == 0
        and slab_count > 1
        and (slab_count * grid_count).bit_count() == 1
        and shard_rows % (slab_count // 2) == 0
        and targets.shape[0] % slab_count == 0
        and targets.shape[0] % 8 == 0
    )


def solution(mesh):
    grid_count, slab_count = mesh.shape["grid"], mesh.shape["slab"]
    out_specs = P("slab", "grid")

    def run(*arrays):
        if not quick_fits(mesh, *arrays):
            in_specs = (P(None, "grid"), P(), P("slab"), P("slab", None))
            return jax.shard_map(plain_body, mesh=mesh, in_specs=in_specs, out_specs=out_specs, check_vma=False)(*arrays)
        halved = Mesh(mesh.devices.reshape(2, slab_count // 2, grid_count), ("half", "part", "grid"))
        slab = ("half", "part")
        in_specs = (P(None, "grid"), P(), P(slab), P(slab, None))
        return jax.shard_map(
            quick_body, mesh=halved, in_specs=in_specs, out_specs=P(slab, "grid"), check_vma=False)(*arrays)

    return run
```

```python
import math

import jax
import jax.numpy as jnp
import ml_dtypes
import numpy as np
from jax import lax
from jax.experimental import pallas as pl
from jax.experimental.pallas import tpu as pltpu
from jax.sharding import Mesh
from jax.sharding import PartitionSpec as P

NG = 48


screening = 4.0
careful = lax.Precision.HIGH
lanes = 128
f32 = jnp.float32
bf16 = jnp.bfloat16
contract_last = (((1,), (1,)), ((), ()))


def dft_tables(length):
    positions = jnp.arange(length, dtype=jnp.int32)
    product = positions[:, None] * positions[None, :] % length
    angles = product.astype(jnp.float32) * (2.0 * math.pi / length)
    return (jnp.cos(angles), jnp.sin(angles))


def kernel_table():
    full_index = jnp.arange(NG, dtype=jnp.int32)
    wrapped = jnp.where(full_index > NG // 2, full_index - NG, full_index).astype(jnp.float32)
    half_index = jnp.arange(NG // 2 + 1, dtype=jnp.int32).astype(jnp.float32)
    step_size = 2.0 * math.pi / NG
    full_sq = wrapped * step_size * (wrapped * step_size)
    half_sq = half_index * step_size * (half_index * step_size)
    summed = full_sq[:, None, None] + full_sq[None, :, None] + half_sq[None, None, :]
    return screening / (screening + summed)


def apply_axis(values, matrix, pattern):
    return jnp.einsum(
        pattern, values, matrix, precision=careful, preferred_element_type=jnp.float32
    )


def split_apply(values, matrix, pattern):
    upper = matrix.astype(jnp.bfloat16)
    lower = (matrix - upper.astype(jnp.float32)).astype(jnp.bfloat16)
    first = jnp.einsum(pattern, values, upper, preferred_element_type=jnp.float32)
    return first + jnp.einsum(pattern, values, lower, preferred_element_type=jnp.float32)


def solve_one(vector_row):
    half_len = NG // 2 + 1
    cosine, sin_table = dft_tables(NG)
    cos_half = cosine[:, :half_len]
    sin_half = sin_table[:, :half_len]
    cube_vals = vector_row.reshape(NG, NG, NG)
    real_part = split_apply(cube_vals, cos_half, "xyz,zm->xym")
    imag_part = -split_apply(cube_vals, sin_half, "xyz,zm->xym")
    for pattern in ("xym,yb->xbm", "xym,xb->bym"):
        real_next = apply_axis(real_part, cosine, pattern) + apply_axis(
            imag_part, sin_table, pattern
        )
        imag_part = apply_axis(imag_part, cosine, pattern) - apply_axis(
            real_part, sin_table, pattern
        )
        real_part = real_next
    weights = kernel_table()
    real_part = real_part * weights
    imag_part = imag_part * weights
    for pattern in ("xym,xb->bym", "xym,yb->xbm"):
        real_next = apply_axis(real_part, cosine, pattern) - apply_axis(
            imag_part, sin_table, pattern
        )
        imag_part = apply_axis(real_part, sin_table, pattern) + apply_axis(
            imag_part, cosine, pattern
        )
        real_part = real_next
    frequency = jnp.arange(half_len, dtype=jnp.int32)
    fold_weight = jnp.where((frequency == 0) | (frequency == NG // 2), 1.0, 2.0).astype(jnp.float32)
    result = apply_axis(real_part * fold_weight, cos_half, "xym,zm->xyz") - apply_axis(
        imag_part * fold_weight, sin_half, "xym,zm->xyz"
    )
    return (result * (1.0 / (NG * NG * NG))).reshape(-1).astype(jnp.bfloat16)


def plain_body(orbitals, targets, points, fit):
    occupied, shard_len = orbitals.shape
    target_count = targets.shape[0]
    group_size = points.shape[0]
    slab_count = lax.axis_size("slab")
    offsets = points - lax.axis_index("grid") * shard_len
    cell_ids = lax.broadcasted_iota(jnp.int32, (group_size, shard_len), 1)
    one_hot = (cell_ids == offsets[:, None]).astype(jnp.bfloat16)
    point_terms = lax.dot_general(
        orbitals, one_hot, (((1,), (1,)), ((), ())), preferred_element_type=jnp.float32
    )
    at_points = lax.psum(point_terms, "grid").astype(jnp.bfloat16)
    chosen = jnp.take(orbitals, targets, axis=0)
    target_points = jnp.take(at_points, targets, axis=0)
    contract_first = (((0,), (0,)), ((), ()))
    density = lax.dot_general(
        at_points, orbitals, contract_first, preferred_element_type=jnp.float32
    ) * (1.0 / math.sqrt(occupied))
    target_density = lax.dot_general(
        target_points, chosen, contract_first, preferred_element_type=jnp.float32
    ) * (1.0 / math.sqrt(target_count))
    pairs = density * target_density
    fitted = lax.dot_general(
        fit,
        pairs,
        contract_first,
        precision=lax.Precision.HIGHEST,
        preferred_element_type=jnp.float32,
    ).astype(jnp.bfloat16)
    vectors = lax.all_to_all(fitted, "grid", split_axis=0, concat_axis=1, tiled=True)
    potential = lax.map(solve_one, vectors)
    returned = lax.all_to_all(potential, "grid", split_axis=1, concat_axis=0, tiled=True)
    weighted = (returned.astype(jnp.float32) * density).astype(jnp.bfloat16)
    prefactor = -1.0 / math.sqrt(group_size * slab_count)
    regrouped = lax.all_to_all(weighted, "slab", split_axis=1, concat_axis=0, tiled=True)
    all_targets = lax.all_gather(target_points, "slab", axis=1, tiled=True)
    block_out = jnp.dot(all_targets, regrouped, preferred_element_type=jnp.float32)
    summed = lax.all_to_all(block_out, "slab", split_axis=0, concat_axis=1, tiled=True)
    return summed * prefactor


def hartley(length):
    angles = np.outer(np.arange(length), np.arange(length)) % length * (2.0 * math.pi / length)
    matrix = np.cos(angles) + np.sin(angles)
    values = np.unique(np.round(np.abs(matrix), 12))
    scales = 2.0 ** (np.arange(1 << 14) / (1 << 14))
    exact = scales[:, None] * values
    errors = ((exact.astype(ml_dtypes.bfloat16).astype(np.float64) - exact) / scales[:, None]) ** 2
    scale = scales[np.argmin(errors.sum(axis=1))]
    return (matrix * scale).astype(ml_dtypes.bfloat16), scale


def split_value(value):
    upper = value.astype(bf16)
    return upper, (value - upper.astype(jnp.float32)).astype(bf16)


class Plan:
    def __init__(self, edge):
        self.edge = edge
        self.half = edge // 2
        self.slot = lanes // 2
        self.inner = lanes // math.gcd(edge, lanes)
        self.outer = edge // self.inner
        self.block = self.inner * edge
        self.block_rows = self.block // lanes
        self.plane_rows = edge * edge // lanes
        self.rows = edge * self.plane_rows
        matrix, scale = hartley(edge)
        self.windows = []
        tables = []
        for j in range(self.inner // 2):
            low, high = 2 * j * edge, (2 * j + 2) * edge
            base = low // lanes * lanes
            self.windows.append((low, high, base))
            table = np.zeros((2 * lanes, 2, 2, self.slot), ml_dtypes.bfloat16)
            for h in range(2):
                for y in range(2):
                    for z in range(edge):
                        table[(low + y * edge + z - base + h * lanes) % (2 * lanes), y, h, :edge] = matrix[z]
            tables.append(table.reshape(2 * lanes, 2 * lanes))
        self.forward = np.concatenate(tables)
        self.backward = np.concatenate([table.T for table in tables])
        step = 2.0 * math.pi / edge
        index = np.arange(edge)
        square = (np.where(index > edge // 2, index - edge, index) * step) ** 2
        weights = screening / (screening + square[:, None, None] + square[None, :, None] + square[None, None, :])
        weights = weights.reshape(2, self.half, edge, edge)
        table = np.zeros((self.half, edge, 2, self.slot))
        table[..., :edge] = np.transpose(weights, (1, 2, 0, 3))
        self.weights = (table.reshape(self.half, edge, lanes) / (edge * scale ** 2) ** 3).astype(np.float32)
        self.left = np.concatenate([matrix, matrix], axis=1)

    def tables(self):
        return [self.left, self.forward, self.backward, self.weights]


def both_parts(value):
    return jnp.concatenate(split_value(value), axis=0)


def dot(a, b):
    return jnp.dot(a, b, preferred_element_type=jnp.float32)


def product(value, table):
    rows = value.shape[0]
    both = dot(both_parts(value), table)
    return both[:rows] + both[rows:]


def solve(plan, cube, left, forward, backward, weights, mid):
    edge, half, inner, outer, block = plan.edge, plan.half, plan.inner, plan.outer, plan.block
    left_all = left[...]
    values = jnp.concatenate(
        [cube[pl.ds(c, edge, stride=plan.plane_rows), :].astype(bf16) for c in range(plan.plane_rows)], axis=1)
    spectrum = dot(left_all[:, :edge], values)

    def tile(h, c):
        return jnp.concatenate([
            spectrum[h * half:(h + 1) * half, b * block + c * lanes:b * block + (c + 1) * lanes] for b in range(outer)], axis=0)

    lane = lax.broadcasted_iota(jnp.int32, (outer * half, lanes), 1)
    tiles = [[tile(h, c) for c in range(plan.block_rows)] for h in range(2)]
    for j, (low, high, base) in enumerate(plan.windows):
        c = base // lanes
        if high - base <= lanes:
            window = [tiles[0][c], tiles[1][c]]
        else:
            window = [jnp.where(lane >= low - base, tiles[0][c], tiles[1][c + 1]),
                      jnp.where(lane < high - base - lanes, tiles[0][c + 1], tiles[1][c])]
        rows = slice(2 * lanes * j, 2 * lanes * (j + 1))
        result = product(jnp.concatenate(window, axis=1), forward[rows, :])
        for b in range(outer):
            for o in range(2):
                y = b * inner + 2 * j + o
                mid[y * half:(y + 1) * half, :] = result[b * half:(b + 1) * half, o * lanes:(o + 1) * lanes]
    for k in range(0, half, 2):
        value = jnp.concatenate([mid[pl.ds(k + o, edge, stride=half), :] for o in range(2)], axis=1)
        value = dot(left_all, both_parts(value))
        value = value * jnp.concatenate([weights[k], weights[k + 1]], axis=1)
        value = dot(left_all, both_parts(value))
        for o in range(2):
            mid[pl.ds(k + o, edge, stride=half), :] = value[:, o * lanes:(o + 1) * lanes]
    results = []
    for j in range(len(plan.windows)):
        rows = slice(2 * lanes * j, 2 * lanes * (j + 1))
        value = jnp.concatenate([
            jnp.concatenate([mid[(b * inner + 2 * j + o) * half:(b * inner + 2 * j + o + 1) * half, :] for b in range(outer)], axis=0)
            for o in range(2)], axis=1)
        results.append(product(value, backward[rows, :]))

    def gathered(h, c):
        value = None
        for (low, high, base), result in zip(plan.windows, results):
            if low < (c + 1) * lanes and high > c * lanes:
                place = (c * lanes - base + h * lanes) % (2 * lanes)
                part = result[:, place:place + lanes]
                value = part if value is None else jnp.where(lane >= low - c * lanes, part, value)
        return value

    tiles = [[gathered(h, c) for c in range(plan.block_rows)] for h in range(2)]
    value = jnp.concatenate([
        jnp.concatenate([tiles[h][c][b * half:(b + 1) * half] for h in range(2)], axis=0)
        for b in range(outer) for c in range(plan.block_rows)], axis=1)
    value = dot(left_all, both_parts(value))
    for c in range(plan.plane_rows):
        cube[pl.ds(c, edge, stride=plan.plane_rows), :] = value[:, c * lanes:(c + 1) * lanes]


def params(mebibytes):
    return pltpu.CompilerParams(vmem_limit_bytes=mebibytes * 1024 * 1024)


whole = pl.BlockSpec(memory_space=pltpu.VMEM)
far = pl.BlockSpec(memory_space=pltpu.HBM)


def iota(shape, axis):
    return lax.broadcasted_iota(jnp.int32, shape, axis)


def read_points(orbitals, targets, points, fit):
    occupied, shard_len = orbitals.shape
    count, group = targets.shape[0], points.shape[0]
    scale = 1.0 / math.sqrt(occupied) / math.sqrt(count)

    def kernel(points_hbm, targets_hbm, fit_hbm, orbitals_ref, out_ref, notes_ref, points_ref, targets_ref, fit_ref, tiles, sems):
        small = [
            pltpu.make_async_copy(source, place, sems.at[group + i])
            for i, (source, place) in enumerate(
                ((points_hbm, points_ref), (targets_hbm, targets_ref), (fit_hbm, fit_ref)))
        ]
        for copy in small:
            copy.start()
        me = lax.axis_index("grid")
        base = me * shard_len
        rows, columns = iota((8, group * lanes), 0), iota((8, group * lanes), 1)
        chosen = jnp.zeros((8, group * lanes), f32)
        copies = []
        small[0].wait()
        for m in range(group):
            local = points_ref[m] - base
            inside = (local >= 0) & (local < shard_len)
            local = jnp.clip(local, 0, shard_len - 1)
            first = pl.multiple_of(local // lanes * lanes, lanes)
            copy = pltpu.make_async_copy(
                orbitals_ref.at[:, pl.ds(first, lanes)], tiles.at[:, pl.ds(m * lanes, lanes)], sems.at[m])
            copy.start()
            copies.append(copy)
            column = jnp.where(inside, local - first + m * lanes, -1)
            chosen = jnp.where((rows == m) & (columns == column), 1.0, chosen)
        chosen = jnp.concatenate([chosen, jnp.zeros_like(chosen)], axis=0).astype(bf16)
        small[1].wait()
        small[2].wait()
        rows, columns = iota((8, lanes), 0), iota((8, lanes), 1)
        counts = jnp.zeros((8, lanes), f32)
        for k in range(count):
            counts = counts + jnp.where(columns == targets_ref[k], 1.0, 0.0)
        notes_ref[:8, :] = counts
        for j in range(group):
            value = jnp.zeros((8, lanes), f32)
            for r in range(8):
                d = r % group
                value = jnp.where(rows == r, fit_ref[(d + j) % group, jnp.bitwise_xor(me, d)], value)
            notes_ref[8 + 8 * j:16 + 8 * j, :] = value * scale
        rows, columns = iota((count, lanes), 0), iota((count, lanes), 1)
        ones = jnp.zeros((count, lanes), f32)
        for k in range(count):
            ones = jnp.where((rows == k) & (columns == targets_ref[k]), 1.0, ones)
        notes_ref[8 + 8 * group:, :] = ones
        for copy in copies:
            copy.wait()
        out = lax.dot_general(chosen, tiles[...], contract_last, preferred_element_type=f32)
        out_ref[...] = jnp.concatenate([out[:8], jnp.zeros((8, lanes - occupied), f32)], axis=1)

    return pl.pallas_call(
        kernel,
        out_shape=[
            pltpu.VMEM((8, lanes), f32),
            pltpu.VMEM((8 + 8 * group + count, lanes), f32),
        ],
        in_specs=[far] * 4,
        out_specs=[whole] * 2,
        scratch_shapes=[
            pltpu.SMEM(points.shape, jnp.int32),
            pltpu.SMEM(targets.shape, jnp.int32),
            pltpu.SMEM(fit.shape, f32),
            pltpu.VMEM((occupied, group * lanes), bf16),
            pltpu.SemaphoreType.DMA((group + 3,)),
        ],
        compiler_params=params(4),
        name="read_points",
    )(*[pltpu.with_memory_space_constraint(value, pltpu.HBM) for value in (points, targets, fit, orbitals)])


def fit_pairs(orbitals, notes, shares):
    occupied, shard_len = orbitals.shape
    group = len(shares)
    shard_rows = shard_len // lanes
    step = shard_rows // 8

    def kernel(notes_ref, orbitals_ref, *refs):
        share_refs, out_refs, at_ref, mid = refs[:group], refs[group:2 * group], refs[2 * group], refs[2 * group + 1]
        at = share_refs[0][...]
        for ref in share_refs[1:]:
            at = at + ref[...]
        at_ref[...] = at
        rows = iota((8, lanes), 0)
        twice = jnp.where(rows < group, at, pltpu.roll(at, group, 0))
        weighted = notes_ref[:8, :] * twice
        upper = weighted.astype(bf16).astype(f32)
        left = jnp.concatenate([twice, upper, weighted - upper, jnp.zeros((8, lanes), f32)], axis=0)
        left = left.astype(bf16)[:, :occupied]
        coefficients = [notes_ref[8 + 8 * j:16 + 8 * j, :] for j in range(group)]
        for c in range(0, shard_rows, step):
            product = jnp.dot(left, orbitals_ref[:, c * lanes:(c + step) * lanes], preferred_element_type=f32)
            for r in range(step):
                part = product[:, r * lanes:(r + 1) * lanes]
                pair = part[:8] * (part[8:16] + part[16:24])
                value = pair * coefficients[0]
                for j in range(1, group):
                    value = value + pltpu.roll(pair, 8 - j, 0) * coefficients[j]
                mid[(c + r) * 8:(c + r + 1) * 8, :] = value
        for d in range(group):
            out_refs[d][...] = mid[pl.ds(d, shard_rows, stride=8), :].astype(bf16)

    piece = jax.ShapeDtypeStruct((shard_rows, lanes), bf16)
    return pl.pallas_call(
        kernel,
        out_shape=[piece] * group + [jax.ShapeDtypeStruct((8, lanes), f32)],
        in_specs=[whole] * (2 + group),
        out_specs=[whole] * (group + 1),
        scratch_shapes=[pltpu.VMEM((shard_rows * 8, lanes), f32)],
        compiler_params=params(16),
        name="fit_pairs",
    )(notes, orbitals, *shares)


def potentials(plan, pieces, offsets, at, parts, place):
    grid_count, piece_rows = len(pieces), pieces[0].shape[0]
    part = piece_rows // parts
    sent = -(-(part + 1) // 8) * 8
    tables = plan.tables()

    def kernel(at_ref, *refs):
        piece_refs, refs = refs[:grid_count], refs[grid_count:]
        table_refs, (out_ref, cube, mid) = refs[:len(tables)], refs[len(tables):]
        me = lax.axis_index("grid")
        for d, ref in zip(offsets, piece_refs):
            start = pl.multiple_of(jnp.bitwise_xor(me, d) * piece_rows, 8)
            cube[pl.ds(start, piece_rows), :] = ref[...].astype(f32)
        solve(plan, cube, *table_refs, mid)
        own = jnp.broadcast_to(at_ref[pl.ds(me, 1), :], (sent, lanes))
        last = iota((sent, lanes), 0) >= part
        for g in range(grid_count):
            for q in range(parts):
                first = g * piece_rows + q * part
                out_ref[place[q * grid_count + g]] = jnp.where(last, own, cube[first:first + sent, :]).astype(bf16)

    return pl.pallas_call(
        kernel,
        out_shape=jax.ShapeDtypeStruct((parts * grid_count, sent, lanes), bf16),
        in_specs=[whole] * (1 + grid_count + len(tables)),
        out_specs=whole,
        scratch_shapes=[
            pltpu.VMEM((plan.rows + 8, lanes), f32),
            pltpu.VMEM((plan.edge * plan.half, lanes), f32),
        ],
        compiler_params=params(24),
        name="potentials",
    )(at, *pieces, *tables)


def apply_part(orbitals, notes, received, part, count, place, halves):
    occupied, shard_len = orbitals.shape
    points, pitch = received.shape[:2]
    slab_count = len(place)
    keep = count // slab_count
    prefactor = -1.0 / math.sqrt(points * halves)

    def kernel(notes_ref, orbitals_ref, received_ref, out_ref, spread, mid, stage):
        for m in range(points):
            spread[m * pitch:(m + 1) * pitch, :] = received_ref[m].astype(f32)
        at = spread[pl.ds(part, points, stride=pitch), :][:, :occupied].astype(bf16)
        first = pl.multiple_of(lax.axis_index("part") * (part * lanes), lanes)
        swapped = lax.axis_index("grid") % 2 == 1
        density = jnp.dot(at, orbitals_ref[:, pl.ds(first, part * lanes)], preferred_element_type=f32)
        chosen = notes_ref[notes_ref.shape[0] - count:, :][:, :occupied].astype(bf16)
        target_points = lax.dot_general(chosen, at, contract_last, preferred_element_type=f32).astype(bf16)
        potential = jnp.concatenate([spread[pl.ds(r, points, stride=pitch), :] for r in range(part)], axis=1)
        weighted = (potential * (density * (1.0 / math.sqrt(occupied)))).astype(bf16)
        applied = jnp.dot(target_points, weighted, preferred_element_type=f32) * prefactor
        for r in range(part):
            mid[r * count:(r + 1) * count, :] = applied[:, r * lanes:(r + 1) * lanes]
        for s in range(slab_count):
            for k in range(keep):
                stage[s, k * part:(k + 1) * part, :] = mid[pl.ds(s * keep + k, part, stride=count), :]
            out_ref[jnp.where(swapped, place[s ^ 1], place[s])] = stage[s].astype(bf16)

    return pl.pallas_call(
        kernel,
        out_shape=jax.ShapeDtypeStruct((slab_count, keep * part, lanes), bf16),
        in_specs=[whole] * 3,
        out_specs=whole,
        scratch_shapes=[
            pltpu.VMEM((points * pitch, lanes), f32),
            pltpu.VMEM((part * count, lanes), f32),
            pltpu.VMEM((slab_count, keep * part, lanes), f32),
        ],
        compiler_params=params(16),
        name="apply_part",
    )(notes, orbitals, received)


def settle(kept, keep, halves, order):
    slab_count, rows = kept.shape[:2]
    parts = slab_count // halves
    part = rows // keep

    def kernel(kept_ref, out_ref, stage):
        swapped = lax.axis_index("grid") % 2 == 1
        for q in range(parts):
            stage[q] = sum(kept_ref[j].astype(f32) for j in range(slab_count) if order[j] % parts == q)
            first = jnp.where(swapped, q ^ 1, q) * part
            for k in range(keep):
                out_ref[pl.ds(first, part), k, :] = stage[q, k * part:(k + 1) * part, :]

    return pl.pallas_call(
        kernel,
        out_shape=jax.ShapeDtypeStruct((parts * part, keep, lanes), f32),
        in_specs=[whole],
        out_specs=whole,
        scratch_shapes=[pltpu.VMEM((parts, rows, lanes), f32)],
        compiler_params=params(4),
        name="settle",
    )(kept)


def bits_reversed(count):
    order = [0]
    while len(order) < count:
        order = [2 * i for i in order] + [2 * i + 1 for i in order]
    return order


def places(order):
    return [order.index(i) for i in range(len(order))]


def exchange(value, grid_count, offset):
    return lax.ppermute(value, "grid", [(i, i ^ offset) for i in range(grid_count)])


def quick_body(orbitals, targets, points, fit):
    grid_count, part_count, halves = (lax.axis_size(name) for name in ("grid", "part", "half"))
    shard_len, slab_count = orbitals.shape[1], part_count * halves
    count = targets.shape[0]
    keep = count // slab_count
    part = shard_len // lanes // part_count
    plan = Plan(round((shard_len * grid_count) ** (1 / 3)))
    share, notes = read_points(orbitals, targets, points, fit)
    shares = [share] + [exchange(share, grid_count, d) for d in range(1, grid_count)]
    *pieces, at = fit_pairs(orbitals, notes, shares)
    offsets = [0] + list(reversed(range(1, grid_count)))
    pieces = [exchange(pieces[d], grid_count, d) if d else pieces[d] for d in offsets]
    near = bits_reversed(part_count * grid_count)[::-1]
    far = [s ^ (s >> 1) ^ 1 for s in reversed(range(slab_count))]
    far_groups = [[(s ^ g % 2) * grid_count + g for s in far] for g in range(grid_count)]
    sent = potentials(plan, pieces, offsets, at, part_count, places(near))
    received = lax.all_to_all(sent, ("part", "grid"), 0, 0, axis_index_groups=[near])
    blocks = apply_part(orbitals, notes, received, part, count, places(far), halves)
    kept = lax.all_to_all(blocks, ("half", "part", "grid"), 0, 0, axis_index_groups=far_groups)
    return jnp.transpose(settle(kept, keep, halves, far), (1, 0, 2)).reshape(keep, shard_len)


def quick_fits(mesh, orbitals, targets, points, fit):
    grid_count, slab_count = mesh.shape["grid"], mesh.shape["slab"]
    occupied, cells = orbitals.shape
    group, edge = fit.shape[1], round(cells ** (1 / 3))
    shard_rows = cells // grid_count // lanes
    return (
        group == grid_count
        and 2 * group == 8
        and occupied <= lanes
        and occupied % 16 == 0
        and edge ** 3 == cells
        and edge % 16 == 0
        and edge <= lanes // 2
        and cells % (grid_count * lanes) == 0
        and shard_rows % 8 == 0
        and slab_count > 2
        and (slab_count * grid_count).bit_count() == 1
        and shard_rows % (slab_count // 2) == 0
        and targets.shape[0] % slab_count == 0
        and targets.shape[0] % 8 == 0
    )


def solution(mesh):
    grid_count, slab_count = mesh.shape["grid"], mesh.shape["slab"]
    out_specs = P("slab", "grid")

    def run(*arrays):
        if not quick_fits(mesh, *arrays):
            in_specs = (P(None, "grid"), P(), P("slab"), P("slab", None))
            return jax.shard_map(plain_body, mesh=mesh, in_specs=in_specs, out_specs=out_specs, check_vma=False)(*arrays)
        halved = Mesh(mesh.devices.reshape(2, slab_count // 2, grid_count), ("half", "part", "grid"))
        slab = ("half", "part")
        in_specs = (P(None, "grid"), P(), P(slab), P(slab, None))
        return jax.shard_map(
            quick_body, mesh=halved, in_specs=in_specs, out_specs=P(slab, "grid"), check_vma=False)(*arrays)

    return run
```

```python
import math

import jax
import jax.numpy as jnp
import ml_dtypes
import numpy as np
from jax import lax
from jax.experimental import pallas as pl
from jax.experimental.pallas import tpu as pltpu
from jax.sharding import Mesh
from jax.sharding import PartitionSpec as P

NG = 48


screening = 4.0
careful = lax.Precision.HIGH
lanes = 128
f32 = jnp.float32
bf16 = jnp.bfloat16
contract_last = (((1,), (1,)), ((), ()))


def dft_tables(length):
    positions = jnp.arange(length, dtype=jnp.int32)
    product = positions[:, None] * positions[None, :] % length
    angles = product.astype(jnp.float32) * (2.0 * math.pi / length)
    return (jnp.cos(angles), jnp.sin(angles))


def kernel_table():
    full_index = jnp.arange(NG, dtype=jnp.int32)
    wrapped = jnp.where(full_index > NG // 2, full_index - NG, full_index).astype(jnp.float32)
    half_index = jnp.arange(NG // 2 + 1, dtype=jnp.int32).astype(jnp.float32)
    step_size = 2.0 * math.pi / NG
    full_sq = wrapped * step_size * (wrapped * step_size)
    half_sq = half_index * step_size * (half_index * step_size)
    summed = full_sq[:, None, None] + full_sq[None, :, None] + half_sq[None, None, :]
    return screening / (screening + summed)


def apply_axis(values, matrix, pattern):
    return jnp.einsum(
        pattern, values, matrix, precision=careful, preferred_element_type=jnp.float32
    )


def split_apply(values, matrix, pattern):
    upper = matrix.astype(jnp.bfloat16)
    lower = (matrix - upper.astype(jnp.float32)).astype(jnp.bfloat16)
    first = jnp.einsum(pattern, values, upper, preferred_element_type=jnp.float32)
    return first + jnp.einsum(pattern, values, lower, preferred_element_type=jnp.float32)


def solve_one(vector_row):
    half_len = NG // 2 + 1
    cosine, sin_table = dft_tables(NG)
    cos_half = cosine[:, :half_len]
    sin_half = sin_table[:, :half_len]
    cube_vals = vector_row.reshape(NG, NG, NG)
    real_part = split_apply(cube_vals, cos_half, "xyz,zm->xym")
    imag_part = -split_apply(cube_vals, sin_half, "xyz,zm->xym")
    for pattern in ("xym,yb->xbm", "xym,xb->bym"):
        real_next = apply_axis(real_part, cosine, pattern) + apply_axis(
            imag_part, sin_table, pattern
        )
        imag_part = apply_axis(imag_part, cosine, pattern) - apply_axis(
            real_part, sin_table, pattern
        )
        real_part = real_next
    weights = kernel_table()
    real_part = real_part * weights
    imag_part = imag_part * weights
    for pattern in ("xym,xb->bym", "xym,yb->xbm"):
        real_next = apply_axis(real_part, cosine, pattern) - apply_axis(
            imag_part, sin_table, pattern
        )
        imag_part = apply_axis(real_part, sin_table, pattern) + apply_axis(
            imag_part, cosine, pattern
        )
        real_part = real_next
    frequency = jnp.arange(half_len, dtype=jnp.int32)
    fold_weight = jnp.where((frequency == 0) | (frequency == NG // 2), 1.0, 2.0).astype(jnp.float32)
    result = apply_axis(real_part * fold_weight, cos_half, "xym,zm->xyz") - apply_axis(
        imag_part * fold_weight, sin_half, "xym,zm->xyz"
    )
    return (result * (1.0 / (NG * NG * NG))).reshape(-1).astype(jnp.bfloat16)


def plain_body(orbitals, targets, points, fit):
    occupied, shard_len = orbitals.shape
    target_count = targets.shape[0]
    group_size = points.shape[0]
    slab_count = lax.axis_size("slab")
    offsets = points - lax.axis_index("grid") * shard_len
    cell_ids = lax.broadcasted_iota(jnp.int32, (group_size, shard_len), 1)
    one_hot = (cell_ids == offsets[:, None]).astype(jnp.bfloat16)
    point_terms = lax.dot_general(
        orbitals, one_hot, (((1,), (1,)), ((), ())), preferred_element_type=jnp.float32
    )
    at_points = lax.psum(point_terms, "grid").astype(jnp.bfloat16)
    chosen = jnp.take(orbitals, targets, axis=0)
    target_points = jnp.take(at_points, targets, axis=0)
    contract_first = (((0,), (0,)), ((), ()))
    density = lax.dot_general(
        at_points, orbitals, contract_first, preferred_element_type=jnp.float32
    ) * (1.0 / math.sqrt(occupied))
    target_density = lax.dot_general(
        target_points, chosen, contract_first, preferred_element_type=jnp.float32
    ) * (1.0 / math.sqrt(target_count))
    pairs = density * target_density
    fitted = lax.dot_general(
        fit,
        pairs,
        contract_first,
        precision=lax.Precision.HIGHEST,
        preferred_element_type=jnp.float32,
    ).astype(jnp.bfloat16)
    vectors = lax.all_to_all(fitted, "grid", split_axis=0, concat_axis=1, tiled=True)
    potential = lax.map(solve_one, vectors)
    returned = lax.all_to_all(potential, "grid", split_axis=1, concat_axis=0, tiled=True)
    weighted = (returned.astype(jnp.float32) * density).astype(jnp.bfloat16)
    prefactor = -1.0 / math.sqrt(group_size * slab_count)
    regrouped = lax.all_to_all(weighted, "slab", split_axis=1, concat_axis=0, tiled=True)
    all_targets = lax.all_gather(target_points, "slab", axis=1, tiled=True)
    block_out = jnp.dot(all_targets, regrouped, preferred_element_type=jnp.float32)
    summed = lax.all_to_all(block_out, "slab", split_axis=0, concat_axis=1, tiled=True)
    return summed * prefactor


def hartley(length):
    angles = np.outer(np.arange(length), np.arange(length)) % length * (2.0 * math.pi / length)
    matrix = np.cos(angles) + np.sin(angles)
    values = np.unique(np.round(np.abs(matrix), 12))
    scales = 2.0 ** (np.arange(1 << 14) / (1 << 14))
    exact = scales[:, None] * values
    errors = ((exact.astype(ml_dtypes.bfloat16).astype(np.float64) - exact) / scales[:, None]) ** 2
    scale = scales[np.argmin(errors.sum(axis=1))]
    return (matrix * scale).astype(ml_dtypes.bfloat16), scale


def split_value(value):
    upper = value.astype(bf16)
    return upper, (value - upper.astype(jnp.float32)).astype(bf16)


class Plan:
    def __init__(self, edge):
        self.edge = edge
        self.half = edge // 2
        self.slot = lanes // 2
        self.inner = lanes // math.gcd(edge, lanes)
        self.outer = edge // self.inner
        self.block = self.inner * edge
        self.block_rows = self.block // lanes
        self.plane_rows = edge * edge // lanes
        self.rows = edge * self.plane_rows
        matrix, scale = hartley(edge)
        self.windows = []
        tables = []
        for j in range(self.inner // 2):
            low, high = 2 * j * edge, (2 * j + 2) * edge
            base = low // lanes * lanes
            self.windows.append((low, high, base))
            table = np.zeros((2 * lanes, 2, 2, self.slot), ml_dtypes.bfloat16)
            for h in range(2):
                for y in range(2):
                    for z in range(edge):
                        table[(low + y * edge + z - base + h * lanes) % (2 * lanes), y, h, :edge] = matrix[z]
            tables.append(table.reshape(2 * lanes, 2 * lanes))
        self.forward = np.concatenate(tables)
        self.backward = np.concatenate([table.T for table in tables])
        step = 2.0 * math.pi / edge
        index = np.arange(edge)
        square = (np.where(index > edge // 2, index - edge, index) * step) ** 2
        weights = screening / (screening + square[:, None, None] + square[None, :, None] + square[None, None, :])
        weights = weights.reshape(2, self.half, edge, edge)
        table = np.zeros((self.half, edge, 2, self.slot))
        table[..., :edge] = np.transpose(weights, (1, 2, 0, 3))
        self.weights = (table.reshape(self.half, edge, lanes) / (edge * scale ** 2) ** 3).astype(np.float32)
        self.left = np.concatenate([matrix, matrix], axis=1)

    def tables(self):
        return [self.left, self.forward, self.backward, self.weights]


def both_parts(value):
    return jnp.concatenate(split_value(value), axis=0)


def dot(a, b):
    return jnp.dot(a, b, preferred_element_type=jnp.float32)


def product(value, table):
    rows = value.shape[0]
    both = dot(both_parts(value), table)
    return both[:rows] + both[rows:]


def solve(plan, cube, left, forward, backward, weights, mid):
    edge, half, inner, outer, block = plan.edge, plan.half, plan.inner, plan.outer, plan.block
    left_all = left[...]
    values = jnp.concatenate(
        [cube[pl.ds(c, edge, stride=plan.plane_rows), :].astype(bf16) for c in range(plan.plane_rows)], axis=1)
    spectrum = dot(left_all[:, :edge], values)

    def tile(h, c):
        return jnp.concatenate([
            spectrum[h * half:(h + 1) * half, b * block + c * lanes:b * block + (c + 1) * lanes] for b in range(outer)], axis=0)

    lane = lax.broadcasted_iota(jnp.int32, (outer * half, lanes), 1)
    tiles = [[tile(h, c) for c in range(plan.block_rows)] for h in range(2)]
    for j, (low, high, base) in enumerate(plan.windows):
        c = base // lanes
        if high - base <= lanes:
            window = [tiles[0][c], tiles[1][c]]
        else:
            window = [jnp.where(lane >= low - base, tiles[0][c], tiles[1][c + 1]),
                      jnp.where(lane < high - base - lanes, tiles[0][c + 1], tiles[1][c])]
        rows = slice(2 * lanes * j, 2 * lanes * (j + 1))
        result = product(jnp.concatenate(window, axis=1), forward[rows, :])
        for b in range(outer):
            for o in range(2):
                y = b * inner + 2 * j + o
                mid[y * half:(y + 1) * half, :] = result[b * half:(b + 1) * half, o * lanes:(o + 1) * lanes]
    for k in range(0, half, 2):
        value = jnp.concatenate([mid[pl.ds(k + o, edge, stride=half), :] for o in range(2)], axis=1)
        value = dot(left_all, both_parts(value))
        value = value * jnp.concatenate([weights[k], weights[k + 1]], axis=1)
        value = dot(left_all, both_parts(value))
        for o in range(2):
            mid[pl.ds(k + o, edge, stride=half), :] = value[:, o * lanes:(o + 1) * lanes]
    results = []
    for j in range(len(plan.windows)):
        rows = slice(2 * lanes * j, 2 * lanes * (j + 1))
        value = jnp.concatenate([
            jnp.concatenate([mid[(b * inner + 2 * j + o) * half:(b * inner + 2 * j + o + 1) * half, :] for b in range(outer)], axis=0)
            for o in range(2)], axis=1)
        results.append(product(value, backward[rows, :]))

    def gathered(h, c):
        value = None
        for (low, high, base), result in zip(plan.windows, results):
            if low < (c + 1) * lanes and high > c * lanes:
                place = (c * lanes - base + h * lanes) % (2 * lanes)
                part = result[:, place:place + lanes]
                value = part if value is None else jnp.where(lane >= low - c * lanes, part, value)
        return value

    tiles = [[gathered(h, c) for c in range(plan.block_rows)] for h in range(2)]
    value = jnp.concatenate([
        jnp.concatenate([tiles[h][c][b * half:(b + 1) * half] for h in range(2)], axis=0)
        for b in range(outer) for c in range(plan.block_rows)], axis=1)
    value = dot(left_all, both_parts(value))
    for c in range(plan.plane_rows):
        cube[pl.ds(c, edge, stride=plan.plane_rows), :] = value[:, c * lanes:(c + 1) * lanes]


def params(mebibytes):
    return pltpu.CompilerParams(vmem_limit_bytes=mebibytes * 1024 * 1024)


whole = pl.BlockSpec(memory_space=pltpu.VMEM)
far = pl.BlockSpec(memory_space=pltpu.HBM)


def iota(shape, axis):
    return lax.broadcasted_iota(jnp.int32, shape, axis)


def read_points(orbitals, targets, points, fit):
    occupied, shard_len = orbitals.shape
    count, group = targets.shape[0], points.shape[0]
    scale = 1.0 / math.sqrt(occupied) / math.sqrt(count)

    def kernel(points_hbm, targets_hbm, fit_hbm, orbitals_ref, out_ref, notes_ref, points_ref, targets_ref, fit_ref, tiles, sems):
        small = [
            pltpu.make_async_copy(source, place, sems.at[group + i])
            for i, (source, place) in enumerate(
                ((points_hbm, points_ref), (targets_hbm, targets_ref), (fit_hbm, fit_ref)))
        ]
        for copy in small:
            copy.start()
        me = lax.axis_index("grid")
        base = me * shard_len
        rows, columns = iota((8, group * lanes), 0), iota((8, group * lanes), 1)
        chosen = jnp.zeros((8, group * lanes), f32)
        copies = []
        small[0].wait()
        for m in range(group):
            local = points_ref[m] - base
            inside = (local >= 0) & (local < shard_len)
            local = jnp.clip(local, 0, shard_len - 1)
            first = pl.multiple_of(local // lanes * lanes, lanes)
            copy = pltpu.make_async_copy(
                orbitals_ref.at[:, pl.ds(first, lanes)], tiles.at[:, pl.ds(m * lanes, lanes)], sems.at[m])
            copy.start()
            copies.append(copy)
            column = jnp.where(inside, local - first + m * lanes, -1)
            chosen = jnp.where((rows == m) & (columns == column), 1.0, chosen)
        chosen = jnp.concatenate([chosen, jnp.zeros_like(chosen)], axis=0).astype(bf16)
        small[1].wait()
        small[2].wait()
        rows, columns = iota((8, lanes), 0), iota((8, lanes), 1)
        counts = jnp.zeros((8, lanes), f32)
        for k in range(count):
            counts = counts + jnp.where(columns == targets_ref[k], 1.0, 0.0)
        notes_ref[:8, :] = counts
        for j in range(group):
            value = jnp.zeros((8, lanes), f32)
            for r in range(8):
                d = r % group
                value = jnp.where(rows == r, fit_ref[(d + j) % group, jnp.bitwise_xor(me, d)], value)
            notes_ref[8 + 8 * j:16 + 8 * j, :] = value * scale
        rows, columns = iota((count, lanes), 0), iota((count, lanes), 1)
        ones = jnp.zeros((count, lanes), f32)
        for k in range(count):
            ones = jnp.where((rows == k) & (columns == targets_ref[k]), 1.0, ones)
        notes_ref[8 + 8 * group:, :] = ones
        for copy in copies:
            copy.wait()
        out = lax.dot_general(chosen, tiles[...], contract_last, preferred_element_type=f32)
        out_ref[...] = jnp.concatenate([out[:8], jnp.zeros((8, lanes - occupied), f32)], axis=1)

    return pl.pallas_call(
        kernel,
        out_shape=[
            pltpu.VMEM((8, lanes), f32),
            pltpu.VMEM((8 + 8 * group + count, lanes), f32),
        ],
        in_specs=[far] * 4,
        out_specs=[whole] * 2,
        scratch_shapes=[
            pltpu.SMEM(points.shape, jnp.int32),
            pltpu.SMEM(targets.shape, jnp.int32),
            pltpu.SMEM(fit.shape, f32),
            pltpu.VMEM((occupied, group * lanes), bf16),
            pltpu.SemaphoreType.DMA((group + 3,)),
        ],
        compiler_params=params(4),
        name="read_points",
    )(*[pltpu.with_memory_space_constraint(value, pltpu.HBM) for value in (points, targets, fit, orbitals)])


def fit_pairs(orbitals, notes, shares):
    occupied, shard_len = orbitals.shape
    group = len(shares)
    shard_rows = shard_len // lanes
    step = shard_rows // 8

    def kernel(notes_ref, orbitals_ref, *refs):
        share_refs, out_refs, at_ref, mid = refs[:group], refs[group:2 * group], refs[2 * group], refs[2 * group + 1]
        at = share_refs[0][...]
        for ref in share_refs[1:]:
            at = at + ref[...]
        at_ref[...] = at
        rows = iota((8, lanes), 0)
        twice = jnp.where(rows < group, at, pltpu.roll(at, group, 0))
        weighted = notes_ref[:8, :] * twice
        upper = weighted.astype(bf16).astype(f32)
        left = jnp.concatenate([twice, upper, weighted - upper, jnp.zeros((8, lanes), f32)], axis=0)
        left = left.astype(bf16)[:, :occupied]
        coefficients = [notes_ref[8 + 8 * j:16 + 8 * j, :] for j in range(group)]
        for c in range(0, shard_rows, step):
            product = jnp.dot(left, orbitals_ref[:, c * lanes:(c + step) * lanes], preferred_element_type=f32)
            for r in range(step):
                part = product[:, r * lanes:(r + 1) * lanes]
                pair = part[:8] * (part[8:16] + part[16:24])
                value = pair * coefficients[0]
                for j in range(1, group):
                    value = value + pltpu.roll(pair, 8 - j, 0) * coefficients[j]
                mid[(c + r) * 8:(c + r + 1) * 8, :] = value
        for d in range(group):
            out_refs[d][...] = mid[pl.ds(d, shard_rows, stride=8), :].astype(bf16)

    piece = jax.ShapeDtypeStruct((shard_rows, lanes), bf16)
    return pl.pallas_call(
        kernel,
        out_shape=[piece] * group + [jax.ShapeDtypeStruct((8, lanes), f32)],
        in_specs=[whole] * (2 + group),
        out_specs=[whole] * (group + 1),
        scratch_shapes=[pltpu.VMEM((shard_rows * 8 + 8, lanes), f32)],
        compiler_params=params(16),
        name="fit_pairs",
    )(notes, orbitals, *shares)


def potentials(plan, pieces, offsets, at, parts, place):
    grid_count, piece_rows = len(pieces), pieces[0].shape[0]
    part = piece_rows // parts
    sent = -(-(part + 1) // 8) * 8
    tables = plan.tables()

    def kernel(at_ref, *refs):
        piece_refs, refs = refs[:grid_count], refs[grid_count:]
        table_refs, (out_ref, cube, mid) = refs[:len(tables)], refs[len(tables):]
        me = lax.axis_index("grid")
        for d, ref in zip(offsets, piece_refs):
            start = pl.multiple_of(jnp.bitwise_xor(me, d) * piece_rows, 8)
            cube[pl.ds(start, piece_rows), :] = ref[...].astype(f32)
        solve(plan, cube, *table_refs, mid)
        own = jnp.broadcast_to(at_ref[pl.ds(me, 1), :], (sent, lanes))
        last = iota((sent, lanes), 0) >= part
        for g in range(grid_count):
            for q in range(parts):
                first = g * piece_rows + q * part
                out_ref[place[q * grid_count + g]] = jnp.where(last, own, cube[first:first + sent, :]).astype(bf16)

    return pl.pallas_call(
        kernel,
        out_shape=jax.ShapeDtypeStruct((parts * grid_count, sent, lanes), bf16),
        in_specs=[whole] * (1 + grid_count + len(tables)),
        out_specs=whole,
        scratch_shapes=[
            pltpu.VMEM((plan.rows + plan.plane_rows + sent, lanes), f32),
            pltpu.VMEM((plan.edge * plan.half + plan.half, lanes), f32),
        ],
        compiler_params=params(24),
        name="potentials",
    )(at, *pieces, *tables)


def apply_part(orbitals, notes, received, part, count, place, halves):
    occupied, shard_len = orbitals.shape
    points, pitch = received.shape[:2]
    slab_count = len(place)
    keep = count // slab_count
    prefactor = -1.0 / math.sqrt(points * halves)

    def kernel(notes_ref, orbitals_ref, received_ref, out_ref, spread, mid, stage):
        for m in range(points):
            spread[m * pitch:(m + 1) * pitch, :] = received_ref[m].astype(f32)
        at = spread[pl.ds(part, points, stride=pitch), :][:, :occupied].astype(bf16)
        first = pl.multiple_of(lax.axis_index("part") * (part * lanes), lanes)
        swapped = lax.axis_index("grid") % 2 == 1
        density = jnp.dot(at, orbitals_ref[:, pl.ds(first, part * lanes)], preferred_element_type=f32)
        chosen = notes_ref[notes_ref.shape[0] - count:, :][:, :occupied].astype(bf16)
        target_points = lax.dot_general(chosen, at, contract_last, preferred_element_type=f32).astype(bf16)
        potential = jnp.concatenate([spread[pl.ds(r, points, stride=pitch), :] for r in range(part)], axis=1)
        weighted = (potential * (density * (1.0 / math.sqrt(occupied)))).astype(bf16)
        applied = jnp.dot(target_points, weighted, preferred_element_type=f32) * prefactor
        for r in range(part):
            mid[r * count:(r + 1) * count, :] = applied[:, r * lanes:(r + 1) * lanes]
        for s in range(slab_count):
            for k in range(keep):
                stage[s, k * part:(k + 1) * part, :] = mid[pl.ds(s * keep + k, part, stride=count), :]
            out_ref[jnp.where(swapped, place[s ^ 1], place[s])] = stage[s, :keep * part, :].astype(bf16)

    return pl.pallas_call(
        kernel,
        out_shape=jax.ShapeDtypeStruct((slab_count, keep * part, lanes), bf16),
        in_specs=[whole] * 3,
        out_specs=whole,
        scratch_shapes=[
            pltpu.VMEM(((points + 1) * pitch, lanes), f32),
            pltpu.VMEM((pitch * count + count, lanes), f32),
            pltpu.VMEM((slab_count, keep * pitch, lanes), f32),
        ],
        compiler_params=params(16),
        name="apply_part",
    )(notes, orbitals, received)


def settle(kept, keep, halves, order):
    slab_count, rows = kept.shape[:2]
    parts = slab_count // halves
    part = rows // keep

    room = -(-part // 8) * 8

    def kernel(kept_ref, out_ref, stage, rowed, sems):
        swapped = lax.axis_index("grid") % 2 == 1
        copies = []
        for q in range(parts):
            stage[q, :rows, :] = sum(kept_ref[j].astype(f32) for j in range(slab_count) if order[j] % parts == q)
            for k in range(keep):
                rowed[q, :part, k, :] = stage[q, k * part:(k + 1) * part, :]
            first = jnp.where(swapped, q ^ 1, q) * part
            copies.append(pltpu.make_async_copy(rowed.at[q, pl.ds(0, part)], out_ref.at[pl.ds(first, part)], sems.at[q]))
            copies[-1].start()
        for copy in copies:
            copy.wait()

    return pl.pallas_call(
        kernel,
        out_shape=jax.ShapeDtypeStruct((parts * part, keep, lanes), f32),
        in_specs=[whole],
        out_specs=far,
        scratch_shapes=[
            pltpu.VMEM((parts, keep * room, lanes), f32),
            pltpu.VMEM((parts, room, keep, lanes), f32),
            pltpu.SemaphoreType.DMA((parts,)),
        ],
        compiler_params=params(4),
        name="settle",
    )(kept)


def bits_reversed(count):
    order = [0]
    while len(order) < count:
        order = [2 * i for i in order] + [2 * i + 1 for i in order]
    return order


def places(order):
    return [order.index(i) for i in range(len(order))]


def exchange(value, grid_count, offset):
    return lax.ppermute(value, "grid", [(i, i ^ offset) for i in range(grid_count)])


def quick_body(orbitals, targets, points, fit):
    grid_count, part_count, halves = (lax.axis_size(name) for name in ("grid", "part", "half"))
    shard_len, slab_count = orbitals.shape[1], part_count * halves
    count = targets.shape[0]
    keep = count // slab_count
    part = shard_len // lanes // part_count
    plan = Plan(round((shard_len * grid_count) ** (1 / 3)))
    share, notes = read_points(orbitals, targets, points, fit)
    shares = [share] + [exchange(share, grid_count, d) for d in range(1, grid_count)]
    *pieces, at = fit_pairs(orbitals, notes, shares)
    offsets = [0] + list(reversed(range(1, grid_count)))
    pieces = [exchange(pieces[d], grid_count, d) if d else pieces[d] for d in offsets]
    near = bits_reversed(part_count * grid_count)[::-1]
    far = [s ^ (s >> 1) ^ 1 for s in reversed(range(slab_count))]
    far_groups = [[(s ^ g % 2) * grid_count + g for s in far] for g in range(grid_count)]
    sent = potentials(plan, pieces, offsets, at, part_count, places(near))
    received = lax.all_to_all(sent, ("part", "grid"), 0, 0, axis_index_groups=[near])
    blocks = apply_part(orbitals, notes, received, part, count, places(far), halves)
    kept = lax.all_to_all(blocks, ("half", "part", "grid"), 0, 0, axis_index_groups=far_groups)
    return jnp.transpose(settle(kept, keep, halves, far), (1, 0, 2)).reshape(keep, shard_len)


def quick_fits(mesh, orbitals, targets, points, fit):
    grid_count, slab_count = mesh.shape["grid"], mesh.shape["slab"]
    occupied, cells = orbitals.shape
    group, edge = fit.shape[1], round(cells ** (1 / 3))
    shard_rows = cells // grid_count // lanes
    return (
        group == grid_count
        and 2 * group == 8
        and occupied <= lanes
        and occupied % 16 == 0
        and edge ** 3 == cells
        and edge % 16 == 0
        and edge <= lanes // 2
        and cells % (grid_count * lanes) == 0
        and shard_rows % 8 == 0
        and slab_count > 2
        and (slab_count * grid_count).bit_count() == 1
        and shard_rows % (slab_count // 2) == 0
        and targets.shape[0] % slab_count == 0
        and targets.shape[0] % 8 == 0
    )


def solution(mesh):
    grid_count, slab_count = mesh.shape["grid"], mesh.shape["slab"]
    out_specs = P("slab", "grid")

    def run(*arrays):
        if not quick_fits(mesh, *arrays):
            in_specs = (P(None, "grid"), P(), P("slab"), P("slab", None))
            return jax.shard_map(plain_body, mesh=mesh, in_specs=in_specs, out_specs=out_specs, check_vma=False)(*arrays)
        halved = Mesh(mesh.devices.reshape(2, slab_count // 2, grid_count), ("half", "part", "grid"))
        slab = ("half", "part")
        in_specs = (P(None, "grid"), P(), P(slab), P(slab, None))
        return jax.shard_map(
            quick_body, mesh=halved, in_specs=in_specs, out_specs=P(slab, "grid"), check_vma=False)(*arrays)

    return run
```

```python
import math

import jax
import jax.numpy as jnp
import ml_dtypes
import numpy as np
from jax import lax
from jax.experimental import pallas as pl
from jax.experimental.pallas import tpu as pltpu
from jax.sharding import Mesh
from jax.sharding import PartitionSpec as P

NG = 48


screening = 4.0
careful = lax.Precision.HIGH
lanes = 128
f32 = jnp.float32
bf16 = jnp.bfloat16
contract_last = (((1,), (1,)), ((), ()))


def dft_tables(length):
    positions = jnp.arange(length, dtype=jnp.int32)
    product = positions[:, None] * positions[None, :] % length
    angles = product.astype(jnp.float32) * (2.0 * math.pi / length)
    return (jnp.cos(angles), jnp.sin(angles))


def kernel_table():
    full_index = jnp.arange(NG, dtype=jnp.int32)
    wrapped = jnp.where(full_index > NG // 2, full_index - NG, full_index).astype(jnp.float32)
    half_index = jnp.arange(NG // 2 + 1, dtype=jnp.int32).astype(jnp.float32)
    step_size = 2.0 * math.pi / NG
    full_sq = wrapped * step_size * (wrapped * step_size)
    half_sq = half_index * step_size * (half_index * step_size)
    summed = full_sq[:, None, None] + full_sq[None, :, None] + half_sq[None, None, :]
    return screening / (screening + summed)


def apply_axis(values, matrix, pattern):
    return jnp.einsum(
        pattern, values, matrix, precision=careful, preferred_element_type=jnp.float32
    )


def split_apply(values, matrix, pattern):
    upper = matrix.astype(jnp.bfloat16)
    lower = (matrix - upper.astype(jnp.float32)).astype(jnp.bfloat16)
    first = jnp.einsum(pattern, values, upper, preferred_element_type=jnp.float32)
    return first + jnp.einsum(pattern, values, lower, preferred_element_type=jnp.float32)


def solve_one(vector_row):
    half_len = NG // 2 + 1
    cosine, sin_table = dft_tables(NG)
    cos_half = cosine[:, :half_len]
    sin_half = sin_table[:, :half_len]
    cube_vals = vector_row.reshape(NG, NG, NG)
    real_part = split_apply(cube_vals, cos_half, "xyz,zm->xym")
    imag_part = -split_apply(cube_vals, sin_half, "xyz,zm->xym")
    for pattern in ("xym,yb->xbm", "xym,xb->bym"):
        real_next = apply_axis(real_part, cosine, pattern) + apply_axis(
            imag_part, sin_table, pattern
        )
        imag_part = apply_axis(imag_part, cosine, pattern) - apply_axis(
            real_part, sin_table, pattern
        )
        real_part = real_next
    weights = kernel_table()
    real_part = real_part * weights
    imag_part = imag_part * weights
    for pattern in ("xym,xb->bym", "xym,yb->xbm"):
        real_next = apply_axis(real_part, cosine, pattern) - apply_axis(
            imag_part, sin_table, pattern
        )
        imag_part = apply_axis(real_part, sin_table, pattern) + apply_axis(
            imag_part, cosine, pattern
        )
        real_part = real_next
    frequency = jnp.arange(half_len, dtype=jnp.int32)
    fold_weight = jnp.where((frequency == 0) | (frequency == NG // 2), 1.0, 2.0).astype(jnp.float32)
    result = apply_axis(real_part * fold_weight, cos_half, "xym,zm->xyz") - apply_axis(
        imag_part * fold_weight, sin_half, "xym,zm->xyz"
    )
    return (result * (1.0 / (NG * NG * NG))).reshape(-1).astype(jnp.bfloat16)


def plain_body(orbitals, targets, points, fit):
    occupied, shard_len = orbitals.shape
    target_count = targets.shape[0]
    group_size = points.shape[0]
    slab_count = lax.axis_size("slab")
    offsets = points - lax.axis_index("grid") * shard_len
    cell_ids = lax.broadcasted_iota(jnp.int32, (group_size, shard_len), 1)
    one_hot = (cell_ids == offsets[:, None]).astype(jnp.bfloat16)
    point_terms = lax.dot_general(
        orbitals, one_hot, (((1,), (1,)), ((), ())), preferred_element_type=jnp.float32
    )
    at_points = lax.psum(point_terms, "grid").astype(jnp.bfloat16)
    chosen = jnp.take(orbitals, targets, axis=0)
    target_points = jnp.take(at_points, targets, axis=0)
    contract_first = (((0,), (0,)), ((), ()))
    density = lax.dot_general(
        at_points, orbitals, contract_first, preferred_element_type=jnp.float32
    ) * (1.0 / math.sqrt(occupied))
    target_density = lax.dot_general(
        target_points, chosen, contract_first, preferred_element_type=jnp.float32
    ) * (1.0 / math.sqrt(target_count))
    pairs = density * target_density
    fitted = lax.dot_general(
        fit,
        pairs,
        contract_first,
        precision=lax.Precision.HIGHEST,
        preferred_element_type=jnp.float32,
    ).astype(jnp.bfloat16)
    vectors = lax.all_to_all(fitted, "grid", split_axis=0, concat_axis=1, tiled=True)
    potential = lax.map(solve_one, vectors)
    returned = lax.all_to_all(potential, "grid", split_axis=1, concat_axis=0, tiled=True)
    weighted = (returned.astype(jnp.float32) * density).astype(jnp.bfloat16)
    prefactor = -1.0 / math.sqrt(group_size * slab_count)
    regrouped = lax.all_to_all(weighted, "slab", split_axis=1, concat_axis=0, tiled=True)
    all_targets = lax.all_gather(target_points, "slab", axis=1, tiled=True)
    block_out = jnp.dot(all_targets, regrouped, preferred_element_type=jnp.float32)
    summed = lax.all_to_all(block_out, "slab", split_axis=0, concat_axis=1, tiled=True)
    return summed * prefactor


def hartley(length):
    product = np.outer(np.arange(length), np.arange(length)) % length
    angles = product * (2.0 * math.pi / length)
    return (np.cos(angles) + np.sin(angles)) / math.sqrt(length)


def split_table(table):
    upper = table.astype(ml_dtypes.bfloat16)
    lower = (table - upper.astype(np.float64)).astype(ml_dtypes.bfloat16)
    return upper, lower


def split_value(value):
    upper = value.astype(bf16)
    return upper, (value - upper.astype(jnp.float32)).astype(bf16)


class Plan:
    def __init__(self, edge):
        self.edge = edge
        self.half = edge // 2
        self.slot = lanes // 2
        self.inner = lanes // math.gcd(edge, lanes)
        self.outer = edge // self.inner
        self.block = self.inner * edge
        self.block_rows = self.block // lanes
        self.plane_rows = edge * edge // lanes
        self.rows = edge * self.plane_rows
        matrix = hartley(edge)
        self.windows = []
        tables = []
        for j in range(self.inner // 2):
            low, high = 2 * j * edge, (2 * j + 2) * edge
            base = low // lanes * lanes
            self.windows.append((low, high, base))
            table = np.zeros((2 * lanes, 2, 2, self.slot))
            for h in range(2):
                for y in range(2):
                    for z in range(edge):
                        table[(low + y * edge + z - base + h * lanes) % (2 * lanes), y, h, :edge] = matrix[z]
            tables.append(table.reshape(2 * lanes, 2 * lanes))
        self.forward = np.concatenate(tables)
        self.backward = np.concatenate([table.T for table in tables])
        step = 2.0 * math.pi / edge
        index = np.arange(edge)
        square = (np.where(index > edge // 2, index - edge, index) * step) ** 2
        weights = screening / (screening + square[:, None, None] + square[None, :, None] + square[None, None, :])
        weights = weights.reshape(2, self.half, edge, edge)
        table = np.zeros((self.half, edge, 2, self.slot))
        table[..., :edge] = np.transpose(weights, (1, 2, 0, 3))
        self.weights = table.reshape(self.half, edge, lanes).astype(np.float32)
        self.left = np.concatenate([*split_table(matrix), split_table(matrix)[0]], axis=1)

    def tables(self):
        fh, fl = split_table(self.forward)
        bh, bl = split_table(self.backward)
        return [self.left, fh, fl, bh, bl, self.weights]


def three(value):
    upper, lower = split_value(value)
    return jnp.concatenate([upper, upper, lower], axis=0)


def dot(a, b):
    return jnp.dot(a, b, preferred_element_type=jnp.float32)


def product(value, upper_table, lower_table):
    rows = value.shape[0]
    upper, lower = split_value(value)
    both = dot(jnp.concatenate([upper, lower], axis=0), upper_table)
    return both[:rows] + both[rows:] + dot(upper, lower_table)


def solve(plan, cube, left, fh, fl, bh, bl, weights, mid):
    edge, half, inner, outer, block = plan.edge, plan.half, plan.inner, plan.outer, plan.block
    left_all = left[...]
    values = jnp.concatenate(
        [cube[pl.ds(c, edge, stride=plan.plane_rows), :].astype(bf16) for c in range(plan.plane_rows)], axis=1)
    spectrum = dot(left_all[:, :2 * edge], jnp.concatenate([values, values], axis=0))

    def tile(h, c):
        return jnp.concatenate([
            spectrum[h * half:(h + 1) * half, b * block + c * lanes:b * block + (c + 1) * lanes] for b in range(outer)], axis=0)

    lane = lax.broadcasted_iota(jnp.int32, (outer * half, lanes), 1)
    tiles = [[tile(h, c) for c in range(plan.block_rows)] for h in range(2)]
    for j, (low, high, base) in enumerate(plan.windows):
        c = base // lanes
        if high - base <= lanes:
            window = [tiles[0][c], tiles[1][c]]
        else:
            window = [jnp.where(lane >= low - base, tiles[0][c], tiles[1][c + 1]),
                      jnp.where(lane < high - base - lanes, tiles[0][c + 1], tiles[1][c])]
        rows = slice(2 * lanes * j, 2 * lanes * (j + 1))
        result = product(jnp.concatenate(window, axis=1), fh[rows, :], fl[rows, :])
        for b in range(outer):
            for o in range(2):
                y = b * inner + 2 * j + o
                mid[y * half:(y + 1) * half, :] = result[b * half:(b + 1) * half, o * lanes:(o + 1) * lanes]
    for k in range(0, half, 2):
        value = jnp.concatenate([mid[pl.ds(k + o, edge, stride=half), :] for o in range(2)], axis=1)
        value = dot(left_all, three(value))
        value = value * jnp.concatenate([weights[k], weights[k + 1]], axis=1)
        value = dot(left_all, three(value))
        for o in range(2):
            mid[pl.ds(k + o, edge, stride=half), :] = value[:, o * lanes:(o + 1) * lanes]
    results = []
    for j in range(len(plan.windows)):
        rows = slice(2 * lanes * j, 2 * lanes * (j + 1))
        value = jnp.concatenate([
            jnp.concatenate([mid[(b * inner + 2 * j + o) * half:(b * inner + 2 * j + o + 1) * half, :] for b in range(outer)], axis=0)
            for o in range(2)], axis=1)
        results.append(product(value, bh[rows, :], bl[rows, :]))

    def gathered(h, c):
        value = None
        for (low, high, base), result in zip(plan.windows, results):
            if low < (c + 1) * lanes and high > c * lanes:
                place = (c * lanes - base + h * lanes) % (2 * lanes)
                part = result[:, place:place + lanes]
                value = part if value is None else jnp.where(lane >= low - c * lanes, part, value)
        return value

    tiles = [[gathered(h, c) for c in range(plan.block_rows)] for h in range(2)]
    value = jnp.concatenate([
        jnp.concatenate([tiles[h][c][b * half:(b + 1) * half] for h in range(2)], axis=0)
        for b in range(outer) for c in range(plan.block_rows)], axis=1)
    value = dot(left_all, three(value))
    for c in range(plan.plane_rows):
        cube[pl.ds(c, edge, stride=plan.plane_rows), :] = value[:, c * lanes:(c + 1) * lanes]


def params(mebibytes):
    return pltpu.CompilerParams(vmem_limit_bytes=mebibytes * 1024 * 1024)


whole = pl.BlockSpec(memory_space=pltpu.VMEM)
far = pl.BlockSpec(memory_space=pltpu.HBM)


def iota(shape, axis):
    return lax.broadcasted_iota(jnp.int32, shape, axis)


def read_points(orbitals, targets, points, fit):
    occupied, shard_len = orbitals.shape
    count, group = targets.shape[0], points.shape[0]
    scale = 1.0 / math.sqrt(occupied) / math.sqrt(count)

    def kernel(points_hbm, targets_hbm, fit_hbm, orbitals_ref, out_ref, notes_ref, points_ref, targets_ref, fit_ref, tiles, sems):
        small = [
            pltpu.make_async_copy(source, place, sems.at[group + i])
            for i, (source, place) in enumerate(
                ((points_hbm, points_ref), (targets_hbm, targets_ref), (fit_hbm, fit_ref)))
        ]
        for copy in small:
            copy.start()
        me = lax.axis_index("grid")
        base = me * shard_len
        rows, columns = iota((8, group * lanes), 0), iota((8, group * lanes), 1)
        chosen = jnp.zeros((8, group * lanes), f32)
        copies = []
        small[0].wait()
        for m in range(group):
            local = points_ref[m] - base
            inside = (local >= 0) & (local < shard_len)
            local = jnp.clip(local, 0, shard_len - 1)
            first = pl.multiple_of(local // lanes * lanes, lanes)
            copy = pltpu.make_async_copy(
                orbitals_ref.at[:, pl.ds(first, lanes)], tiles.at[:, pl.ds(m * lanes, lanes)], sems.at[m])
            copy.start()
            copies.append(copy)
            column = jnp.where(inside, local - first + m * lanes, -1)
            chosen = jnp.where((rows == m) & (columns == column), 1.0, chosen)
        chosen = jnp.concatenate([chosen, jnp.zeros_like(chosen)], axis=0).astype(bf16)
        small[1].wait()
        small[2].wait()
        rows, columns = iota((8, lanes), 0), iota((8, lanes), 1)
        counts = jnp.zeros((8, lanes), f32)
        for k in range(count):
            counts = counts + jnp.where(columns == targets_ref[k], 1.0, 0.0)
        notes_ref[:8, :] = counts
        for j in range(group):
            value = jnp.zeros((8, lanes), f32)
            for r in range(8):
                d = r % group
                value = jnp.where(rows == r, fit_ref[(d + j) % group, jnp.bitwise_xor(me, d)], value)
            notes_ref[8 + 8 * j:16 + 8 * j, :] = value * scale
        rows, columns = iota((count, lanes), 0), iota((count, lanes), 1)
        ones = jnp.zeros((count, lanes), f32)
        for k in range(count):
            ones = jnp.where((rows == k) & (columns == targets_ref[k]), 1.0, ones)
        notes_ref[8 + 8 * group:, :] = ones
        for copy in copies:
            copy.wait()
        out = lax.dot_general(chosen, tiles[...], contract_last, preferred_element_type=f32)
        out_ref[...] = jnp.concatenate([out[:8], jnp.zeros((8, lanes - occupied), f32)], axis=1)

    return pl.pallas_call(
        kernel,
        out_shape=[
            pltpu.VMEM((8, lanes), f32),
            pltpu.VMEM((8 + 8 * group + count, lanes), f32),
        ],
        in_specs=[far] * 4,
        out_specs=[whole] * 2,
        scratch_shapes=[
            pltpu.SMEM(points.shape, jnp.int32),
            pltpu.SMEM(targets.shape, jnp.int32),
            pltpu.SMEM(fit.shape, f32),
            pltpu.VMEM((occupied, group * lanes), bf16),
            pltpu.SemaphoreType.DMA((group + 3,)),
        ],
        compiler_params=params(4),
        name="read_points",
    )(*[pltpu.with_memory_space_constraint(value, pltpu.HBM) for value in (points, targets, fit, orbitals)])


def fit_pairs(orbitals, notes, shares):
    occupied, shard_len = orbitals.shape
    group = len(shares)
    shard_rows = shard_len // lanes
    step = shard_rows // 8

    def kernel(notes_ref, orbitals_ref, *refs):
        share_refs, out_refs, at_ref, mid = refs[:group], refs[group:2 * group], refs[2 * group], refs[2 * group + 1]
        at = share_refs[0][...]
        for ref in share_refs[1:]:
            at = at + ref[...]
        at_ref[...] = at
        rows = iota((8, lanes), 0)
        twice = jnp.where(rows < group, at, pltpu.roll(at, group, 0))
        weighted = notes_ref[:8, :] * twice
        upper = weighted.astype(bf16).astype(f32)
        left = jnp.concatenate([twice, upper, weighted - upper, jnp.zeros((8, lanes), f32)], axis=0)
        left = left.astype(bf16)[:, :occupied]
        coefficients = [notes_ref[8 + 8 * j:16 + 8 * j, :] for j in range(group)]
        for c in range(0, shard_rows, step):
            product = jnp.dot(left, orbitals_ref[:, c * lanes:(c + step) * lanes], preferred_element_type=f32)
            for r in range(step):
                part = product[:, r * lanes:(r + 1) * lanes]
                pair = part[:8] * (part[8:16] + part[16:24])
                value = pair * coefficients[0]
                for j in range(1, group):
                    value = value + pltpu.roll(pair, 8 - j, 0) * coefficients[j]
                mid[(c + r) * 8:(c + r + 1) * 8, :] = value
        for d in range(group):
            out_refs[d][...] = mid[pl.ds(d, shard_rows, stride=8), :].astype(bf16)

    piece = jax.ShapeDtypeStruct((shard_rows, lanes), bf16)
    return pl.pallas_call(
        kernel,
        out_shape=[piece] * group + [jax.ShapeDtypeStruct((8, lanes), f32)],
        in_specs=[whole] * (2 + group),
        out_specs=[whole] * (group + 1),
        scratch_shapes=[pltpu.VMEM((shard_rows * 8 + 8, lanes), f32)],
        compiler_params=params(16),
        name="fit_pairs",
    )(notes, orbitals, *shares)


def potentials(plan, pieces, offsets, at, parts, place):
    grid_count, piece_rows = len(pieces), pieces[0].shape[0]
    part = piece_rows // parts
    sent = -(-(part + 1) // 8) * 8
    tables = plan.tables()

    def kernel(at_ref, *refs):
        piece_refs, refs = refs[:grid_count], refs[grid_count:]
        table_refs, (out_ref, cube, mid) = refs[:len(tables)], refs[len(tables):]
        me = lax.axis_index("grid")
        for d, ref in zip(offsets, piece_refs):
            start = pl.multiple_of(jnp.bitwise_xor(me, d) * piece_rows, 8)
            cube[pl.ds(start, piece_rows), :] = ref[...].astype(f32)
        solve(plan, cube, *table_refs, mid)
        own = jnp.broadcast_to(at_ref[pl.ds(me, 1), :], (sent, lanes))
        last = iota((sent, lanes), 0) >= part
        for g in range(grid_count):
            for q in range(parts):
                first = g * piece_rows + q * part
                out_ref[place[q * grid_count + g]] = jnp.where(last, own, cube[first:first + sent, :]).astype(bf16)

    return pl.pallas_call(
        kernel,
        out_shape=jax.ShapeDtypeStruct((parts * grid_count, sent, lanes), bf16),
        in_specs=[whole] * (1 + grid_count + len(tables)),
        out_specs=whole,
        scratch_shapes=[
            pltpu.VMEM((plan.rows + plan.plane_rows + sent, lanes), f32),
            pltpu.VMEM((plan.edge * plan.half + plan.half, lanes), f32),
        ],
        compiler_params=params(24),
        name="potentials",
    )(at, *pieces, *tables)


def apply_part(orbitals, notes, received, part, count, place, halves):
    occupied, shard_len = orbitals.shape
    points, pitch = received.shape[:2]
    slab_count = len(place)
    keep = count // slab_count
    prefactor = -1.0 / math.sqrt(points * halves)

    def kernel(notes_ref, orbitals_ref, received_ref, out_ref, spread, mid, stage):
        for m in range(points):
            spread[m * pitch:(m + 1) * pitch, :] = received_ref[m].astype(f32)
        at = spread[pl.ds(part, points, stride=pitch), :][:, :occupied].astype(bf16)
        first = pl.multiple_of(lax.axis_index("part") * (part * lanes), lanes)
        swapped = lax.axis_index("grid") % 2 == 1
        density = jnp.dot(at, orbitals_ref[:, pl.ds(first, part * lanes)], preferred_element_type=f32)
        chosen = notes_ref[notes_ref.shape[0] - count:, :][:, :occupied].astype(bf16)
        target_points = lax.dot_general(chosen, at, contract_last, preferred_element_type=f32).astype(bf16)
        potential = jnp.concatenate([spread[pl.ds(r, points, stride=pitch), :] for r in range(part)], axis=1)
        weighted = (potential * (density * (1.0 / math.sqrt(occupied)))).astype(bf16)
        applied = jnp.dot(target_points, weighted, preferred_element_type=f32) * prefactor
        for r in range(part):
            mid[r * count:(r + 1) * count, :] = applied[:, r * lanes:(r + 1) * lanes]
        for s in range(slab_count):
            for k in range(keep):
                stage[s, k * part:(k + 1) * part, :] = mid[pl.ds(s * keep + k, part, stride=count), :]
            out_ref[jnp.where(swapped, place[s ^ 1], place[s])] = stage[s, :keep * part, :].astype(bf16)

    return pl.pallas_call(
        kernel,
        out_shape=jax.ShapeDtypeStruct((slab_count, keep * part, lanes), bf16),
        in_specs=[whole] * 3,
        out_specs=whole,
        scratch_shapes=[
            pltpu.VMEM(((points + 1) * pitch, lanes), f32),
            pltpu.VMEM((pitch * count + count, lanes), f32),
            pltpu.VMEM((slab_count, keep * pitch, lanes), f32),
        ],
        compiler_params=params(16),
        name="apply_part",
    )(notes, orbitals, received)


def settle(kept, keep, halves, order):
    slab_count, rows = kept.shape[:2]
    parts = slab_count // halves
    part = rows // keep

    room = -(-part // 8) * 8

    def kernel(kept_ref, out_ref, stage, rowed, sems):
        swapped = lax.axis_index("grid") % 2 == 1
        copies = []
        for q in range(parts):
            stage[q, :rows, :] = sum(kept_ref[j].astype(f32) for j in range(slab_count) if order[j] % parts == q)
            for k in range(keep):
                rowed[q, :part, k, :] = stage[q, k * part:(k + 1) * part, :]
            first = jnp.where(swapped, q ^ 1, q) * part
            copies.append(pltpu.make_async_copy(rowed.at[q, pl.ds(0, part)], out_ref.at[pl.ds(first, part)], sems.at[q]))
            copies[-1].start()
        for copy in copies:
            copy.wait()

    return pl.pallas_call(
        kernel,
        out_shape=jax.ShapeDtypeStruct((parts * part, keep, lanes), f32),
        in_specs=[whole],
        out_specs=far,
        scratch_shapes=[
            pltpu.VMEM((parts, keep * room, lanes), f32),
            pltpu.VMEM((parts, room, keep, lanes), f32),
            pltpu.SemaphoreType.DMA((parts,)),
        ],
        compiler_params=params(4),
        name="settle",
    )(kept)


def bits_reversed(count):
    order = [0]
    while len(order) < count:
        order = [2 * i for i in order] + [2 * i + 1 for i in order]
    return order


def places(order):
    return [order.index(i) for i in range(len(order))]


def exchange(value, grid_count, offset):
    return lax.ppermute(value, "grid", [(i, i ^ offset) for i in range(grid_count)])


def quick_body(orbitals, targets, points, fit):
    grid_count, part_count, halves = (lax.axis_size(name) for name in ("grid", "part", "half"))
    shard_len, slab_count = orbitals.shape[1], part_count * halves
    count = targets.shape[0]
    keep = count // slab_count
    part = shard_len // lanes // part_count
    plan = Plan(round((shard_len * grid_count) ** (1 / 3)))
    share, notes = read_points(orbitals, targets, points, fit)
    shares = [share] + [exchange(share, grid_count, d) for d in range(1, grid_count)]
    *pieces, at = fit_pairs(orbitals, notes, shares)
    offsets = [0] + list(reversed(range(1, grid_count)))
    pieces = [exchange(pieces[d], grid_count, d) if d else pieces[d] for d in offsets]
    near = bits_reversed(part_count * grid_count)[::-1]
    far = [s ^ (s >> 1) ^ 1 for s in reversed(range(slab_count))]
    far_groups = [[(s ^ g % 2) * grid_count + g for s in far] for g in range(grid_count)]
    sent = potentials(plan, pieces, offsets, at, part_count, places(near))
    received = lax.all_to_all(sent, ("part", "grid"), 0, 0, axis_index_groups=[near])
    blocks = apply_part(orbitals, notes, received, part, count, places(far), halves)
    kept = lax.all_to_all(blocks, ("half", "part", "grid"), 0, 0, axis_index_groups=far_groups)
    return jnp.transpose(settle(kept, keep, halves, far), (1, 0, 2)).reshape(keep, shard_len)


def quick_fits(mesh, orbitals, targets, points, fit):
    grid_count, slab_count = mesh.shape["grid"], mesh.shape["slab"]
    occupied, cells = orbitals.shape
    group, edge = fit.shape[1], round(cells ** (1 / 3))
    shard_rows = cells // grid_count // lanes
    return (
        group == grid_count
        and 2 * group == 8
        and occupied <= lanes
        and occupied % 16 == 0
        and edge ** 3 == cells
        and edge % 16 == 0
        and edge <= lanes // 2
        and cells % (grid_count * lanes) == 0
        and shard_rows % 8 == 0
        and slab_count > 2
        and (slab_count * grid_count).bit_count() == 1
        and shard_rows % (slab_count // 2) == 0
        and targets.shape[0] % slab_count == 0
        and targets.shape[0] % 8 == 0
    )


def solution(mesh):
    grid_count, slab_count = mesh.shape["grid"], mesh.shape["slab"]
    out_specs = P("slab", "grid")

    def run(*arrays):
        if not quick_fits(mesh, *arrays):
            in_specs = (P(None, "grid"), P(), P("slab"), P("slab", None))
            return jax.shard_map(plain_body, mesh=mesh, in_specs=in_specs, out_specs=out_specs, check_vma=False)(*arrays)
        halved = Mesh(mesh.devices.reshape(2, slab_count // 2, grid_count), ("half", "part", "grid"))
        slab = ("half", "part")
        in_specs = (P(None, "grid"), P(), P(slab), P(slab, None))
        return jax.shard_map(
            quick_body, mesh=halved, in_specs=in_specs, out_specs=P(slab, "grid"), check_vma=False)(*arrays)

    return run
```

```python
import math

import jax
import jax.numpy as jnp
import ml_dtypes
import numpy as np
from jax import lax
from jax.experimental import pallas as pl
from jax.experimental.pallas import tpu as pltpu
from jax.sharding import Mesh
from jax.sharding import PartitionSpec as P

NG = 48


screening = 4.0
careful = lax.Precision.HIGH
lanes = 128
f32 = jnp.float32
bf16 = jnp.bfloat16
contract_last = (((1,), (1,)), ((), ()))


def dft_tables(length):
    positions = jnp.arange(length, dtype=jnp.int32)
    product = positions[:, None] * positions[None, :] % length
    angles = product.astype(jnp.float32) * (2.0 * math.pi / length)
    return (jnp.cos(angles), jnp.sin(angles))


def kernel_table():
    full_index = jnp.arange(NG, dtype=jnp.int32)
    wrapped = jnp.where(full_index > NG // 2, full_index - NG, full_index).astype(jnp.float32)
    half_index = jnp.arange(NG // 2 + 1, dtype=jnp.int32).astype(jnp.float32)
    step_size = 2.0 * math.pi / NG
    full_sq = wrapped * step_size * (wrapped * step_size)
    half_sq = half_index * step_size * (half_index * step_size)
    summed = full_sq[:, None, None] + full_sq[None, :, None] + half_sq[None, None, :]
    return screening / (screening + summed)


def apply_axis(values, matrix, pattern):
    return jnp.einsum(
        pattern, values, matrix, precision=careful, preferred_element_type=jnp.float32
    )


def split_apply(values, matrix, pattern):
    upper = matrix.astype(jnp.bfloat16)
    lower = (matrix - upper.astype(jnp.float32)).astype(jnp.bfloat16)
    first = jnp.einsum(pattern, values, upper, preferred_element_type=jnp.float32)
    return first + jnp.einsum(pattern, values, lower, preferred_element_type=jnp.float32)


def solve_one(vector_row):
    half_len = NG // 2 + 1
    cosine, sin_table = dft_tables(NG)
    cos_half = cosine[:, :half_len]
    sin_half = sin_table[:, :half_len]
    cube_vals = vector_row.reshape(NG, NG, NG)
    real_part = split_apply(cube_vals, cos_half, "xyz,zm->xym")
    imag_part = -split_apply(cube_vals, sin_half, "xyz,zm->xym")
    for pattern in ("xym,yb->xbm", "xym,xb->bym"):
        real_next = apply_axis(real_part, cosine, pattern) + apply_axis(
            imag_part, sin_table, pattern
        )
        imag_part = apply_axis(imag_part, cosine, pattern) - apply_axis(
            real_part, sin_table, pattern
        )
        real_part = real_next
    weights = kernel_table()
    real_part = real_part * weights
    imag_part = imag_part * weights
    for pattern in ("xym,xb->bym", "xym,yb->xbm"):
        real_next = apply_axis(real_part, cosine, pattern) - apply_axis(
            imag_part, sin_table, pattern
        )
        imag_part = apply_axis(real_part, sin_table, pattern) + apply_axis(
            imag_part, cosine, pattern
        )
        real_part = real_next
    frequency = jnp.arange(half_len, dtype=jnp.int32)
    fold_weight = jnp.where((frequency == 0) | (frequency == NG // 2), 1.0, 2.0).astype(jnp.float32)
    result = apply_axis(real_part * fold_weight, cos_half, "xym,zm->xyz") - apply_axis(
        imag_part * fold_weight, sin_half, "xym,zm->xyz"
    )
    return (result * (1.0 / (NG * NG * NG))).reshape(-1).astype(jnp.bfloat16)


def plain_body(orbitals, targets, points, fit):
    occupied, shard_len = orbitals.shape
    target_count = targets.shape[0]
    group_size = points.shape[0]
    slab_count = lax.axis_size("slab")
    offsets = points - lax.axis_index("grid") * shard_len
    cell_ids = lax.broadcasted_iota(jnp.int32, (group_size, shard_len), 1)
    one_hot = (cell_ids == offsets[:, None]).astype(jnp.bfloat16)
    point_terms = lax.dot_general(
        orbitals, one_hot, (((1,), (1,)), ((), ())), preferred_element_type=jnp.float32
    )
    at_points = lax.psum(point_terms, "grid").astype(jnp.bfloat16)
    chosen = jnp.take(orbitals, targets, axis=0)
    target_points = jnp.take(at_points, targets, axis=0)
    contract_first = (((0,), (0,)), ((), ()))
    density = lax.dot_general(
        at_points, orbitals, contract_first, preferred_element_type=jnp.float32
    ) * (1.0 / math.sqrt(occupied))
    target_density = lax.dot_general(
        target_points, chosen, contract_first, preferred_element_type=jnp.float32
    ) * (1.0 / math.sqrt(target_count))
    pairs = density * target_density
    fitted = lax.dot_general(
        fit,
        pairs,
        contract_first,
        precision=lax.Precision.HIGHEST,
        preferred_element_type=jnp.float32,
    ).astype(jnp.bfloat16)
    vectors = lax.all_to_all(fitted, "grid", split_axis=0, concat_axis=1, tiled=True)
    potential = lax.map(solve_one, vectors)
    returned = lax.all_to_all(potential, "grid", split_axis=1, concat_axis=0, tiled=True)
    weighted = (returned.astype(jnp.float32) * density).astype(jnp.bfloat16)
    prefactor = -1.0 / math.sqrt(group_size * slab_count)
    regrouped = lax.all_to_all(weighted, "slab", split_axis=1, concat_axis=0, tiled=True)
    all_targets = lax.all_gather(target_points, "slab", axis=1, tiled=True)
    block_out = jnp.dot(all_targets, regrouped, preferred_element_type=jnp.float32)
    summed = lax.all_to_all(block_out, "slab", split_axis=0, concat_axis=1, tiled=True)
    return summed * prefactor


def hartley(length):
    angles = np.outer(np.arange(length), np.arange(length)) % length * (2.0 * math.pi / length)
    matrix = np.cos(angles) + np.sin(angles)
    values = np.unique(np.round(np.abs(matrix), 12))
    scales = 2.0 ** (np.arange(1 << 14) / (1 << 14))
    exact = scales[:, None] * values
    errors = ((exact.astype(ml_dtypes.bfloat16).astype(np.float64) - exact) / scales[:, None]) ** 2
    scale = scales[np.argmin(errors.sum(axis=1))]
    return (matrix * scale).astype(ml_dtypes.bfloat16), scale


def split_value(value):
    upper = value.astype(bf16)
    return upper, (value - upper.astype(jnp.float32)).astype(bf16)


class Plan:
    def __init__(self, edge):
        self.edge = edge
        self.half = edge // 2
        self.slot = lanes // 2
        self.inner = lanes // math.gcd(edge, lanes)
        self.outer = edge // self.inner
        self.block = self.inner * edge
        self.block_rows = self.block // lanes
        self.plane_rows = edge * edge // lanes
        self.rows = edge * self.plane_rows
        matrix, scale = hartley(edge)
        self.windows = []
        tables = []
        for j in range(self.inner // 2):
            low, high = 2 * j * edge, (2 * j + 2) * edge
            base = low // lanes * lanes
            self.windows.append((low, high, base))
            table = np.zeros((2 * lanes, 2, 2, self.slot), ml_dtypes.bfloat16)
            for h in range(2):
                for y in range(2):
                    for z in range(edge):
                        table[(low + y * edge + z - base + h * lanes) % (2 * lanes), y, h, :edge] = matrix[z]
            tables.append(table.reshape(2 * lanes, 2 * lanes))
        self.forward = np.concatenate(tables)
        self.backward = np.concatenate([table.T for table in tables])
        step = 2.0 * math.pi / edge
        index = np.arange(edge)
        square = (np.where(index > edge // 2, index - edge, index) * step) ** 2
        weights = screening / (screening + square[:, None, None] + square[None, :, None] + square[None, None, :])
        weights = weights.reshape(2, self.half, edge, edge)
        table = np.zeros((self.half, edge, 2, self.slot))
        table[..., :edge] = np.transpose(weights, (1, 2, 0, 3))
        self.weights = (table.reshape(self.half, edge, lanes) / (edge * scale ** 2) ** 3).astype(np.float32)
        self.left = np.concatenate([matrix, matrix], axis=1)

    def tables(self):
        return [self.left, self.forward, self.backward, self.weights]


def both_parts(value):
    return jnp.concatenate(split_value(value), axis=0)


def dot(a, b):
    return jnp.dot(a, b, preferred_element_type=jnp.float32)


def product(value, table):
    rows = value.shape[0]
    both = dot(both_parts(value), table)
    return both[:rows] + both[rows:]


def solve(plan, cube, left, forward, backward, weights, mid):
    edge, half, inner, outer, block = plan.edge, plan.half, plan.inner, plan.outer, plan.block
    left_all = left[...]
    values = jnp.concatenate(
        [cube[pl.ds(c, edge, stride=plan.plane_rows), :].astype(bf16) for c in range(plan.plane_rows)], axis=1)
    spectrum = dot(left_all[:, :edge], values)

    def tile(h, c):
        return jnp.concatenate([
            spectrum[h * half:(h + 1) * half, b * block + c * lanes:b * block + (c + 1) * lanes] for b in range(outer)], axis=0)

    lane = lax.broadcasted_iota(jnp.int32, (outer * half, lanes), 1)
    tiles = [[tile(h, c) for c in range(plan.block_rows)] for h in range(2)]
    for j, (low, high, base) in enumerate(plan.windows):
        c = base // lanes
        if high - base <= lanes:
            window = [tiles[0][c], tiles[1][c]]
        else:
            window = [jnp.where(lane >= low - base, tiles[0][c], tiles[1][c + 1]),
                      jnp.where(lane < high - base - lanes, tiles[0][c + 1], tiles[1][c])]
        rows = slice(2 * lanes * j, 2 * lanes * (j + 1))
        result = product(jnp.concatenate(window, axis=1), forward[rows, :])
        for b in range(outer):
            for o in range(2):
                y = b * inner + 2 * j + o
                mid[y * half:(y + 1) * half, :] = result[b * half:(b + 1) * half, o * lanes:(o + 1) * lanes]
    for k in range(0, half, 2):
        value = jnp.concatenate([mid[pl.ds(k + o, edge, stride=half), :] for o in range(2)], axis=1)
        value = dot(left_all, both_parts(value))
        value = value * jnp.concatenate([weights[k], weights[k + 1]], axis=1)
        value = dot(left_all, both_parts(value))
        for o in range(2):
            mid[pl.ds(k + o, edge, stride=half), :] = value[:, o * lanes:(o + 1) * lanes]
    results = []
    for j in range(len(plan.windows)):
        rows = slice(2 * lanes * j, 2 * lanes * (j + 1))
        value = jnp.concatenate([
            jnp.concatenate([mid[(b * inner + 2 * j + o) * half:(b * inner + 2 * j + o + 1) * half, :] for b in range(outer)], axis=0)
            for o in range(2)], axis=1)
        results.append(product(value, backward[rows, :]))

    def gathered(h, c):
        value = None
        for (low, high, base), result in zip(plan.windows, results):
            if low < (c + 1) * lanes and high > c * lanes:
                place = (c * lanes - base + h * lanes) % (2 * lanes)
                part = result[:, place:place + lanes]
                value = part if value is None else jnp.where(lane >= low - c * lanes, part, value)
        return value

    tiles = [[gathered(h, c) for c in range(plan.block_rows)] for h in range(2)]
    value = jnp.concatenate([
        jnp.concatenate([tiles[h][c][b * half:(b + 1) * half] for h in range(2)], axis=0)
        for b in range(outer) for c in range(plan.block_rows)], axis=1)
    value = dot(left_all, both_parts(value))
    for c in range(plan.plane_rows):
        cube[pl.ds(c, edge, stride=plan.plane_rows), :] = value[:, c * lanes:(c + 1) * lanes]


def params(mebibytes):
    return pltpu.CompilerParams(vmem_limit_bytes=mebibytes * 1024 * 1024)


whole = pl.BlockSpec(memory_space=pltpu.VMEM)
far = pl.BlockSpec(memory_space=pltpu.HBM)


def iota(shape, axis):
    return lax.broadcasted_iota(jnp.int32, shape, axis)


def read_points(orbitals, targets, points, fit):
    occupied, shard_len = orbitals.shape
    count, group = targets.shape[0], points.shape[0]
    scale = 1.0 / math.sqrt(occupied) / math.sqrt(count)

    def kernel(points_hbm, targets_hbm, fit_hbm, orbitals_ref, out_ref, notes_ref, points_ref, targets_ref, fit_ref, tiles, sems):
        small = [
            pltpu.make_async_copy(source, place, sems.at[group + i])
            for i, (source, place) in enumerate(
                ((points_hbm, points_ref), (targets_hbm, targets_ref), (fit_hbm, fit_ref)))
        ]
        for copy in small:
            copy.start()
        me = lax.axis_index("grid")
        base = me * shard_len
        rows, columns = iota((8, group * lanes), 0), iota((8, group * lanes), 1)
        chosen = jnp.zeros((8, group * lanes), f32)
        copies = []
        small[0].wait()
        for m in range(group):
            local = points_ref[m] - base
            inside = (local >= 0) & (local < shard_len)
            local = jnp.clip(local, 0, shard_len - 1)
            first = pl.multiple_of(local // lanes * lanes, lanes)
            copy = pltpu.make_async_copy(
                orbitals_ref.at[:, pl.ds(first, lanes)], tiles.at[:, pl.ds(m * lanes, lanes)], sems.at[m])
            copy.start()
            copies.append(copy)
            column = jnp.where(inside, local - first + m * lanes, -1)
            chosen = jnp.where((rows == m) & (columns == column), 1.0, chosen)
        chosen = jnp.concatenate([chosen, jnp.zeros_like(chosen)], axis=0).astype(bf16)
        small[1].wait()
        small[2].wait()
        rows, columns = iota((8, lanes), 0), iota((8, lanes), 1)
        counts = jnp.zeros((8, lanes), f32)
        for k in range(count):
            counts = counts + jnp.where(columns == targets_ref[k], 1.0, 0.0)
        notes_ref[:8, :] = counts
        for j in range(group):
            value = jnp.zeros((8, lanes), f32)
            for r in range(8):
                d = r % group
                value = jnp.where(rows == r, fit_ref[(d + j) % group, jnp.bitwise_xor(me, d)], value)
            notes_ref[8 + 8 * j:16 + 8 * j, :] = value * scale
        rows, columns = iota((count, lanes), 0), iota((count, lanes), 1)
        ones = jnp.zeros((count, lanes), f32)
        for k in range(count):
            ones = jnp.where((rows == k) & (columns == targets_ref[k]), 1.0, ones)
        notes_ref[8 + 8 * group:, :] = ones
        for copy in copies:
            copy.wait()
        out = lax.dot_general(chosen, tiles[...], contract_last, preferred_element_type=f32)
        out_ref[...] = jnp.concatenate([out[:8], jnp.zeros((8, lanes - occupied), f32)], axis=1)

    return pl.pallas_call(
        kernel,
        out_shape=[
            pltpu.VMEM((8, lanes), f32),
            pltpu.VMEM((8 + 8 * group + count, lanes), f32),
        ],
        in_specs=[far] * 4,
        out_specs=[whole] * 2,
        scratch_shapes=[
            pltpu.SMEM(points.shape, jnp.int32),
            pltpu.SMEM(targets.shape, jnp.int32),
            pltpu.SMEM(fit.shape, f32),
            pltpu.VMEM((occupied, group * lanes), bf16),
            pltpu.SemaphoreType.DMA((group + 3,)),
        ],
        compiler_params=params(4),
        name="read_points",
    )(*[pltpu.with_memory_space_constraint(value, pltpu.HBM) for value in (points, targets, fit, orbitals)])


def fit_pairs(orbitals, notes, shares):
    occupied, shard_len = orbitals.shape
    group = len(shares)
    shard_rows = shard_len // lanes
    step = shard_rows // 8

    def kernel(notes_ref, orbitals_ref, *refs):
        share_refs, out_refs, at_ref, mid = refs[:group], refs[group:2 * group], refs[2 * group], refs[2 * group + 1]
        at = share_refs[0][...]
        for ref in share_refs[1:]:
            at = at + ref[...]
        at_ref[...] = at
        rows = iota((8, lanes), 0)
        twice = jnp.where(rows < group, at, pltpu.roll(at, group, 0))
        weighted = notes_ref[:8, :] * twice
        upper = weighted.astype(bf16).astype(f32)
        left = jnp.concatenate([twice, upper, weighted - upper, jnp.zeros((8, lanes), f32)], axis=0)
        left = left.astype(bf16)[:, :occupied]
        coefficients = [notes_ref[8 + 8 * j:16 + 8 * j, :] for j in range(group)]
        for c in range(0, shard_rows, step):
            product = jnp.dot(left, orbitals_ref[:, c * lanes:(c + step) * lanes], preferred_element_type=f32)
            for r in range(step):
                part = product[:, r * lanes:(r + 1) * lanes]
                pair = part[:8] * (part[8:16] + part[16:24])
                value = pair * coefficients[0]
                for j in range(1, group):
                    value = value + pltpu.roll(pair, 8 - j, 0) * coefficients[j]
                mid[(c + r) * 8:(c + r + 1) * 8, :] = value
        for d in range(group):
            out_refs[d][...] = mid[pl.ds(d, shard_rows, stride=8), :].astype(bf16)

    piece = jax.ShapeDtypeStruct((shard_rows, lanes), bf16)
    return pl.pallas_call(
        kernel,
        out_shape=[piece] * group + [jax.ShapeDtypeStruct((8, lanes), f32)],
        in_specs=[whole] * (2 + group),
        out_specs=[whole] * (group + 1),
        scratch_shapes=[pltpu.VMEM((shard_rows * 8 + 8, lanes), f32)],
        compiler_params=params(16),
        name="fit_pairs",
    )(notes, orbitals, *shares)


def potentials(plan, pieces, offsets, at, parts, place):
    grid_count, piece_rows = len(pieces), pieces[0].shape[0]
    part = piece_rows // parts
    sent = -(-(part + 1) // 8) * 8
    tables = plan.tables()

    def kernel(at_ref, *refs):
        piece_refs, refs = refs[:grid_count], refs[grid_count:]
        table_refs, (out_ref, cube, mid) = refs[:len(tables)], refs[len(tables):]
        me = lax.axis_index("grid")
        for d, ref in zip(offsets, piece_refs):
            start = pl.multiple_of(jnp.bitwise_xor(me, d) * piece_rows, 8)
            cube[pl.ds(start, piece_rows), :] = ref[...].astype(f32)
        solve(plan, cube, *table_refs, mid)
        own = jnp.broadcast_to(at_ref[pl.ds(me, 1), :], (sent, lanes))
        last = iota((sent, lanes), 0) >= part
        for g in range(grid_count):
            for q in range(parts):
                first = g * piece_rows + q * part
                out_ref[place[q * grid_count + g]] = jnp.where(last, own, cube[first:first + sent, :]).astype(bf16)

    return pl.pallas_call(
        kernel,
        out_shape=jax.ShapeDtypeStruct((parts * grid_count, sent, lanes), bf16),
        in_specs=[whole] * (1 + grid_count + len(tables)),
        out_specs=whole,
        scratch_shapes=[
            pltpu.VMEM((plan.rows + plan.plane_rows + sent, lanes), f32),
            pltpu.VMEM((plan.edge * plan.half + plan.half, lanes), f32),
        ],
        compiler_params=params(24),
        name="potentials",
    )(at, *pieces, *tables)


def apply_part(orbitals, notes, received, part, count, place, halves):
    occupied, shard_len = orbitals.shape
    points, pitch = received.shape[:2]
    slab_count = len(place)
    keep = count // slab_count
    prefactor = -1.0 / math.sqrt(points * halves)

    def kernel(notes_ref, orbitals_ref, received_ref, out_ref, spread, mid, stage):
        for m in range(points):
            spread[m * pitch:(m + 1) * pitch, :] = received_ref[m].astype(f32)
        at = spread[pl.ds(part, points, stride=pitch), :][:, :occupied].astype(bf16)
        first = pl.multiple_of(lax.axis_index("part") * (part * lanes), lanes)
        swapped = lax.axis_index("grid") % 2 == 1
        density = jnp.dot(at, orbitals_ref[:, pl.ds(first, part * lanes)], preferred_element_type=f32)
        chosen = notes_ref[notes_ref.shape[0] - count:, :][:, :occupied].astype(bf16)
        target_points = lax.dot_general(chosen, at, contract_last, preferred_element_type=f32).astype(bf16)
        potential = jnp.concatenate([spread[pl.ds(r, points, stride=pitch), :] for r in range(part)], axis=1)
        weighted = (potential * (density * (1.0 / math.sqrt(occupied)))).astype(bf16)
        applied = jnp.dot(target_points, weighted, preferred_element_type=f32) * prefactor
        for r in range(part):
            mid[r * count:(r + 1) * count, :] = applied[:, r * lanes:(r + 1) * lanes]
        for s in range(slab_count):
            for k in range(keep):
                stage[s, k * part:(k + 1) * part, :] = mid[pl.ds(s * keep + k, part, stride=count), :]
            out_ref[jnp.where(swapped, place[s ^ 1], place[s])] = stage[s, :keep * part, :].astype(bf16)

    return pl.pallas_call(
        kernel,
        out_shape=jax.ShapeDtypeStruct((slab_count, keep * part, lanes), bf16),
        in_specs=[whole] * 3,
        out_specs=whole,
        scratch_shapes=[
            pltpu.VMEM(((points + 1) * pitch, lanes), f32),
            pltpu.VMEM((pitch * count + count, lanes), f32),
            pltpu.VMEM((slab_count, keep * pitch, lanes), f32),
        ],
        compiler_params=params(16),
        name="apply_part",
    )(notes, orbitals, received)


def settle(kept, keep, halves, order):
    slab_count, rows = kept.shape[:2]
    parts = slab_count // halves
    part = rows // keep

    room = -(-part // 8) * 8

    def kernel(kept_ref, out_ref, stage, rowed, sems):
        swapped = lax.axis_index("grid") % 2 == 1
        copies = []
        for q in range(parts):
            stage[q, :rows, :] = sum(kept_ref[j].astype(f32) for j in range(slab_count) if order[j] % parts == q)
            for k in range(keep):
                rowed[q, :part, k, :] = stage[q, k * part:(k + 1) * part, :]
            first = jnp.where(swapped, q ^ 1, q) * part
            copies.append(pltpu.make_async_copy(rowed.at[q, pl.ds(0, part)], out_ref.at[pl.ds(first, part)], sems.at[q]))
            copies[-1].start()
        for copy in copies:
            copy.wait()

    return pl.pallas_call(
        kernel,
        out_shape=jax.ShapeDtypeStruct((parts * part, keep, lanes), f32),
        in_specs=[whole],
        out_specs=far,
        scratch_shapes=[
            pltpu.VMEM((parts, keep * room, lanes), f32),
            pltpu.VMEM((parts, room, keep, lanes), f32),
            pltpu.SemaphoreType.DMA((parts,)),
        ],
        compiler_params=params(4),
        name="settle",
    )(kept)


def bits_reversed(count):
    order = [0]
    while len(order) < count:
        order = [2 * i for i in order] + [2 * i + 1 for i in order]
    return order


def places(order):
    return [order.index(i) for i in range(len(order))]


def exchange(value, grid_count, offset):
    return lax.ppermute(value, "grid", [(i, i ^ offset) for i in range(grid_count)])


def quick_body(orbitals, targets, points, fit):
    grid_count, part_count, halves = (lax.axis_size(name) for name in ("grid", "part", "half"))
    shard_len, slab_count = orbitals.shape[1], part_count * halves
    count = targets.shape[0]
    keep = count // slab_count
    part = shard_len // lanes // part_count
    plan = Plan(round((shard_len * grid_count) ** (1 / 3)))
    share, notes = read_points(orbitals, targets, points, fit)
    shares = [share] + [exchange(share, grid_count, d) for d in range(1, grid_count)]
    *pieces, at = fit_pairs(orbitals, notes, shares)
    offsets = [0, grid_count - 1, *range(1, grid_count - 1)]
    pieces = [exchange(pieces[d], grid_count, d) if d else pieces[d] for d in offsets]
    near = bits_reversed(part_count * grid_count)[::-1]
    far = [s ^ (s >> 1) ^ 1 for s in reversed(range(slab_count))]
    far_groups = [[(s ^ g % 2) * grid_count + g for s in far] for g in range(grid_count)]
    sent = potentials(plan, pieces, offsets, at, part_count, places(near))
    received = lax.all_to_all(sent, ("part", "grid"), 0, 0, axis_index_groups=[near])
    blocks = apply_part(orbitals, notes, received, part, count, places(far), halves)
    kept = lax.all_to_all(blocks, ("half", "part", "grid"), 0, 0, axis_index_groups=far_groups)
    return jnp.transpose(settle(kept, keep, halves, far), (1, 0, 2)).reshape(keep, shard_len)


def quick_fits(mesh, orbitals, targets, points, fit):
    grid_count, slab_count = mesh.shape["grid"], mesh.shape["slab"]
    occupied, cells = orbitals.shape
    group, edge = fit.shape[1], round(cells ** (1 / 3))
    shard_rows = cells // grid_count // lanes
    return (
        group == grid_count
        and 2 * group == 8
        and occupied <= lanes
        and occupied % 16 == 0
        and edge ** 3 == cells
        and edge % 16 == 0
        and edge <= lanes // 2
        and cells % (grid_count * lanes) == 0
        and shard_rows % 8 == 0
        and slab_count > 2
        and (slab_count * grid_count).bit_count() == 1
        and shard_rows % (slab_count // 2) == 0
        and targets.shape[0] % slab_count == 0
        and targets.shape[0] % 8 == 0
    )


def solution(mesh):
    grid_count, slab_count = mesh.shape["grid"], mesh.shape["slab"]
    out_specs = P("slab", "grid")

    def run(*arrays):
        if not quick_fits(mesh, *arrays):
            in_specs = (P(None, "grid"), P(), P("slab"), P("slab", None))
            return jax.shard_map(plain_body, mesh=mesh, in_specs=in_specs, out_specs=out_specs, check_vma=False)(*arrays)
        halved = Mesh(mesh.devices.reshape(2, slab_count // 2, grid_count), ("half", "part", "grid"))
        slab = ("half", "part")
        in_specs = (P(None, "grid"), P(), P(slab), P(slab, None))
        return jax.shard_map(
            quick_body, mesh=halved, in_specs=in_specs, out_specs=P(slab, "grid"), check_vma=False)(*arrays)

    return run
```

```python
import math

import jax
import jax.numpy as jnp
import ml_dtypes
import numpy as np
from jax import lax
from jax.experimental import pallas as pl
from jax.experimental.pallas import tpu as pltpu
from jax.sharding import Mesh
from jax.sharding import PartitionSpec as P

NG = 48


screening = 4.0
careful = lax.Precision.HIGH
lanes = 128
f32 = jnp.float32
bf16 = jnp.bfloat16
contract_last = (((1,), (1,)), ((), ()))


def dft_tables(length):
    positions = jnp.arange(length, dtype=jnp.int32)
    product = positions[:, None] * positions[None, :] % length
    angles = product.astype(jnp.float32) * (2.0 * math.pi / length)
    return (jnp.cos(angles), jnp.sin(angles))


def kernel_table():
    full_index = jnp.arange(NG, dtype=jnp.int32)
    wrapped = jnp.where(full_index > NG // 2, full_index - NG, full_index).astype(jnp.float32)
    half_index = jnp.arange(NG // 2 + 1, dtype=jnp.int32).astype(jnp.float32)
    step_size = 2.0 * math.pi / NG
    full_sq = wrapped * step_size * (wrapped * step_size)
    half_sq = half_index * step_size * (half_index * step_size)
    summed = full_sq[:, None, None] + full_sq[None, :, None] + half_sq[None, None, :]
    return screening / (screening + summed)


def apply_axis(values, matrix, pattern):
    return jnp.einsum(
        pattern, values, matrix, precision=careful, preferred_element_type=jnp.float32
    )


def split_apply(values, matrix, pattern):
    upper = matrix.astype(jnp.bfloat16)
    lower = (matrix - upper.astype(jnp.float32)).astype(jnp.bfloat16)
    first = jnp.einsum(pattern, values, upper, preferred_element_type=jnp.float32)
    return first + jnp.einsum(pattern, values, lower, preferred_element_type=jnp.float32)


def solve_one(vector_row):
    half_len = NG // 2 + 1
    cosine, sin_table = dft_tables(NG)
    cos_half = cosine[:, :half_len]
    sin_half = sin_table[:, :half_len]
    cube_vals = vector_row.reshape(NG, NG, NG)
    real_part = split_apply(cube_vals, cos_half, "xyz,zm->xym")
    imag_part = -split_apply(cube_vals, sin_half, "xyz,zm->xym")
    for pattern in ("xym,yb->xbm", "xym,xb->bym"):
        real_next = apply_axis(real_part, cosine, pattern) + apply_axis(
            imag_part, sin_table, pattern
        )
        imag_part = apply_axis(imag_part, cosine, pattern) - apply_axis(
            real_part, sin_table, pattern
        )
        real_part = real_next
    weights = kernel_table()
    real_part = real_part * weights
    imag_part = imag_part * weights
    for pattern in ("xym,xb->bym", "xym,yb->xbm"):
        real_next = apply_axis(real_part, cosine, pattern) - apply_axis(
            imag_part, sin_table, pattern
        )
        imag_part = apply_axis(real_part, sin_table, pattern) + apply_axis(
            imag_part, cosine, pattern
        )
        real_part = real_next
    frequency = jnp.arange(half_len, dtype=jnp.int32)
    fold_weight = jnp.where((frequency == 0) | (frequency == NG // 2), 1.0, 2.0).astype(jnp.float32)
    result = apply_axis(real_part * fold_weight, cos_half, "xym,zm->xyz") - apply_axis(
        imag_part * fold_weight, sin_half, "xym,zm->xyz"
    )
    return (result * (1.0 / (NG * NG * NG))).reshape(-1).astype(jnp.bfloat16)


def plain_body(orbitals, targets, points, fit):
    occupied, shard_len = orbitals.shape
    target_count = targets.shape[0]
    group_size = points.shape[0]
    slab_count = lax.axis_size("slab")
    offsets = points - lax.axis_index("grid") * shard_len
    cell_ids = lax.broadcasted_iota(jnp.int32, (group_size, shard_len), 1)
    one_hot = (cell_ids == offsets[:, None]).astype(jnp.bfloat16)
    point_terms = lax.dot_general(
        orbitals, one_hot, (((1,), (1,)), ((), ())), preferred_element_type=jnp.float32
    )
    at_points = lax.psum(point_terms, "grid").astype(jnp.bfloat16)
    chosen = jnp.take(orbitals, targets, axis=0)
    target_points = jnp.take(at_points, targets, axis=0)
    contract_first = (((0,), (0,)), ((), ()))
    density = lax.dot_general(
        at_points, orbitals, contract_first, preferred_element_type=jnp.float32
    ) * (1.0 / math.sqrt(occupied))
    target_density = lax.dot_general(
        target_points, chosen, contract_first, preferred_element_type=jnp.float32
    ) * (1.0 / math.sqrt(target_count))
    pairs = density * target_density
    fitted = lax.dot_general(
        fit,
        pairs,
        contract_first,
        precision=lax.Precision.HIGHEST,
        preferred_element_type=jnp.float32,
    ).astype(jnp.bfloat16)
    vectors = lax.all_to_all(fitted, "grid", split_axis=0, concat_axis=1, tiled=True)
    potential = lax.map(solve_one, vectors)
    returned = lax.all_to_all(potential, "grid", split_axis=1, concat_axis=0, tiled=True)
    weighted = (returned.astype(jnp.float32) * density).astype(jnp.bfloat16)
    prefactor = -1.0 / math.sqrt(group_size * slab_count)
    regrouped = lax.all_to_all(weighted, "slab", split_axis=1, concat_axis=0, tiled=True)
    all_targets = lax.all_gather(target_points, "slab", axis=1, tiled=True)
    block_out = jnp.dot(all_targets, regrouped, preferred_element_type=jnp.float32)
    summed = lax.all_to_all(block_out, "slab", split_axis=0, concat_axis=1, tiled=True)
    return summed * prefactor


def hartley(length):
    angles = np.outer(np.arange(length), np.arange(length)) % length * (2.0 * math.pi / length)
    matrix = np.cos(angles) + np.sin(angles)
    values = np.unique(np.round(np.abs(matrix), 12))
    scales = 2.0 ** (np.arange(1 << 14) / (1 << 14))
    exact = scales[:, None] * values
    errors = ((exact.astype(ml_dtypes.bfloat16).astype(np.float64) - exact) / scales[:, None]) ** 2
    scale = scales[np.argmin(errors.sum(axis=1))]
    return (matrix * scale).astype(ml_dtypes.bfloat16), scale


def split_value(value):
    upper = value.astype(bf16)
    return upper, (value - upper.astype(jnp.float32)).astype(bf16)


class Plan:
    def __init__(self, edge):
        self.edge = edge
        self.half = edge // 2
        self.slot = lanes // 2
        self.inner = lanes // math.gcd(edge, lanes)
        self.outer = edge // self.inner
        self.block = self.inner * edge
        self.block_rows = self.block // lanes
        self.plane_rows = edge * edge // lanes
        self.rows = edge * self.plane_rows
        matrix, scale = hartley(edge)
        self.windows = []
        tables = []
        for j in range(self.inner // 2):
            low, high = 2 * j * edge, (2 * j + 2) * edge
            base = low // lanes * lanes
            self.windows.append((low, high, base))
            table = np.zeros((2 * lanes, 2, 2, self.slot), ml_dtypes.bfloat16)
            for h in range(2):
                for y in range(2):
                    for z in range(edge):
                        table[(low + y * edge + z - base + h * lanes) % (2 * lanes), y, h, :edge] = matrix[z]
            tables.append(table.reshape(2 * lanes, 2 * lanes))
        self.forward = np.concatenate(tables)
        self.backward = np.concatenate([table.T for table in tables])
        step = 2.0 * math.pi / edge
        index = np.arange(edge)
        square = (np.where(index > edge // 2, index - edge, index) * step) ** 2
        weights = screening / (screening + square[:, None, None] + square[None, :, None] + square[None, None, :])
        weights = weights.reshape(2, self.half, edge, edge)
        table = np.zeros((self.half, edge, 2, self.slot))
        table[..., :edge] = np.transpose(weights, (1, 2, 0, 3))
        self.weights = (table.reshape(self.half, edge, lanes) / (edge * scale ** 2) ** 3).astype(np.float32)
        self.left = np.concatenate([matrix, matrix], axis=1)

    def tables(self):
        return [self.left, self.forward, self.backward, self.weights]


def both_parts(value):
    return jnp.concatenate(split_value(value), axis=0)


def dot(a, b):
    return jnp.dot(a, b, preferred_element_type=jnp.float32)


def product(value, table):
    rows = value.shape[0]
    both = dot(both_parts(value), table)
    return both[:rows] + both[rows:]


def solve(plan, cube, left, forward, backward, weights, mid):
    edge, half, inner, outer, block = plan.edge, plan.half, plan.inner, plan.outer, plan.block
    left_all = left[...]
    values = jnp.concatenate(
        [cube[pl.ds(c, edge, stride=plan.plane_rows), :].astype(bf16) for c in range(plan.plane_rows)], axis=1)
    spectrum = dot(left_all[:, :edge], values)

    def tile(h, c):
        return jnp.concatenate([
            spectrum[h * half:(h + 1) * half, b * block + c * lanes:b * block + (c + 1) * lanes] for b in range(outer)], axis=0)

    lane = lax.broadcasted_iota(jnp.int32, (outer * half, lanes), 1)
    tiles = [[tile(h, c) for c in range(plan.block_rows)] for h in range(2)]
    for j, (low, high, base) in enumerate(plan.windows):
        c = base // lanes
        if high - base <= lanes:
            window = [tiles[0][c], tiles[1][c]]
        else:
            window = [jnp.where(lane >= low - base, tiles[0][c], tiles[1][c + 1]),
                      jnp.where(lane < high - base - lanes, tiles[0][c + 1], tiles[1][c])]
        rows = slice(2 * lanes * j, 2 * lanes * (j + 1))
        result = product(jnp.concatenate(window, axis=1), forward[rows, :])
        for b in range(outer):
            for o in range(2):
                y = b * inner + 2 * j + o
                mid[y * half:(y + 1) * half, :] = result[b * half:(b + 1) * half, o * lanes:(o + 1) * lanes]
    for k in range(0, half, 2):
        value = jnp.concatenate([mid[pl.ds(k + o, edge, stride=half), :] for o in range(2)], axis=1)
        value = dot(left_all, both_parts(value))
        value = value * jnp.concatenate([weights[k], weights[k + 1]], axis=1)
        value = dot(left_all, both_parts(value))
        for o in range(2):
            mid[pl.ds(k + o, edge, stride=half), :] = value[:, o * lanes:(o + 1) * lanes]
    results = []
    for j in range(len(plan.windows)):
        rows = slice(2 * lanes * j, 2 * lanes * (j + 1))
        value = jnp.concatenate([
            jnp.concatenate([mid[(b * inner + 2 * j + o) * half:(b * inner + 2 * j + o + 1) * half, :] for b in range(outer)], axis=0)
            for o in range(2)], axis=1)
        results.append(product(value, backward[rows, :]))

    def gathered(h, c):
        value = None
        for (low, high, base), result in zip(plan.windows, results):
            if low < (c + 1) * lanes and high > c * lanes:
                place = (c * lanes - base + h * lanes) % (2 * lanes)
                part = result[:, place:place + lanes]
                value = part if value is None else jnp.where(lane >= low - c * lanes, part, value)
        return value

    tiles = [[gathered(h, c) for c in range(plan.block_rows)] for h in range(2)]
    value = jnp.concatenate([
        jnp.concatenate([tiles[h][c][b * half:(b + 1) * half] for h in range(2)], axis=0)
        for b in range(outer) for c in range(plan.block_rows)], axis=1)
    value = dot(left_all, both_parts(value))
    for c in range(plan.plane_rows):
        cube[pl.ds(c, edge, stride=plan.plane_rows), :] = value[:, c * lanes:(c + 1) * lanes]


def params(mebibytes):
    return pltpu.CompilerParams(vmem_limit_bytes=mebibytes * 1024 * 1024)


whole = pl.BlockSpec(memory_space=pltpu.VMEM)
far = pl.BlockSpec(memory_space=pltpu.HBM)


def iota(shape, axis):
    return lax.broadcasted_iota(jnp.int32, shape, axis)


def read_points(orbitals, targets, points, fit):
    occupied, shard_len = orbitals.shape
    count, group = targets.shape[0], points.shape[0]
    scale = 1.0 / math.sqrt(occupied) / math.sqrt(count)

    def kernel(points_hbm, targets_hbm, fit_hbm, orbitals_ref, out_ref, notes_ref, points_ref, targets_ref, fit_ref, tiles, sems):
        small = [
            pltpu.make_async_copy(source, place, sems.at[group + i])
            for i, (source, place) in enumerate(
                ((points_hbm, points_ref), (targets_hbm, targets_ref), (fit_hbm, fit_ref)))
        ]
        for copy in small:
            copy.start()
        me = lax.axis_index("grid")
        base = me * shard_len
        rows, columns = iota((8, group * lanes), 0), iota((8, group * lanes), 1)
        chosen = jnp.zeros((8, group * lanes), f32)
        copies = []
        small[0].wait()
        for m in range(group):
            local = points_ref[m] - base
            inside = (local >= 0) & (local < shard_len)
            local = jnp.clip(local, 0, shard_len - 1)
            first = pl.multiple_of(local // lanes * lanes, lanes)
            copy = pltpu.make_async_copy(
                orbitals_ref.at[:, pl.ds(first, lanes)], tiles.at[:, pl.ds(m * lanes, lanes)], sems.at[m])
            copy.start()
            copies.append(copy)
            column = jnp.where(inside, local - first + m * lanes, -1)
            chosen = jnp.where((rows == m) & (columns == column), 1.0, chosen)
        chosen = jnp.concatenate([chosen, jnp.zeros_like(chosen)], axis=0).astype(bf16)
        small[1].wait()
        small[2].wait()
        rows, columns = iota((8, lanes), 0), iota((8, lanes), 1)
        counts = jnp.zeros((8, lanes), f32)
        for k in range(count):
            counts = counts + jnp.where(columns == targets_ref[k], 1.0, 0.0)
        notes_ref[:8, :] = counts
        for j in range(group):
            value = jnp.zeros((8, lanes), f32)
            for r in range(8):
                d = r % group
                value = jnp.where(rows == r, fit_ref[(d + j) % group, jnp.bitwise_xor(me, d)], value)
            notes_ref[8 + 8 * j:16 + 8 * j, :] = value * scale
        rows, columns = iota((count, lanes), 0), iota((count, lanes), 1)
        ones = jnp.zeros((count, lanes), f32)
        for k in range(count):
            ones = jnp.where((rows == k) & (columns == targets_ref[k]), 1.0, ones)
        notes_ref[8 + 8 * group:, :] = ones
        for copy in copies:
            copy.wait()
        out = lax.dot_general(chosen, tiles[...], contract_last, preferred_element_type=f32)
        out_ref[...] = jnp.concatenate([out[:8], jnp.zeros((8, lanes - occupied), f32)], axis=1)

    return pl.pallas_call(
        kernel,
        out_shape=[
            pltpu.VMEM((8, lanes), f32),
            pltpu.VMEM((8 + 8 * group + count, lanes), f32),
        ],
        in_specs=[far] * 4,
        out_specs=[whole] * 2,
        scratch_shapes=[
            pltpu.SMEM(points.shape, jnp.int32),
            pltpu.SMEM(targets.shape, jnp.int32),
            pltpu.SMEM(fit.shape, f32),
            pltpu.VMEM((occupied, group * lanes), bf16),
            pltpu.SemaphoreType.DMA((group + 3,)),
        ],
        compiler_params=params(4),
        name="read_points",
    )(*[pltpu.with_memory_space_constraint(value, pltpu.HBM) for value in (points, targets, fit, orbitals)])


def fit_pairs(orbitals, notes, shares):
    occupied, shard_len = orbitals.shape
    group = len(shares)
    shard_rows = shard_len // lanes
    step = shard_rows // 8

    def kernel(notes_ref, orbitals_ref, *refs):
        share_refs, out_refs, at_ref, mid = refs[:group], refs[group:2 * group], refs[2 * group], refs[2 * group + 1]
        at = share_refs[0][...]
        for ref in share_refs[1:]:
            at = at + ref[...]
        at_ref[...] = at
        rows = iota((8, lanes), 0)
        twice = jnp.where(rows < group, at, pltpu.roll(at, group, 0))
        weighted = notes_ref[:8, :] * twice
        upper = weighted.astype(bf16).astype(f32)
        left = jnp.concatenate([twice, upper, weighted - upper, jnp.zeros((8, lanes), f32)], axis=0)
        left = left.astype(bf16)[:, :occupied]
        coefficients = [notes_ref[8 + 8 * j:16 + 8 * j, :] for j in range(group)]
        for c in range(0, shard_rows, step):
            product = jnp.dot(left, orbitals_ref[:, c * lanes:(c + step) * lanes], preferred_element_type=f32)
            for r in range(step):
                part = product[:, r * lanes:(r + 1) * lanes]
                pair = part[:8] * (part[8:16] + part[16:24])
                value = pair * coefficients[0]
                for j in range(1, group):
                    value = value + pltpu.roll(pair, 8 - j, 0) * coefficients[j]
                mid[(c + r) * 8:(c + r + 1) * 8, :] = value
        for d in range(group):
            out_refs[d][...] = mid[pl.ds(d, shard_rows, stride=8), :].astype(bf16)

    piece = jax.ShapeDtypeStruct((shard_rows, lanes), bf16)
    return pl.pallas_call(
        kernel,
        out_shape=[piece] * group + [jax.ShapeDtypeStruct((8, lanes), f32)],
        in_specs=[whole] * (2 + group),
        out_specs=[whole] * (group + 1),
        scratch_shapes=[pltpu.VMEM((shard_rows * 8 + 8, lanes), f32)],
        compiler_params=params(16),
        name="fit_pairs",
    )(notes, orbitals, *shares)


def potentials(plan, pieces, offsets, at, parts, place):
    grid_count, piece_rows = len(pieces), pieces[0].shape[0]
    part = piece_rows // parts
    sent = -(-(part + 1) // 8) * 8
    tables = plan.tables()

    def kernel(at_ref, *refs):
        piece_refs, refs = refs[:grid_count], refs[grid_count:]
        table_refs, (out_ref, cube, mid) = refs[:len(tables)], refs[len(tables):]
        me = lax.axis_index("grid")
        for d, ref in zip(offsets, piece_refs):
            start = pl.multiple_of(jnp.bitwise_xor(me, d) * piece_rows, 8)
            cube[pl.ds(start, piece_rows), :] = ref[...].astype(f32)
        solve(plan, cube, *table_refs, mid)
        own = jnp.broadcast_to(at_ref[pl.ds(me, 1), :], (sent, lanes))
        last = iota((sent, lanes), 0) >= part
        for g in range(grid_count):
            for q in range(parts):
                first = g * piece_rows + q * part
                out_ref[place[q * grid_count + g]] = jnp.where(last, own, cube[first:first + sent, :]).astype(bf16)

    return pl.pallas_call(
        kernel,
        out_shape=jax.ShapeDtypeStruct((parts * grid_count, sent, lanes), bf16),
        in_specs=[whole] * (1 + grid_count + len(tables)),
        out_specs=whole,
        scratch_shapes=[
            pltpu.VMEM((plan.rows + plan.plane_rows + sent, lanes), f32),
            pltpu.VMEM((plan.edge * plan.half + plan.half, lanes), f32),
        ],
        compiler_params=params(24),
        name="potentials",
    )(at, *pieces, *tables)


def apply_part(orbitals, notes, received, part, count, place, halves):
    occupied, shard_len = orbitals.shape
    points, pitch = received.shape[:2]
    slab_count = len(place)
    keep = count // slab_count
    prefactor = -1.0 / math.sqrt(points * halves)

    def kernel(notes_ref, orbitals_ref, received_ref, out_ref, spread, mid, stage):
        for m in range(points):
            spread[m * pitch:(m + 1) * pitch, :] = received_ref[m].astype(f32)
        at = spread[pl.ds(part, points, stride=pitch), :][:, :occupied].astype(bf16)
        first = pl.multiple_of(lax.axis_index("part") * (part * lanes), lanes)
        swapped = lax.axis_index("grid") % 2 == 1
        density = jnp.dot(at, orbitals_ref[:, pl.ds(first, part * lanes)], preferred_element_type=f32)
        chosen = notes_ref[notes_ref.shape[0] - count:, :][:, :occupied].astype(bf16)
        target_points = lax.dot_general(chosen, at, contract_last, preferred_element_type=f32).astype(bf16)
        potential = jnp.concatenate([spread[pl.ds(r, points, stride=pitch), :] for r in range(part)], axis=1)
        weighted = (potential * (density * (1.0 / math.sqrt(occupied)))).astype(bf16)
        applied = jnp.dot(target_points, weighted, preferred_element_type=f32) * prefactor
        for r in range(part):
            mid[r * count:(r + 1) * count, :] = applied[:, r * lanes:(r + 1) * lanes]
        for s in range(slab_count):
            for k in range(keep):
                stage[s, k * part:(k + 1) * part, :] = mid[pl.ds(s * keep + k, part, stride=count), :]
            out_ref[jnp.where(swapped, place[s ^ 1], place[s])] = stage[s, :keep * part, :].astype(bf16)

    return pl.pallas_call(
        kernel,
        out_shape=jax.ShapeDtypeStruct((slab_count, keep * part, lanes), bf16),
        in_specs=[whole] * 3,
        out_specs=whole,
        scratch_shapes=[
            pltpu.VMEM(((points + 1) * pitch, lanes), f32),
            pltpu.VMEM((pitch * count + count, lanes), f32),
            pltpu.VMEM((slab_count, keep * pitch, lanes), f32),
        ],
        compiler_params=params(16),
        name="apply_part",
    )(notes, orbitals, received)


def settle(kept, keep, halves, order):
    slab_count, rows = kept.shape[:2]
    parts = slab_count // halves
    part = rows // keep

    room = -(-part // 8) * 8

    def kernel(kept_ref, out_ref, stage, rowed, sems):
        swapped = lax.axis_index("grid") % 2 == 1
        copies = []
        for q in range(parts):
            stage[q, :rows, :] = sum(kept_ref[j].astype(f32) for j in range(slab_count) if order[j] % parts == q)
            for k in range(keep):
                rowed[q, :part, k, :] = stage[q, k * part:(k + 1) * part, :]
            first = jnp.where(swapped, q ^ 1, q) * part
            copies.append(pltpu.make_async_copy(rowed.at[q, pl.ds(0, part)], out_ref.at[pl.ds(first, part)], sems.at[q]))
            copies[-1].start()
        for copy in copies:
            copy.wait()

    return pl.pallas_call(
        kernel,
        out_shape=jax.ShapeDtypeStruct((parts * part, keep, lanes), f32),
        in_specs=[whole],
        out_specs=far,
        scratch_shapes=[
            pltpu.VMEM((parts, keep * room, lanes), f32),
            pltpu.VMEM((parts, room, keep, lanes), f32),
            pltpu.SemaphoreType.DMA((parts,)),
        ],
        compiler_params=params(4),
        name="settle",
    )(kept)


def bits_reversed(count):
    order = [0]
    while len(order) < count:
        order = [2 * i for i in order] + [2 * i + 1 for i in order]
    return order


def places(order):
    return [order.index(i) for i in range(len(order))]


def exchange(value, grid_count, offset):
    return lax.ppermute(value, "grid", [(i, i ^ offset) for i in range(grid_count)])


def quick_body(orbitals, targets, points, fit):
    grid_count, part_count, halves = (lax.axis_size(name) for name in ("grid", "part", "half"))
    shard_len, slab_count = orbitals.shape[1], part_count * halves
    count = targets.shape[0]
    keep = count // slab_count
    part = shard_len // lanes // part_count
    plan = Plan(round((shard_len * grid_count) ** (1 / 3)))
    share, notes = read_points(orbitals, targets, points, fit)
    shares = [share] + [exchange(share, grid_count, d) for d in (1, *reversed(range(2, grid_count)))]
    *pieces, at = fit_pairs(orbitals, notes, shares)
    offsets = [0] + list(reversed(range(1, grid_count)))
    pieces = [exchange(pieces[d], grid_count, d) if d else pieces[d] for d in offsets]
    near = bits_reversed(part_count * grid_count)[::-1]
    far = [s ^ (s >> 1) ^ 1 for s in reversed(range(slab_count))]
    far_groups = [[(s ^ g % 2) * grid_count + g for s in far] for g in range(grid_count)]
    sent = potentials(plan, pieces, offsets, at, part_count, places(near))
    received = lax.all_to_all(sent, ("part", "grid"), 0, 0, axis_index_groups=[near])
    blocks = apply_part(orbitals, notes, received, part, count, places(far), halves)
    kept = lax.all_to_all(blocks, ("half", "part", "grid"), 0, 0, axis_index_groups=far_groups)
    return jnp.transpose(settle(kept, keep, halves, far), (1, 0, 2)).reshape(keep, shard_len)


def quick_fits(mesh, orbitals, targets, points, fit):
    grid_count, slab_count = mesh.shape["grid"], mesh.shape["slab"]
    occupied, cells = orbitals.shape
    group, edge = fit.shape[1], round(cells ** (1 / 3))
    shard_rows = cells // grid_count // lanes
    return (
        group == grid_count
        and 2 * group == 8
        and occupied <= lanes
        and occupied % 16 == 0
        and edge ** 3 == cells
        and edge % 16 == 0
        and edge <= lanes // 2
        and cells % (grid_count * lanes) == 0
        and shard_rows % 8 == 0
        and slab_count > 2
        and (slab_count * grid_count).bit_count() == 1
        and shard_rows % (slab_count // 2) == 0
        and targets.shape[0] % slab_count == 0
        and targets.shape[0] % 8 == 0
    )


def solution(mesh):
    grid_count, slab_count = mesh.shape["grid"], mesh.shape["slab"]
    out_specs = P("slab", "grid")

    def run(*arrays):
        if not quick_fits(mesh, *arrays):
            in_specs = (P(None, "grid"), P(), P("slab"), P("slab", None))
            return jax.shard_map(plain_body, mesh=mesh, in_specs=in_specs, out_specs=out_specs, check_vma=False)(*arrays)
        halved = Mesh(mesh.devices.reshape(2, slab_count // 2, grid_count), ("half", "part", "grid"))
        slab = ("half", "part")
        in_specs = (P(None, "grid"), P(), P(slab), P(slab, None))
        return jax.shard_map(
            quick_body, mesh=halved, in_specs=in_specs, out_specs=P(slab, "grid"), check_vma=False)(*arrays)

    return run
```
